32 devices in a mesh: dp: 8 (over z, x), blk: 2 (over y), head: 2 (over core).
Axes of the slice: x: 2, y: 2, z: 4, core: 2. Of those that a mesh axis runs over, the one named last changes fastest.
Arguments:
- tokens: bfloat16 [32, 512, 1024], P('dp', ('blk', 'head')), may hold values from -6 to 6
- doc_lengths: int32 [32, 32], P('dp'), may hold values from 0 to 448, as said below
- qkv_weight: bfloat16 [1024, 3072], P(('dp', 'blk', 'head')), may hold values from -0.1875 to 0.1875
- out_weight: bfloat16 [1024, 1024], P(('dp', 'blk', 'head')), may hold values from -0.75 to 0.75
- up_weight: bfloat16 [1024, 4096], P(('dp', 'blk', 'head')), may hold values from -0.1875 to 0.1875
- down_weight: bfloat16 [4096, 1024], P(('dp', 'blk', 'head')), may hold values from -0.09375 to 0.09375
- norm_params: bfloat16 [1024, 4], P(('dp', 'blk', 'head')), may hold values from -0.5 to 1.5, as said below
- out_cotangent: bfloat16 [32, 512, 1024], P('dp', ('blk', 'head')), may hold values from -6 to 6
Outputs:
- layer_out: bfloat16 [32, 512, 1024], P('dp', ('blk', 'head'))
- input_grad: float32 [32, 512, 1024], P('dp', ('blk', 'head'))
- qkv_grad: float32 [1024, 3072], P(('dp', 'blk', 'head'))
- proj_grad: float32 [1024, 1024], P(('dp', 'blk', 'head'))
- up_grad: float32 [1024, 4096], P(('dp', 'blk', 'head'))
- down_grad: float32 [4096, 1024], P(('dp', 'blk', 'head'))
- norm_grad: float32 [1024, 4], P(('dp', 'blk', 'head'))
The draws below stay inside these ranges and needn't reach their ends.
Inputs may be any that keep to these rules, and one draw needn't show every extreme that they name: `doc_lengths`: each sequence's lengths sum to at most 512; positions past the sum are padding; a length may be zero. One sequence of each 4 consecutive ones holds a document of 448 tokens that starts at one of positions 0 to 64. `norm_params`: columns 0 and 2 are gains, columns 1 and 3 shifts.
All inputs are finite; a program needn't handle non-finite values.
Results may differ from the reference program's by a relative error of at most 0.015.
Values may be sent and summed in bfloat16 or wider, within the bound.
No kernel may reach another device: no remote copies, remote signals or barrier semaphores. Data moves between devices by JAX's collectives and lax.ppermute only.
A program may use at most 192 MiB of HBM per device.

```python
import math
import jax
import jax.numpy as jnp
from jax import lax

D = 1024
HEADS = 16
HEAD_DIM = 64
FF = 4096
LEN = 512
DOCS = 32
SEQ_DEV = 4
SEQS = 32


def draw_doc_lengths(key, part):
    key = jax.random.fold_in(key, 11)
    key_list = jax.random.split(key, 5)
    exponent = jax.random.randint(key_list[0], (SEQS, DOCS), 0, 6)
    ceiling = jnp.left_shift(jnp.full((SEQS, DOCS), 8, jnp.int32), exponent)
    raw_lengths = 1 + jax.random.randint(key_list[1], (SEQS, DOCS), 0, 1048576) % ceiling
    raw_lengths = jnp.minimum(raw_lengths, LEN // 2)
    padding = jax.random.randint(key_list[2], (SEQS, 1), 0, LEN // 4 + 1)
    budget = LEN - padding
    doc_starts = jnp.cumsum(raw_lengths, axis=-1, dtype=jnp.int32) - raw_lengths
    trimmed = jnp.minimum(raw_lengths, jnp.maximum(budget - doc_starts, 0))
    offset = jax.random.randint(key_list[3], (SEQS, 1), 0, LEN // 8 + 1)
    slot_index = jnp.arange(DOCS, dtype=jnp.int32)[None, :]
    long_lengths = jnp.where(slot_index == 0, offset, 0) + jnp.where(slot_index == 1, LEN - LEN // 8, 0) + jnp.where(slot_index == 2, LEN // 8 - offset, 0)
    chosen = jax.random.randint(key_list[4], (SEQS // SEQ_DEV,), 0, SEQ_DEV)
    marker = jnp.repeat(chosen, SEQ_DEV) == jnp.arange(SEQS, dtype=jnp.int32) % SEQ_DEV
    return jnp.where(marker[:, None], long_lengths, trimmed).astype(jnp.int32)


def draw_norm_params(key, part):
    key = jax.random.fold_in(key, 17)
    uniform_part = jax.random.uniform(key, (D, 4), jnp.float32, -1.0, 1.0)
    gain_column = jnp.array([1.0, 0.0, 1.0, 0.0], jnp.float32)[None, :]
    return (gain_column + 0.5 * uniform_part).astype(jnp.bfloat16)


def shard_levels(key, shape, cuts, low, high):
    def one(dim, parts):
        draws = jax.random.uniform(jax.random.fold_in(jax.random.fold_in(key, 6), dim), (parts,), jnp.float32, low / len(cuts), high / len(cuts))
        return jnp.repeat(jnp.exp(draws), shape[dim] // parts).reshape((-1,) + (1,) * (len(shape) - dim - 1))

    loudness = one(*cuts[0])
    for cut in cuts[1:]:
        loudness = loudness * one(*cut)
    return loudness


def gaussian(rng, shape, scale, bound, pieces=(), kind=jnp.bfloat16):
    values = scale * jax.random.normal(rng, shape, jnp.float32)
    if pieces:
        values = values * shard_levels(rng, shape, pieces, -0.22, 0.18)
    return jnp.clip(values, -bound, bound).astype(kind)


def setup_inputs(seed: int = 0) -> dict:
    key_of = jax.random.split(jax.random.key(seed), 9)
    return {
        "tokens": gaussian(key_of[0], (SEQS, LEN, D), 1.0, 6.0, ((0, 8), (1, 4))),
        "doc_lengths": draw_doc_lengths(jax.random.fold_in(key_of[8], 71), 0),
        "qkv_weight": gaussian(key_of[2], (D, 3 * D), D ** -0.5, 0.1875, ((0, 32),)),
        "out_weight": gaussian(key_of[3], (D, D), (D // 16) ** -0.5, 0.75, ((0, 32),)),
        "up_weight": gaussian(key_of[4], (D, FF), D ** -0.5, 0.1875, ((0, 32),)),
        "down_weight": gaussian(key_of[5], (FF, D), FF ** -0.5, 0.09375, ((0, 32),)),
        "norm_params": draw_norm_params(jax.random.fold_in(key_of[8], 71), 0),
        "out_cotangent": gaussian(key_of[7], (SEQS, LEN, D), 1.0, 6.0, ((0, 8), (1, 4))),
    }


@jax.custom_vjp
def low(v):
    return lax.optimization_barrier(v.astype(jnp.bfloat16)).astype(jnp.float32)

@jax.custom_vjp
def low_back(v):
    return v

def low_keep(v):
    return (low(v), None)

def low_pass(kept, grad):
    return (grad,)

def back_keep(v):
    return (v, None)

def back_low(kept, grad):
    return (low(grad),)
low.defvjp(low_keep, low_pass)
low_back.defvjp(back_keep, back_low)
epsilon = 1e-12
highest = lax.Precision.HIGHEST

def segments_of(doc_lengths, length):
    doc_ends = jnp.cumsum(doc_lengths, axis=-1, dtype=jnp.int32)
    places = jnp.arange(length, dtype=jnp.int32)
    passed = lax.optimization_barrier(jnp.sum((doc_ends[..., None, :] <= places[:, None]).astype(jnp.int32), axis=-1, dtype=jnp.int32))
    return jnp.where(places < doc_ends[..., -1:], passed + 1, 0).astype(jnp.int32)

def layer_norm(hidden, gain, shift):
    average = lax.optimization_barrier(jnp.mean(hidden, axis=-1, keepdims=True))
    centred = hidden - average
    spread = lax.optimization_barrier(jnp.mean(centred * centred, axis=-1, keepdims=True))
    return centred * lax.rsqrt(spread + epsilon) * gain + shift

def gelu_exact(values_in):
    return jax.nn.gelu(values_in, approximate=False)

def block_forward(tokens_f, token_segments, weights):
    qkv_w, out_w, up_w, down_w, norm_w = weights
    group_seqs = tokens_f.shape[0]
    flat_rows = tokens_f.reshape(-1, D)
    projected = low_back(low(jnp.dot(flat_rows, qkv_w, precision=highest)))
    projected = projected.reshape(group_seqs, LEN, 3, HEADS, HEAD_DIM)
    raw_scores = jnp.einsum('gqhd,gkhd->ghqk', projected[:, :, 0], projected[:, :, 1], precision=highest)
    scores = low_back(raw_scores * HEAD_DIM ** (-0.5))
    allowed = token_segments[:, None, :, None] == token_segments[:, None, None, :]
    softmax_out = jax.nn.softmax(jnp.where(allowed, scores, -1e+30), axis=-1)
    context = jnp.einsum('ghqk,gkhd->gqhd', low(softmax_out), projected[:, :, 2], precision=highest)
    live_rows = (token_segments != 0).astype(jnp.float32)
    context = low_back(low(context * live_rows[:, :, None, None])).reshape(-1, D)
    first_in = flat_rows + low_back(jnp.dot(context, out_w, precision=highest))
    first_out = layer_norm(first_in, norm_w[:, 0], norm_w[:, 1])
    pre_act = low_back(jnp.dot(low(first_out), up_w, precision=highest))
    ff_out = low_back(jnp.dot(low(gelu_exact(pre_act)), down_w, precision=highest))
    second_out = layer_norm(first_out + ff_out, norm_w[:, 2], norm_w[:, 3])
    return second_out.reshape(group_seqs, LEN, D)

def reference(tokens, doc_lengths, qkv_weight, out_weight, up_weight, down_weight, norm_params, out_cotangent):
    token_segments = segments_of(doc_lengths, LEN)
    per_step = math.gcd(SEQS, 8)
    step_count = SEQS // per_step

    def forward(tokens_f, qkv_w, out_w, up_w, down_w, norm_w):
        weights = (qkv_w, out_w, up_w, down_w, norm_w)
        token_blocks = tokens_f.reshape(step_count, per_step, LEN, D)
        segment_blocks = token_segments.reshape(step_count, per_step, LEN)

        def run_block(block_pair):
            return block_forward(block_pair[0], block_pair[1], weights)
        outputs = lax.map(jax.checkpoint(run_block), (token_blocks, segment_blocks))
        return outputs.reshape(SEQS, LEN, D)
    inputs_f = [tokens.astype(jnp.float32), qkv_weight.astype(jnp.float32), out_weight.astype(jnp.float32), up_weight.astype(jnp.float32), down_weight.astype(jnp.float32), norm_params.astype(jnp.float32)]
    result, pull_back = jax.vjp(forward, *inputs_f)
    gradients = pull_back(out_cotangent.astype(jnp.float32))
    return (result.astype(jnp.bfloat16), gradients[0], gradients[1], gradients[2], gradients[3], gradients[4], gradients[5])
```

```python
import jax
import jax.numpy as jnp
from jax import lax
from jax.experimental import pallas as pl
from jax.experimental.pallas import tpu as pltpu
from jax.sharding import PartitionSpec as P

HEAD_DIM = 64
ALL = ("dp", "blk", "head")
GROUP = ("blk", "head")


epsilon = 1e-12


def segments_of(doc_lengths, length):
    doc_ends = jnp.cumsum(doc_lengths, axis=-1, dtype=jnp.int32)
    places = jnp.arange(length, dtype=jnp.int32)
    passed = jnp.sum(
        (doc_ends[..., None, :] <= places[:, None]).astype(jnp.int32), axis=-1, dtype=jnp.int32
    )
    return jnp.where(places < doc_ends[..., -1:], passed + 1, 0)


def layer_norm(hidden, gain, shift):
    average = jnp.mean(hidden, axis=-1, keepdims=True)
    centred = hidden - average
    spread = jnp.mean(centred * centred, axis=-1, keepdims=True)
    return centred * lax.rsqrt(spread + epsilon) * gain + shift


def gelu_exact(values_in):
    return jax.nn.gelu(values_in, approximate=False)


def attn_fwd_kernel(q_ref, k_ref, v_ref, segc_ref, segr_ref, out_ref, lse_ref):
    length = q_ref.shape[0]
    scaled = q_ref[...] * jnp.bfloat16(HEAD_DIM ** (-0.5))
    key_pair = k_ref[...]
    value_t = v_ref[...].T
    lanes = lax.broadcasted_iota(jnp.int32, key_pair.shape, 1)
    allowed = segc_ref[...] == segr_ref[...]
    parts = []
    for h in range(2):
        own = (lanes >= h * HEAD_DIM) & (lanes < (h + 1) * HEAD_DIM)
        keys = jnp.where(own, key_pair, jnp.zeros_like(key_pair))
        scores = lax.dot_general(
            keys, scaled, (((1,), (1,)), ((), ())), preferred_element_type=jnp.float32
        )
        scores = jnp.where(allowed, scores, -1e30)
        largest = jnp.max(scores, axis=0, keepdims=True)
        powers = jnp.exp(scores - largest)
        totals = jnp.sum(powers, axis=0, keepdims=True)
        probs = (powers * (1.0 / totals)).astype(jnp.bfloat16)
        parts.append(
            jnp.dot(
                value_t[h * HEAD_DIM : (h + 1) * HEAD_DIM], probs, preferred_element_type=jnp.float32
            )
        )
        lse_ref[0, h : h + 1, :] = largest + jnp.log(totals)
    live = (segc_ref[...] != 0).astype(jnp.float32)
    context = jnp.concatenate(parts, axis=0).T * live
    out_ref[...] = context.astype(jnp.bfloat16)


def attn_bwd_kernel(
    q_ref, k_ref, v_ref, g_ref, segc_ref, segr_ref, lse_ref, dq_ref, dk_ref, dv_ref
):
    scaled = q_ref[...] * jnp.bfloat16(HEAD_DIM ** (-0.5))
    key_pair = k_ref[...]
    value_pair = v_ref[...]
    key_t = key_pair.T
    grads = jnp.where(segc_ref[...] != 0, g_ref[...], jnp.zeros_like(g_ref[...]))
    lanes = lax.broadcasted_iota(jnp.int32, key_pair.shape, 1)
    allowed = segc_ref[...] == segr_ref[...]
    contract = (((1,), (1,)), ((), ()))
    dq_parts = []
    dk = None
    dv = None
    for h in range(2):
        own = (lanes >= h * HEAD_DIM) & (lanes < (h + 1) * HEAD_DIM)
        zero = jnp.zeros_like(key_pair)
        keys = jnp.where(own, key_pair, zero)
        values = jnp.where(own, value_pair, zero)
        queries = jnp.where(own, scaled, zero)
        grad_own = jnp.where(own, grads, zero)
        scores = lax.dot_general(keys, scaled, contract, preferred_element_type=jnp.float32)
        scores = jnp.where(allowed, scores, -1e30)
        probs = jnp.exp(scores - lse_ref[0, h : h + 1, :])
        grad_probs = lax.dot_general(values, grads, contract, preferred_element_type=jnp.float32)
        inner = jnp.sum(probs * grad_probs, axis=0, keepdims=True)
        grad_scores = (probs * (grad_probs - inner)).astype(jnp.bfloat16)
        dv_h = jnp.dot(probs.astype(jnp.bfloat16), grad_own, preferred_element_type=jnp.float32)
        dk_h = jnp.dot(grad_scores, queries, preferred_element_type=jnp.float32)
        dv = dv_h if dv is None else dv + dv_h
        dk = dk_h if dk is None else dk + dk_h
        dq_parts.append(
            jnp.dot(
                key_t[h * HEAD_DIM : (h + 1) * HEAD_DIM],
                grad_scores,
                preferred_element_type=jnp.float32,
            )
        )
    dq = jnp.concatenate(dq_parts, axis=0).T * (HEAD_DIM ** (-0.5))
    dq_ref[...] = dq.astype(jnp.bfloat16)
    dk_ref[...] = dk.astype(jnp.bfloat16)
    dv_ref[...] = dv.astype(jnp.bfloat16)


def attention(projected, seg_col, seg_row):
    length, width3 = projected.shape
    pairs = width3 // 3 // (2 * HEAD_DIM)
    lane = 2 * HEAD_DIM
    col = lambda base: pl.BlockSpec((length, lane), lambda i: (0, base * pairs + i))
    return pl.pallas_call(
        attn_fwd_kernel,
        grid=(pairs,),
        in_specs=[
            col(0),
            col(1),
            col(2),
            pl.BlockSpec((length, 1), lambda i: (0, 0)),
            pl.BlockSpec((1, length), lambda i: (0, 0)),
        ],
        out_specs=[
            pl.BlockSpec((length, lane), lambda i: (0, i)),
            pl.BlockSpec((1, 2, length), lambda i: (i, 0, 0)),
        ],
        out_shape=[
            jax.ShapeDtypeStruct((length, width3 // 3), jnp.bfloat16),
            jax.ShapeDtypeStruct((pairs, 2, length), jnp.float32),
        ],
        compiler_params=pltpu.CompilerParams(vmem_limit_bytes=32 * 2**20),
    )(projected, projected, projected, seg_col, seg_row)


def attention_back(projected, grad_context, seg_col, seg_row, lse):
    length, width3 = projected.shape
    width = width3 // 3
    pairs = width // (2 * HEAD_DIM)
    lane = 2 * HEAD_DIM
    col = lambda base: pl.BlockSpec((length, lane), lambda i: (0, base * pairs + i))
    return pl.pallas_call(
        attn_bwd_kernel,
        grid=(pairs,),
        in_specs=[
            col(0),
            col(1),
            col(2),
            col(0),
            pl.BlockSpec((length, 1), lambda i: (0, 0)),
            pl.BlockSpec((1, length), lambda i: (0, 0)),
            pl.BlockSpec((1, 2, length), lambda i: (i, 0, 0)),
        ],
        out_specs=[col(0)] * 3,
        out_shape=[jax.ShapeDtypeStruct((length, width), jnp.bfloat16)] * 3,
        compiler_params=pltpu.CompilerParams(vmem_limit_bytes=32 * 2**20),
    )(projected, projected, projected, grad_context, seg_col, seg_row, lse)


def body(
    tokens, doc_lengths, qkv_weight, out_weight, up_weight, down_weight, norm_params, out_cotangent
):
    seqs_here, local_len, width = tokens.shape
    group = lax.axis_size("blk") * lax.axis_size("head")
    place = lax.axis_index("blk") * lax.axis_size("head") + lax.axis_index("head")
    full_len = local_len * group

    def to_sequences(v):
        return lax.all_to_all(v, GROUP, split_axis=0, concat_axis=1, tiled=True).reshape(
            -1, width
        )

    def to_positions(v):
        v = v.reshape(seqs_here // group, full_len, width)
        return lax.all_to_all(v, GROUP, split_axis=1, concat_axis=0, tiled=True)

    flat_rows = to_sequences(tokens)
    upstream = to_sequences(out_cotangent).astype(jnp.float32)
    gather = lambda w: lax.all_gather(w, ALL, axis=0, tiled=True)
    wqkv, wout, wup, wdown, wnorm = (
        gather(qkv_weight),
        gather(out_weight),
        gather(up_weight),
        gather(down_weight),
        gather(norm_params),
    )
    norm_values = wnorm.astype(jnp.float32)
    gain_one, shift_one = (norm_values[:, 0], norm_values[:, 1])
    gain_two, shift_two = (norm_values[:, 2], norm_values[:, 3])
    own_lengths = lax.dynamic_slice_in_dim(doc_lengths, place, 1, 0)
    token_segments = segments_of(own_lengths, full_len)
    seg_row = token_segments
    seg_col = token_segments.reshape(full_len, 1)
    projected = jnp.dot(flat_rows, wqkv, preferred_element_type=jnp.float32).astype(jnp.bfloat16)
    context, log_sums = attention(projected, seg_col, seg_row)
    tokens_f = flat_rows.astype(jnp.float32)
    branch = jnp.dot(context, wout, preferred_element_type=jnp.float32)
    first_in = tokens_f + branch
    first_out = layer_norm(first_in, gain_one, shift_one)
    first_low = first_out.astype(jnp.bfloat16)
    pre_act = jnp.dot(first_low, wup, preferred_element_type=jnp.float32)
    act_low = gelu_exact(pre_act).astype(jnp.bfloat16)
    ff_out = jnp.dot(act_low, wdown, preferred_element_type=jnp.float32)
    second_in = first_out + ff_out
    result = layer_norm(second_in, gain_two, shift_two)
    unused_two, second_back = jax.vjp(layer_norm, second_in, gain_two, shift_two)
    grad_second, grad_gain_two, grad_shift_two = second_back(upstream)
    grad_ff = grad_second.astype(jnp.bfloat16)
    scatter = lambda g: lax.psum_scatter(
        g.astype(jnp.bfloat16), ALL, scatter_dimension=0, tiled=True
    ).astype(jnp.float32)
    grad_down = scatter(
        jnp.einsum("tf,td->fd", act_low, grad_ff, preferred_element_type=jnp.float32)
    )
    grad_act = jnp.einsum("td,fd->tf", grad_ff, wdown, preferred_element_type=jnp.float32)
    unused_act, gelu_back = jax.vjp(gelu_exact, pre_act)
    grad_pre = gelu_back(grad_act)[0].astype(jnp.bfloat16)
    grad_up = scatter(
        jnp.einsum("td,tf->df", first_low, grad_pre, preferred_element_type=jnp.float32)
    )
    grad_first = grad_second + jnp.einsum(
        "tf,df->td", grad_pre, wup, preferred_element_type=jnp.float32
    )
    unused_one, first_back = jax.vjp(layer_norm, first_in, gain_one, shift_one)
    grad_first_in, grad_gain_one, grad_shift_one = first_back(grad_first)
    grad_branch = grad_first_in.astype(jnp.bfloat16)
    grad_out_w = scatter(
        jnp.einsum("td,te->de", context, grad_branch, preferred_element_type=jnp.float32)
    )
    grad_context = jnp.einsum(
        "te,de->td", grad_branch, wout, preferred_element_type=jnp.float32
    ).astype(jnp.bfloat16)
    grad_q, grad_k, grad_v = attention_back(projected, grad_context, seg_col, seg_row, log_sums)
    grad_mixed = jnp.concatenate([grad_q, grad_k, grad_v], axis=1)
    grad_qkv = scatter(
        jnp.einsum("td,te->de", flat_rows, grad_mixed, preferred_element_type=jnp.float32)
    )
    grad_tokens = grad_first_in + jnp.einsum(
        "te,de->td", grad_mixed, wqkv, preferred_element_type=jnp.float32
    )
    grad_norm = jnp.stack([grad_gain_one, grad_shift_one, grad_gain_two, grad_shift_two], axis=1)
    grad_norm = lax.psum_scatter(grad_norm, ALL, scatter_dimension=0, tiled=True)
    layer_out = to_positions(result.astype(jnp.bfloat16))
    input_grad = to_positions(grad_tokens.astype(jnp.bfloat16)).astype(jnp.float32)
    return (layer_out, input_grad, grad_qkv, grad_out_w, grad_up, grad_down, grad_norm)


def solution(mesh):
    placed = (
        P("dp", ("blk", "head"), None),
        P("dp", None),
        P(("dp", "blk", "head"), None),
        P(("dp", "blk", "head"), None),
        P(("dp", "blk", "head"), None),
        P(("dp", "blk", "head"), None),
        P(("dp", "blk", "head"), None),
        P("dp", ("blk", "head"), None),
    )
    return jax.shard_map(
        body,
        mesh=mesh,
        in_specs=placed,
        out_specs=(
            P("dp", ("blk", "head"), None),
            P("dp", ("blk", "head"), None),
            P(("dp", "blk", "head"), None),
            P(("dp", "blk", "head"), None),
            P(("dp", "blk", "head"), None),
            P(("dp", "blk", "head"), None),
            P(("dp", "blk", "head"), None),
        ),
        check_vma=False,
    )
```

```python
import functools

import jax
import jax.numpy as jnp
from jax import lax
from jax.experimental import pallas as pl
from jax.experimental.pallas import tpu as pltpu
from jax.sharding import PartitionSpec as P

HEAD_DIM = 64
ALL = ("dp", "blk", "head")
GROUP = ("blk", "head")
LINES = [[0, 2, 4, 6], [1, 3, 5, 7]]
epsilon = 1e-12


def segments_of(doc_lengths, length):
    doc_ends = jnp.cumsum(doc_lengths, axis=-1, dtype=jnp.int32)
    places = jnp.arange(length, dtype=jnp.int32)
    passed = jnp.sum(
        (doc_ends[..., None, :] <= places[:, None]).astype(jnp.int32), axis=-1, dtype=jnp.int32
    )
    return jnp.where(places < doc_ends[..., -1:], passed + 1, 0)


def run(kernel, operands, after=(), in_specs=(), scalars=0, grid=(1,), out_specs=None, scratch_shapes=(), **rest):
    count = len(operands)

    def body(*refs):
        kernel(*refs[:count], *refs[count + len(after) :])

    specs = list(in_specs) + [pl.BlockSpec(memory_space=pl.ANY)] * len(after)
    spec = pltpu.PrefetchScalarGridSpec(
        num_scalar_prefetch=scalars,
        grid=grid,
        in_specs=specs,
        out_specs=out_specs,
        scratch_shapes=scratch_shapes,
    )
    return pl.pallas_call(body, grid_spec=spec, **rest)(*operands, *after)


MIB = 2**20
NO_COST = pl.CostEstimate(flops=1, bytes_accessed=1, transcendentals=0)
LAST = (((1,), (1,)), ((), ()))
FIRST = (((0,), (0,)), ((), ()))


def grant(mib):
    return pltpu.CompilerParams(vmem_limit_bytes=mib * MIB)


def dot(left, right, form=(((1,), (0,)), ((), ()))):
    return lax.dot_general(left, right, form, preferred_element_type=jnp.float32)


def whole(shape):
    return pl.BlockSpec(shape, lambda *_: (0,) * len(shape))


HBM = pl.BlockSpec(memory_space=pltpu.HBM)
SCALARS = pl.BlockSpec(memory_space=pltpu.SMEM)


def attn_fwd_kernel(q_ref, k_ref, v_ref, segc_ref, segr_ref, out_ref, lse_ref):
    length = q_ref.shape[0]
    scaled = q_ref[...] * jnp.bfloat16(HEAD_DIM ** (-0.5))
    key_pair = k_ref[...]
    value_t = v_ref[...].T
    lanes = lax.broadcasted_iota(jnp.int32, key_pair.shape, 1)
    allowed = segc_ref[...] == segr_ref[...]
    parts = []
    for h in range(2):
        own = (lanes >= h * HEAD_DIM) & (lanes < (h + 1) * HEAD_DIM)
        keys = jnp.where(own, key_pair, jnp.zeros_like(key_pair))
        scores = lax.dot_general(
            keys, scaled, (((1,), (1,)), ((), ())), preferred_element_type=jnp.float32
        )
        scores = jnp.where(allowed, scores, -1e30)
        largest = jnp.max(scores, axis=0, keepdims=True)
        powers = jnp.exp(scores - largest)
        totals = jnp.sum(powers, axis=0, keepdims=True)
        probs = (powers * (1.0 / totals)).astype(jnp.bfloat16)
        parts.append(
            jnp.dot(
                value_t[h * HEAD_DIM : (h + 1) * HEAD_DIM], probs, preferred_element_type=jnp.float32
            )
        )
        lse_ref[0, h : h + 1, :] = largest + jnp.log(totals)
    live = (segc_ref[...] != 0).astype(jnp.float32)
    context = jnp.concatenate(parts, axis=0).T * live
    out_ref[...] = context.astype(jnp.bfloat16)


def attn_bwd_kernel(
    q_ref, k_ref, v_ref, g_ref, segc_ref, segr_ref, lse_ref, *refs
):
    out_ref = refs[-1]
    scaled = q_ref[...] * jnp.bfloat16(HEAD_DIM ** (-0.5))
    key_pair = k_ref[...]
    value_pair = v_ref[...]
    key_t = key_pair.T
    grads = jnp.where(segc_ref[...] != 0, g_ref[...], jnp.zeros_like(g_ref[...]))
    lanes = lax.broadcasted_iota(jnp.int32, key_pair.shape, 1)
    allowed = segc_ref[...] == segr_ref[...]
    contract = (((1,), (1,)), ((), ()))
    dq_parts = []
    dk = None
    dv = None
    for h in range(2):
        own = (lanes >= h * HEAD_DIM) & (lanes < (h + 1) * HEAD_DIM)
        zero = jnp.zeros_like(key_pair)
        keys = jnp.where(own, key_pair, zero)
        values = jnp.where(own, value_pair, zero)
        queries = jnp.where(own, scaled, zero)
        grad_own = jnp.where(own, grads, zero)
        scores = lax.dot_general(keys, scaled, contract, preferred_element_type=jnp.float32)
        scores = jnp.where(allowed, scores, -1e30)
        probs = jnp.exp(scores - lse_ref[0, h : h + 1, :])
        grad_probs = lax.dot_general(values, grads, contract, preferred_element_type=jnp.float32)
        inner = jnp.sum(probs * grad_probs, axis=0, keepdims=True)
        grad_scores = (probs * (grad_probs - inner)).astype(jnp.bfloat16)
        dv_h = jnp.dot(probs.astype(jnp.bfloat16), grad_own, preferred_element_type=jnp.float32)
        dk_h = jnp.dot(grad_scores, queries, preferred_element_type=jnp.float32)
        dv = dv_h if dv is None else dv + dv_h
        dk = dk_h if dk is None else dk + dk_h
        dq_parts.append(
            jnp.dot(
                key_t[h * HEAD_DIM : (h + 1) * HEAD_DIM],
                grad_scores,
                preferred_element_type=jnp.float32,
            )
        )
    dq = jnp.concatenate(dq_parts, axis=0).T * (HEAD_DIM ** (-0.5))
    out_ref[0] = dq.astype(jnp.bfloat16)
    out_ref[1] = dk.astype(jnp.bfloat16)
    out_ref[2] = dv.astype(jnp.bfloat16)


def attention(projected, seg_col, seg_row, after=()):
    length, width3 = projected.shape
    width = width3 // 3
    pairs = width // (2 * HEAD_DIM)
    lane = 2 * HEAD_DIM
    col = lambda base: pl.BlockSpec((length, lane), lambda i: (0, base * pairs + i))
    return run(
        attn_fwd_kernel,
        (projected, projected, projected, seg_col, seg_row,),
        after,
        grid=(pairs,),
        in_specs=[
            col(0),
            col(1),
            col(2),
            pl.BlockSpec((length, 1), lambda i: (0, 0)),
            pl.BlockSpec((1, length), lambda i: (0, 0)),
        ],
        out_specs=[
            pl.BlockSpec((length, lane), lambda i: (0, i)),
            pl.BlockSpec((1, 2, length), lambda i: (i, 0, 0)),
        ],
        out_shape=[
            jax.ShapeDtypeStruct((length, width3 // 3), jnp.bfloat16),
            jax.ShapeDtypeStruct((pairs, 2, length), jnp.float32),
        ],
        compiler_params=grant(56),
        cost_estimate=NO_COST,
    )


def attention_back(projected, grad_context, seg_col, seg_row, lse, first=0, count=None, into=None, after=()):
    length, width3 = projected.shape
    width = width3 // 3
    pairs = width // (2 * HEAD_DIM)
    count = count or pairs
    lane = 2 * HEAD_DIM
    col = lambda base: pl.BlockSpec((length, lane), lambda i: (0, base * pairs + first + i))
    into = () if into is None else (into,)
    return run(
        attn_bwd_kernel,
        (projected, projected, projected, grad_context, seg_col, seg_row, lse, *into,),
        after,
        grid=(count,),
        in_specs=[
            col(0),
            col(1),
            col(2),
            col(0),
            pl.BlockSpec((length, 1), lambda i: (0, 0)),
            pl.BlockSpec((1, length), lambda i: (0, 0)),
            pl.BlockSpec((1, 2, length), lambda i: (first + i, 0, 0)),
        ]
        + [HBM] * len(into),
        out_specs=pl.BlockSpec((3, length, lane), lambda i: (0, 0, first + i)),
        out_shape=jax.ShapeDtypeStruct((3, length, width), jnp.bfloat16),
        input_output_aliases={7: 0} if into else {},
        compiler_params=grant(20),
        cost_estimate=NO_COST,
    )


def start_slabs(table_ref, sources, full_ref, sem):
    copies = []
    for source in sources:
        outer, inner, rows, _ = source.shape
        for o in range(outer):
            for i in range(inner):
                start = pl.multiple_of(table_ref[len(copies)], rows)
                copies.append(
                    pltpu.make_async_copy(source.at[o, i], full_ref.at[pl.ds(start, rows)], sem)
                )
                copies[-1].start()
    return copies


def project_kernel(count, table_ref, x_ref, *refs):
    sources, (out_ref, norms_ref, kept_ref, full_ref, sem, back_sem) = refs[:count], refs[count:]
    for copy in start_slabs(table_ref, sources, full_ref, sem):
        copy.wait()
    back = pltpu.make_async_copy(full_ref, kept_ref, back_sem)
    back.start()
    norms_ref[...] = full_ref[:, -128:].astype(jnp.float32).T[:8]
    x = x_ref[...]
    step = 512
    for j in range(out_ref.shape[1] // step):
        here = slice(j * step, (j + 1) * step)
        out_ref[:, here] = dot(x, full_ref[:, here]).astype(jnp.bfloat16)
    back.wait()


def project(x, table, buffers, columns, after=()):
    total, full_columns = x.shape[1], buffers[0].shape[3]
    return run(
        functools.partial(project_kernel, len(buffers)),
        (table, x, *buffers,),
        after,
        in_specs=[SCALARS, whole(x.shape)] + [HBM] * len(buffers),
        out_specs=[whole((x.shape[0], columns)), whole((8, total)), HBM],
        out_shape=[
            jax.ShapeDtypeStruct((x.shape[0], columns), jnp.bfloat16),
            jax.ShapeDtypeStruct((8, total), jnp.float32),
            jax.ShapeDtypeStruct((total, full_columns), jnp.bfloat16),
        ],
        grid=(1,),
        scratch_shapes=[
            pltpu.VMEM((total, full_columns), jnp.bfloat16),
            pltpu.SemaphoreType.DMA,
            pltpu.SemaphoreType.DMA,
        ],
        compiler_params=grant(56),
        cost_estimate=NO_COST,
    )


def normalise(hidden):
    average = jnp.mean(hidden, axis=-1, keepdims=True)
    centred = hidden - average
    spread = jnp.mean(centred * centred, axis=-1, keepdims=True)
    scale = lax.rsqrt(spread + epsilon)
    return centred * scale, scale


def norm_back(grad, xhat, scale, gain):
    inner = grad * gain
    return scale * (
        inner
        - jnp.mean(inner, axis=-1, keepdims=True)
        - xhat * jnp.mean(inner * xhat, axis=-1, keepdims=True)
    )


def branch_kernel(context_ref, w_ref, tokens_ref, norm_ref, xhat_ref, scale_ref, low_ref):
    step = 128
    for j in range(context_ref.shape[0] // step):
        here = slice(j * step, (j + 1) * step)
        first_in = tokens_ref[here].astype(jnp.float32) + dot(context_ref[here], w_ref[...])
        xhat, scale = normalise(first_in)
        xhat_ref[here] = xhat
        scale_ref[here] = scale
        low_ref[here] = (xhat * norm_ref[0:1] + norm_ref[1:2]).astype(jnp.bfloat16)


def branch(context, w_first, tokens, norm_rows, after=()):
    rows, width = context.shape
    return run(
        branch_kernel,
        (context, w_first, tokens, norm_rows,),
        after,
        grid=(1,),
        in_specs=[
            whole((rows, width)),
            pl.BlockSpec((width, width), lambda i: (0, 3)),
            whole((rows, width)),
            whole(norm_rows.shape),
        ],
        out_specs=[whole((rows, width)), whole((rows, 1)), whole((rows, width))],
        out_shape=[
            jax.ShapeDtypeStruct((rows, width), jnp.float32),
            jax.ShapeDtypeStruct((rows, 1), jnp.float32),
            jax.ShapeDtypeStruct((rows, width), jnp.bfloat16),
        ],
        compiler_params=grant(56),
        cost_estimate=NO_COST,
    )


def up_kernel(count, table_ref, x_ref, *refs):
    sources, (act_ref, slope_ref, kept_ref, full_ref, sem, back_sem) = refs[:count], refs[count:]
    for copy in start_slabs(table_ref, sources, full_ref, sem):
        copy.wait()
    back = pltpu.make_async_copy(full_ref, kept_ref, back_sem)
    back.start()
    x = x_ref[...]
    step = 256
    for j in range(act_ref.shape[1] // step):
        here = slice(j * step, (j + 1) * step)
        pre = dot(x, full_ref[:, here])
        below = 0.5 + 0.5 * lax.erf(pre * 0.7071067811865476)
        bell = jnp.exp(pre * pre * -0.5) * 0.3989422804014327
        act_ref[:, here] = (pre * below).astype(jnp.bfloat16)
        slope_ref[:, here] = (below + pre * bell).astype(jnp.bfloat16)
    back.wait()


def up_gelu(x, table, buffers, after=()):
    total, columns = x.shape[1], buffers[0].shape[3]
    rows = x.shape[0]
    return run(
        functools.partial(up_kernel, len(buffers)),
        (table, x, *buffers,),
        after,
        in_specs=[SCALARS, whole(x.shape)] + [HBM] * len(buffers),
        out_specs=[whole((rows, columns)), whole((rows, columns)), HBM],
        out_shape=[
            jax.ShapeDtypeStruct((rows, columns), jnp.bfloat16),
            jax.ShapeDtypeStruct((rows, columns), jnp.bfloat16),
            jax.ShapeDtypeStruct((total, columns), jnp.bfloat16),
        ],
        grid=(1,),
        scratch_shapes=[
            pltpu.VMEM((total, columns), jnp.bfloat16),
            pltpu.SemaphoreType.DMA,
            pltpu.SemaphoreType.DMA,
        ],
        compiler_params=grant(56),
        cost_estimate=NO_COST,
    )


def down_kernel(count, table_ref, act_ref, xhat_ref, norm_ref, up_ref, *refs):
    sources = refs[:count]
    out_ref, second_ref, ff_ref, norms_ref, kept_ref, full_ref, sem, back_sem = refs[count:]
    for copy in start_slabs(table_ref, sources, full_ref, sem):
        copy.wait()
    back = pltpu.make_async_copy(full_ref, kept_ref, back_sem)
    back.start()
    gain_sum = shift_sum = 0.0
    step = 128
    for j in range(act_ref.shape[0] // step):
        here = slice(j * step, (j + 1) * step)
        first_out = xhat_ref[here] * norm_ref[0:1] + norm_ref[1:2]
        xhat, scale = normalise(first_out + dot(act_ref[here], full_ref[...]))
        out_ref[here] = (xhat * norm_ref[2:3] + norm_ref[3:4]).astype(jnp.bfloat16)
        upstream = up_ref[here].astype(jnp.float32)
        grad = norm_back(upstream, xhat, scale, norm_ref[2:3])
        second_ref[here] = grad
        ff_ref[here] = grad.astype(jnp.bfloat16)
        gain_sum = gain_sum + jnp.sum(upstream * xhat, axis=0, keepdims=True)
        shift_sum = shift_sum + jnp.sum(upstream, axis=0, keepdims=True)
    norms_ref[0:1] = gain_sum
    norms_ref[1:2] = shift_sum
    back.wait()


def down_norm(act, table, buffers, xhat, norm_rows, upstream, after=()):
    rows, inner = act.shape
    width = xhat.shape[1]
    return run(
        functools.partial(down_kernel, len(buffers)),
        (table, act, xhat, norm_rows, upstream, *buffers,),
        after,
        in_specs=[
            SCALARS,
            whole(act.shape),
            whole(xhat.shape),
            whole(norm_rows.shape),
            whole(upstream.shape),
        ]
        + [HBM] * len(buffers),
        out_specs=[whole((rows, width))] * 3 + [whole((2, width)), HBM],
        out_shape=[
            jax.ShapeDtypeStruct((rows, width), jnp.bfloat16),
            jax.ShapeDtypeStruct((rows, width), jnp.float32),
            jax.ShapeDtypeStruct((rows, width), jnp.bfloat16),
            jax.ShapeDtypeStruct((2, width), jnp.float32),
            jax.ShapeDtypeStruct((inner, width), jnp.bfloat16),
        ],
        grid=(1,),
        scratch_shapes=[
            pltpu.VMEM((inner, width), jnp.bfloat16),
            pltpu.SemaphoreType.DMA,
            pltpu.SemaphoreType.DMA,
        ],
        compiler_params=grant(56),
        cost_estimate=NO_COST,
    )


def share(core, value, kept_ref, sent_ref, columns):
    places, rows, _ = kept_ref.shape
    value = value.astype(jnp.bfloat16).reshape(places, 2, rows, value.shape[1])
    low, high = value[:, 0], value[:, 1]
    kept_ref[:, :, columns] = jnp.where(core == 0, low, high)
    sent_ref[:, :, columns] = jnp.where(core == 0, high, low)


def rows_grad_kernel(core_ref, left_ref, right_ref, *refs):
    kept_ref, sent_ref, turned_ref = refs[-3:]

    @pl.when(pl.program_id(0) == 0)
    def _():
        turned_ref[...] = left_ref[...].T

    right = right_ref[...].reshape(right_ref.shape[-2:])
    share(core_ref[0], dot(turned_ref[...], right), kept_ref, sent_ref, slice(None))


def rows_grad(core, left, right, rows, into=None, after=()):
    tokens, width = left.shape
    places = width // rows // 2
    step = 512
    each = right.shape[-1] // step
    steps = right.size // tokens // step
    if right.ndim == 3:
        block = pl.BlockSpec((1, tokens, step), lambda i: (i // each, 0, i % each))
    else:
        block = pl.BlockSpec((tokens, step), lambda i: (0, i))
    out = pl.BlockSpec((places, rows, step), lambda i: (0, 0, i))
    into = tuple(into) if into else ()
    columns = into[0].shape[2] if into else steps * step
    return run(
        rows_grad_kernel,
        (core, left, right, *into,),
        after,
        grid=(steps,),
        in_specs=[SCALARS, whole((tokens, width)), block] + [HBM] * len(into),
        out_specs=[out, out],
        out_shape=[jax.ShapeDtypeStruct((places, rows, columns), jnp.bfloat16)] * 2,
        input_output_aliases={3: 0, 4: 1} if into else {},
        scratch_shapes=[pltpu.VMEM((width, tokens), jnp.bfloat16)],
        compiler_params=grant(56),
        cost_estimate=NO_COST,
    )


def ffn_back_kernel(
    core_ref,
    act_ref,
    slope_ref,
    w_down_ref,
    w_up_ref,
    grad_ref,
    low_ref,
    second_ref,
    xhat_ref,
    scale_ref,
    norm_ref,
    down_kept_ref,
    down_sent_ref,
    up_kept_ref,
    up_sent_ref,
    in_ref,
    branch_ref,
    norms_ref,
    turned_ref,
    sum_ref,
):
    step = pl.program_id(0)
    core = core_ref[0]

    @pl.when(step == 0)
    def _():
        turned_ref[...] = low_ref[...].T
        sum_ref[...] = second_ref[...]

    grad = grad_ref[...]
    back = dot(grad, w_down_ref[...], LAST) * slope_ref[...].astype(jnp.float32)
    back = back.astype(jnp.bfloat16)
    share(core, dot(act_ref[...].T, grad), down_kept_ref, down_sent_ref, slice(None))
    share(core, dot(turned_ref[...], back), up_kept_ref, up_sent_ref, slice(None))
    sum_ref[...] += dot(back, w_up_ref[...], LAST)

    @pl.when(step == pl.num_programs(0) - 1)
    def _():
        gain_sum = shift_sum = 0.0
        chunk = 128
        for j in range(sum_ref.shape[0] // chunk):
            here = slice(j * chunk, (j + 1) * chunk)
            first, xhat = sum_ref[here], xhat_ref[here]
            back = norm_back(first, xhat, scale_ref[here], norm_ref[0:1])
            in_ref[here] = back
            branch_ref[here] = back.astype(jnp.bfloat16)
            gain_sum = gain_sum + jnp.sum(first * xhat, axis=0, keepdims=True)
            shift_sum = shift_sum + jnp.sum(first, axis=0, keepdims=True)
        norms_ref[0:1] = gain_sum
        norms_ref[1:2] = shift_sum


def ffn_back(core, act, slope, w_down, w_up, grad, low, second, xhat, scale, norm_rows, rows, ff_rows):
    tokens, inner = act.shape
    width = grad.shape[1]
    step = 512
    places = width // rows // 2
    ff_places = inner // ff_rows // 2
    here = step // ff_rows // 2
    columns = pl.BlockSpec((tokens, step), lambda i: (0, i))
    down_out = pl.BlockSpec((here, ff_rows, width), lambda i: (i, 0, 0))
    up_out = pl.BlockSpec((places, rows, step), lambda i: (0, 0, i))
    down_shape = jax.ShapeDtypeStruct((ff_places, ff_rows, width), jnp.bfloat16)
    up_shape = jax.ShapeDtypeStruct((places, rows, inner + width + 128), jnp.bfloat16)
    return run(
        ffn_back_kernel,
        (core, act, slope, w_down, w_up, grad, low, second, xhat, scale, norm_rows),
        grid=(inner // step,),
        in_specs=[
            SCALARS,
            columns,
            columns,
            pl.BlockSpec((step, width), lambda i: (i, 0)),
            pl.BlockSpec((width, step), lambda i: (0, i)),
            whole((tokens, width)),
            whole((tokens, width)),
            whole((tokens, width)),
            whole((tokens, width)),
            whole((tokens, 1)),
            whole(norm_rows.shape),
        ],
        out_specs=[down_out, down_out, up_out, up_out]
        + [whole((tokens, width))] * 2
        + [whole((2, width))],
        out_shape=[
            down_shape,
            down_shape,
            up_shape,
            up_shape,
            jax.ShapeDtypeStruct((tokens, width), jnp.float32),
            jax.ShapeDtypeStruct((tokens, width), jnp.bfloat16),
            jax.ShapeDtypeStruct((2, width), jnp.float32),
        ],
        scratch_shapes=[
            pltpu.VMEM((width, tokens), jnp.bfloat16),
            pltpu.VMEM((tokens, width), jnp.float32),
        ],
        compiler_params=grant(56),
        cost_estimate=NO_COST,
    )


def out_grad_kernel(
    core_ref,
    context_ref,
    grad_ref,
    w_ref,
    one_ref,
    two_ref,
    kept_in,
    sent_in,
    back_ref,
    kept_hbm,
    sent_hbm,
    kept_ref,
    sent_ref,
    sems,
):
    core = core_ref[0]
    width = w_ref.shape[0]
    grad = grad_ref[...]
    turned = context_ref[...].T
    step = 256
    for j in range(width // step):
        here = slice(j * step, (j + 1) * step)
        share(core, dot(turned, grad[:, here]), kept_ref, sent_ref, here)
    norms = jnp.concatenate([one_ref[...], two_ref[...], jnp.zeros((124, width), jnp.float32)], 0)
    share(core, norms.T, kept_ref, sent_ref, slice(width, width + 128))
    last = pl.ds(kept_hbm.shape[2] - width - 128, width + 128)
    copies = [
        pltpu.make_async_copy(kept_ref, kept_hbm.at[:, :, last], sems.at[0]),
        pltpu.make_async_copy(sent_ref, sent_hbm.at[:, :, last], sems.at[1]),
    ]
    for copy in copies:
        copy.start()
    for j in range(width // step):
        here = slice(j * step, (j + 1) * step)
        back_ref[:, here] = dot(grad, w_ref[here], LAST).astype(jnp.bfloat16)
    for copy in copies:
        copy.wait()


def out_grad(core, context, grad, w_first, norms_one, norms_two, kept, sent, after=()):
    tokens, width = context.shape
    part = pltpu.VMEM(kept.shape[:2] + (width + 128,), jnp.bfloat16)
    out = kept.shape
    return run(
        out_grad_kernel,
        (core, context, grad, w_first, norms_one, norms_two, kept, sent),
        after,
        grid=(1,),
        in_specs=[
            SCALARS,
            whole((tokens, width)),
            whole((tokens, width)),
            pl.BlockSpec((width, width), lambda i: (0, 3)),
            whole((2, width)),
            whole((2, width)),
            HBM,
            HBM,
        ],
        out_specs=[whole((tokens, width)), HBM, HBM],
        out_shape=[
            jax.ShapeDtypeStruct((tokens, width), jnp.bfloat16),
            jax.ShapeDtypeStruct(out, jnp.bfloat16),
            jax.ShapeDtypeStruct(out, jnp.bfloat16),
        ],
        input_output_aliases={6: 1, 7: 2},
        scratch_shapes=[part, part, pltpu.SemaphoreType.DMA((2,))],
        compiler_params=grant(56),
        cost_estimate=NO_COST,
    )


def tokens_grad_kernel(grad_ref, w_ref, first_ref, out_ref, sum_ref):
    step = pl.program_id(0)

    @pl.when(step == 0)
    def _():
        sum_ref[...] = first_ref[...]

    sum_ref[...] += dot(grad_ref[0], w_ref[...], LAST)

    @pl.when(step == pl.num_programs(0) - 1)
    def _():
        out_ref[...] = sum_ref[...].astype(jnp.bfloat16)


def tokens_grad(grad_mixed, w_first, first, after=()):
    count, tokens, width = grad_mixed.shape
    return run(
        tokens_grad_kernel,
        (grad_mixed, w_first, first,),
        after,
        grid=(count,),
        in_specs=[
            pl.BlockSpec((1, tokens, width), lambda i: (i, 0, 0)),
            pl.BlockSpec((width, width), lambda i: (0, i)),
            whole((tokens, width)),
        ],
        out_specs=whole((tokens, width)),
        out_shape=jax.ShapeDtypeStruct((tokens, width), jnp.bfloat16),
        scratch_shapes=[pltpu.VMEM((tokens, width), jnp.float32)],
        compiler_params=grant(56),
        cost_estimate=NO_COST,
    )


def fold_kernel(place_ref, kept_ref, came_ref, a_own_ref, a_out_ref, b_own_ref, b_out_ref):
    x, y = place_ref[0], place_ref[1]
    half = a_own_ref.shape[2]
    part = lambda ref, i, j, rows: ref[0, i, j, rows].astype(jnp.float32)
    low, high = pl.ds(0, half), pl.ds(half, half)
    for i in range(2):
        both = lambda a, b, rows: (part(kept_ref, a, b, rows) + part(came_ref, a, b, rows)).astype(
            jnp.bfloat16
        )
        a_own_ref[0, i] = both(i, y, low)
        a_out_ref[0, i] = both(i, 1 - y, low)
        b_own_ref[0, i] = both(x, i, high)
        b_out_ref[0, i] = both(1 - x, i, high)


def fold_plane_kernel(place_ref, *refs):
    for i in range(2):
        own_ref, came_ref = refs[2 * i], refs[2 * i + 1]
        keep_ref, out_ref = refs[4 + 2 * i], refs[5 + 2 * i]
        place = place_ref[i]
        for ref, index in ((keep_ref, place), (out_ref, 1 - place)):
            total = own_ref[0, index].astype(jnp.float32) + came_ref[0, index].astype(jnp.float32)
            ref[0] = total.astype(jnp.bfloat16)


def fold_plane(place, a_own, a_came, b_own, b_came, after=()):
    zs, both, rows, columns = a_own.shape
    block = pl.BlockSpec((1, both, rows, columns), lambda i: (i, 0, 0, 0))
    out = pl.BlockSpec((1, rows, columns), lambda i: (i, 0, 0))
    return run(
        fold_plane_kernel,
        (place, a_own, a_came, b_own, b_came),
        after,
        grid=(zs,),
        in_specs=[SCALARS] + [block] * 4,
        out_specs=[out] * 4,
        out_shape=[jax.ShapeDtypeStruct((zs, rows, columns), jnp.bfloat16)] * 4,
        compiler_params=grant(20),
        cost_estimate=NO_COST,
    )


def fold(place, kept, came, after=()):
    zs, xs, ys, rows, columns = kept.shape
    out = pl.BlockSpec((1, 2, rows // 2, columns), lambda i: (i, 0, 0, 0))
    block = pl.BlockSpec((1, xs, ys, rows, columns), lambda i: (i, 0, 0, 0, 0))
    return run(
        fold_kernel,
        (place, kept, came,),
        after,
        grid=(zs,),
        in_specs=[SCALARS, block, block],
        out_specs=[out] * 4,
        out_shape=[jax.ShapeDtypeStruct((zs, 2, rows // 2, columns), jnp.bfloat16)] * 4,
        compiler_params=grant(20),
        cost_estimate=NO_COST,
    )


def gate(values, after=()):
    return run(
        lambda *refs: None,
        values,
        after,
        in_specs=[pl.BlockSpec(memory_space=pl.ANY)] * len(values),
        out_specs=[pl.BlockSpec(memory_space=pl.ANY)] * len(values),
        out_shape=[jax.ShapeDtypeStruct(v.shape, v.dtype) for v in values],
        input_output_aliases={i: i for i in range(len(values))},
    )


def routes(move):
    pairs = []
    for place in range(32):
        z, x, y, c = place // 8, place // 4 % 2, place // 2 % 2, place % 2
        target = move(z, x, y, c)
        if target is not None:
            tz, tx, ty, tc = target
            pairs.append((place, tz * 8 + tx * 4 + ty * 2 + tc))
    return pairs


ROUTE_X = routes(lambda z, x, y, c: (z, 1 - x, y, c))
ROUTE_Y = routes(lambda z, x, y, c: (z, x, 1 - y, c))
ROUTE_C = routes(lambda z, x, y, c: (z, x, y, 1 - c))


def route_up(low, high):
    return routes(lambda z, x, y, c: (z + 1, x, y, c) if low <= z <= high else None)


def route_down(low, high):
    return routes(lambda z, x, y, c: (z - 1, x, y, c) if low <= z <= high else None)


def send(value, route):
    return lax.ppermute(value, ALL, route)


def coordinates():
    dp = lax.axis_index("dp")
    return dp // 2, dp % 2, lax.axis_index("blk"), lax.axis_index("head")


def line_gather(own, below, above, step):
    if step == 0:
        return send(own, route_up(0, 2)), send(own, route_down(1, 3))
    return send(below, route_up(step, 2)), send(above, route_down(1, 3 - step))


def line_blocks(own, below, above, z):
    blocks = []
    for target in range(4):
        value = own
        for place in range(4):
            if place > target:
                value = jnp.where(z == place, below[place - target - 1], value)
            elif place < target:
                value = jnp.where(z == place, above[target - place - 1], value)
        blocks.append(value)
    return blocks


def line_scatter(blocks, z, step, from_above=None, from_below=None):
    down = pick(blocks, jnp.clip(z - 3 + step, 0, 3), 0)
    up = pick(blocks, jnp.clip(z + 3 - step, 0, 3), 0)
    if step:
        down = sum_of([down, from_above]).astype(jnp.bfloat16)
        up = sum_of([up, from_below]).astype(jnp.bfloat16)
    return down, up


def line_send(down, up, step):
    return send(down, route_down(3 - step, 3)), send(up, route_up(0, step))


def sum_of(values):
    total = None
    for value in values:
        value = value.astype(jnp.float32)
        total = value if total is None else total + value
    return total


def slot_rows(buffers, rows):
    z, x, y, c = coordinates()
    tables = []
    for value, part, axis, dx, dy, dc in buffers:
        js = jnp.arange(value.shape[0])[:, None]
        zs = jnp.arange(4)[None, :]
        sx = (x ^ dx ^ js) if axis == 0 else x ^ dx
        sy = (y ^ dy ^ js) if axis == 1 else y ^ dy
        device = ((zs * 2 + sx) * 2 + sy) * 2 + (c ^ dc)
        tables.append((device * rows + part * (rows // 2)).reshape(-1))
    return jnp.concatenate(tables).astype(jnp.int32)


def pick(value, index, axis):
    return lax.dynamic_index_in_dim(value, index, axis, keepdims=False)


def fold_cores(kept, came, after):
    z, x, y, c = coordinates()
    shape = (4, 2, 2) + kept.shape[1:]
    return fold(jnp.stack([x, y]), kept.reshape(shape), came.reshape(shape), after)


def natural(kept, sent):
    return jnp.stack([kept, sent], axis=1).reshape(-1, kept.shape[2])


def joined_shards(qkv_weight, out_weight, norm_params):
    norm_wide = jnp.pad(norm_params, ((0, 0), (0, 128 - norm_params.shape[1])))
    return jnp.concatenate([qkv_weight, out_weight, norm_wide], axis=1)


def split_up(grad, width):
    inner = grad.shape[1] - width - 128
    last = inner + width
    return grad[:, :inner], grad[:, inner:last], grad[:, last : last + 4]


def buffers_of(a2, ay, b2, bx):
    return [(a2, 0, 0, 0, 0), (ay, 0, 0, 0, 1), (b2, 1, 1, 0, 0), (bx, 1, 1, 1, 0)]


def with_partner(shard, own, partner):
    buffers = [b + (0,) for b in own]
    buffers += [(v,) + b[1:] + (1,) for v, b in zip(partner, own)]
    return slot_rows(buffers, shard.shape[0]), [b[0] for b in buffers]


def body_lines(
    tokens, doc_lengths, qkv_weight, out_weight, up_weight, down_weight, norm_params, out_cotangent
):
    seqs_here, local_len, width = tokens.shape
    full_len = local_len * 4
    z, x, y, c = coordinates()
    place = y * 2 + c
    core = c.reshape(1)
    slab, ff_slab = up_weight.shape[0], down_weight.shape[0]
    exchange = lambda v: lax.all_to_all(v, GROUP, split_axis=0, concat_axis=0, tiled=True)
    to_sequence = lambda v: exchange(v).reshape(full_len, width)
    to_positions = lambda v: exchange(v.reshape(seqs_here, local_len, width))
    own_lengths = lax.dynamic_slice_in_dim(doc_lengths, place, 1, 0)
    seg_row = segments_of(own_lengths, full_len)
    seg_col = seg_row.reshape(full_len, 1)
    first_own, up_own = joined_shards(qkv_weight, out_weight, norm_params), up_weight
    half, ff_half = slab // 2, ff_slab // 2

    fb0, fa0 = line_gather(first_own, None, None, 0)
    ub0, ua0 = line_gather(up_own, None, None, 0)
    both = exchange(jnp.concatenate([tokens, out_cotangent], axis=1))

    fb0, fa0, ub0, ua0, down_a, down_b = gate(
        (fb0, fa0, ub0, ua0, down_weight[:ff_half], down_weight[ff_half:])
    )
    down_ax, down_by = send(down_a, ROUTE_X), send(down_b, ROUTE_Y)
    fb1, fa1 = line_gather(None, fb0, fa0, 1)
    ub1, ua1 = line_gather(None, ub0, ua0, 1)

    fb1, fa1, ub1, ua1, down_ax, down_by = gate(
        (fb1, fa1, ub1, ua1, down_ax, down_by), (both,)
    )
    fb2, fa2 = line_gather(None, fb1, fa1, 2)
    ub2, ua2 = line_gather(None, ub1, ua1, 2)

    blocks = line_blocks(first_own, (fb0, fb1, fb2), (fa0, fa1, fa2), z)
    a, b, down_own = gate(
        (
            jnp.stack([v[:half] for v in blocks]),
            jnp.stack([v[half:] for v in blocks]),
            jnp.stack([down_a, down_ax, down_b, down_by]),
        ),
        (ub2, ua2),
    )
    ax, by = send(a, ROUTE_X), send(b, ROUTE_Y)
    down_line = lax.all_gather(down_own, "dp", axis_index_groups=LINES)
    blocks = line_blocks(up_own, (ub0, ub1, ub2), (ua0, ua1, ua2), z)

    a2, b2, up_a, up_b = gate(
        (
            jnp.stack([a, ax]),
            jnp.stack([b, by]),
            jnp.stack([v[:half] for v in blocks]),
            jnp.stack([v[half:] for v in blocks]),
        )
    )
    ay, bx = send(a2, ROUTE_Y), send(b2, ROUTE_X)
    a2c, b2c = send(a2, ROUTE_C), send(b2, ROUTE_C)
    up_ax, up_by = send(up_a, ROUTE_X), send(up_b, ROUTE_Y)
    rows, upstream = (
        v.reshape(full_len, width) for v in (both[:, :local_len], both[:, local_len:])
    )

    ay, bx, up_a2, up_b2, a2c, b2c, down_line = gate(
        (ay, bx, jnp.stack([up_a, up_ax]), jnp.stack([up_b, up_by]), a2c, b2c, down_line)
    )
    ayc, bxc = send(ay, ROUTE_C), send(bx, ROUTE_C)
    up_ay, up_bx = send(up_a2, ROUTE_Y), send(up_b2, ROUTE_X)
    up_a2c, up_b2c = send(up_a2, ROUTE_C), send(up_b2, ROUTE_C)
    table, buffers = with_partner(
        first_own, buffers_of(a2, ay, b2, bx), (a2c, ayc, b2c, bxc)
    )
    projected, norm_rows, w_first = project(rows, table, buffers, 3 * width)
    context, log_sums = attention(projected, seg_col, seg_row)
    down_line = jnp.swapaxes(down_line, 0, 1)

    up_ay, up_bx, up_a2c, up_b2c, down_a2, down_b2, context = gate(
        (
            up_ay,
            up_bx,
            up_a2c,
            up_b2c,
            down_line[:2],
            down_line[2:],
            context,
        )
    )
    up_ayc, up_bxc = send(up_ay, ROUTE_C), send(up_bx, ROUTE_C)
    down_ay, down_bx = send(down_a2, ROUTE_Y), send(down_b2, ROUTE_X)
    down_a2c, down_b2c = send(down_a2, ROUTE_C), send(down_b2, ROUTE_C)
    xhat, scale, first_low = branch(context, w_first, rows, norm_rows)
    table, buffers = with_partner(
        up_own, buffers_of(up_a2, up_ay, up_b2, up_bx), (up_a2c, up_ayc, up_b2c, up_bxc)
    )
    act, slope, w_up = up_gelu(first_low, table, buffers)

    down_ay, down_bx, down_a2c, down_b2c, act = gate((down_ay, down_bx, down_a2c, down_b2c, act))
    down_ayc, down_bxc = send(down_ay, ROUTE_C), send(down_bx, ROUTE_C)
    table, buffers = with_partner(
        down_weight,
        buffers_of(down_a2, down_ay, down_b2, down_bx),
        (down_a2c, down_ayc, down_b2c, down_bxc),
    )
    result, grad_second, grad_ff, norms_two, w_down = down_norm(
        act, table, buffers, xhat, norm_rows, upstream
    )

    low = lambda *v: sum_of(v).astype(jnp.bfloat16)
    place_xy = jnp.stack([x, y])
    layer_out = to_positions(result)
    down_kept, down_sent, up_kept, up_sent, grad_first_in, grad_branch, norms_one = ffn_back(
        core,
        act,
        slope,
        w_down,
        w_up,
        grad_ff,
        first_low,
        grad_second,
        xhat,
        scale,
        norm_rows,
        slab,
        ff_slab,
    )

    down_sent, grad_branch = gate((down_sent, grad_branch), (layer_out,))
    down_came = send(down_sent, ROUTE_C)
    grad_context, up_kept, up_sent = out_grad(
        core, context, grad_branch, w_first, norms_one, norms_two, up_kept, up_sent
    )

    da_own, da_out, db_own, db_out = fold_cores(down_kept, down_came, (grad_context,))
    da_out, db_out, up_sent, grad_context = gate((da_out, db_out, up_sent, grad_context))
    da_in, db_in = send(da_out, ROUTE_Y), send(db_out, ROUTE_X)
    up_came = send(up_sent, ROUTE_C)
    grad_mixed = attention_back(projected, grad_context, seg_col, seg_row, log_sums)

    ua_own, ua_out, ub_own, ub_out = fold_cores(up_kept, up_came, (grad_mixed, da_in, db_in))
    down_blocks = jnp.concatenate([low(da_own, da_in), low(db_own, db_in)], axis=1)
    ua_out, ub_out, down_blocks, grad_mixed = gate((ua_out, ub_out, down_blocks, grad_mixed))
    ua_in, ub_in = send(ua_out, ROUTE_Y), send(ub_out, ROUTE_X)
    down_sum = lax.psum_scatter(
        down_blocks, "dp", scatter_dimension=0, axis_index_groups=LINES, tiled=False
    )
    last_kept, last_sent = rows_grad(core, rows, grad_mixed, slab)
    grad_tokens = tokens_grad(grad_mixed, w_first, grad_first_in, (last_sent,))

    ua_own, ua_out, ub_own, ub_out = fold_plane(
        place_xy, ua_own, ua_in, ub_own, ub_in, (grad_tokens,)
    )
    ua_out, ub_out, last_sent = gate((ua_out, ub_out, last_sent))
    ua_in2, ub_in2 = send(ua_out, ROUTE_X), send(ub_out, ROUTE_Y)
    last_came = send(last_sent, ROUTE_C)

    la_own, la_out, lb_own, lb_out = fold_cores(last_kept, last_came, (ua_in2, ub_in2))
    up_blocks = jnp.concatenate([low(ua_own, ua_in2), low(ub_own, ub_in2)], axis=1)
    up_blocks, la_out, lb_out, down_sum = gate((up_blocks, la_out, lb_out, down_sum))
    up_sum = lax.psum_scatter(
        up_blocks, "dp", scatter_dimension=0, axis_index_groups=LINES, tiled=False
    )
    la_in, lb_in = send(la_out, ROUTE_Y), send(lb_out, ROUTE_X)
    da_in = send(pick(down_sum[:2], 1 - x, 0), ROUTE_X)
    db_in = send(pick(down_sum[2:], 1 - y, 0), ROUTE_Y)

    la_own, la_out, lb_own, lb_out = fold_plane(
        place_xy, la_own, la_in, lb_own, lb_in, (da_in, db_in)
    )
    la_out, lb_out, grad_tokens = gate((la_out, lb_out, grad_tokens))
    la_in2, lb_in2 = send(la_out, ROUTE_X), send(lb_out, ROUTE_Y)
    grad_down = jnp.concatenate(
        [sum_of([pick(down_sum[:2], x, 0), da_in]), sum_of([pick(down_sum[2:], y, 0), db_in])],
        axis=0,
    )

    last_blocks = jnp.concatenate([low(la_own, la_in2), low(lb_own, lb_in2)], axis=1)
    *goes, grad_tokens = gate((*line_scatter(last_blocks, z, 0), grad_tokens))
    input_grad = to_positions(grad_tokens)
    from_above, from_below = line_send(*goes, 0)

    goes = gate(line_scatter(last_blocks, z, 1, from_above, from_below))
    from_above, from_below = line_send(*goes, 1)

    goes = gate(line_scatter(last_blocks, z, 2, from_above, from_below), (input_grad, up_sum))
    from_above, from_below = line_send(*goes, 2)
    grad_qkv = sum_of([pick(last_blocks, z, 0), from_above, from_below])
    grad_up, grad_out, grad_norm = split_up(up_sum.astype(jnp.float32), width)
    return (
        layer_out,
        input_grad.astype(jnp.float32),
        grad_qkv,
        grad_out,
        grad_up,
        grad_down,
        grad_norm,
    )


def body_any(
    tokens, doc_lengths, qkv_weight, out_weight, up_weight, down_weight, norm_params, out_cotangent
):
    seqs_here, local_len, width = tokens.shape
    ff = up_weight.shape[1]
    full_len = local_len * lax.axis_size("blk") * lax.axis_size("head")
    place = lax.axis_index("blk") * lax.axis_size("head") + lax.axis_index("head")
    core = jnp.zeros((1,), jnp.int32)
    slab, ff_slab = width // 32, ff // 32
    exchange = lambda v: lax.all_to_all(v, GROUP, split_axis=0, concat_axis=0, tiled=True)
    to_sequence = lambda v: exchange(v).reshape(full_len, width)
    to_positions = lambda v: exchange(v.reshape(seqs_here, local_len, width))

    def gather(shard):
        return core, [lax.all_gather(shard, ALL, axis=0, tiled=True)[None, None]]

    def scatter(kept, sent):
        total = lax.psum_scatter(natural(kept, sent), ALL, scatter_dimension=0, tiled=True)
        return total.astype(jnp.float32)

    rows = to_sequence(tokens)
    upstream = to_sequence(out_cotangent)
    own_lengths = lax.dynamic_slice_in_dim(doc_lengths, place, 1, 0)
    seg_row = segments_of(own_lengths, full_len)
    seg_col = seg_row.reshape(full_len, 1)
    first_slots = gather(joined_shards(qkv_weight, out_weight, norm_params))
    projected, norm_rows, w_first = project(rows, *first_slots, 3 * width)
    context, log_sums = attention(projected, seg_col, seg_row)
    xhat, scale, first_low = branch(context, w_first, rows, norm_rows)
    act, slope, w_up = up_gelu(first_low, *gather(up_weight))
    result, grad_second, grad_ff, norms_two, w_down = down_norm(
        act, *gather(down_weight), xhat, norm_rows, upstream
    )
    down_kept, down_sent, up_kept, up_sent, grad_first_in, grad_branch, norms_one = ffn_back(
        core,
        act,
        slope,
        w_down,
        w_up,
        grad_ff,
        first_low,
        grad_second,
        xhat,
        scale,
        norm_rows,
        slab,
        ff_slab,
    )
    grad_down = scatter(down_kept, down_sent)
    grad_context, up_kept, up_sent = out_grad(
        core, context, grad_branch, w_first, norms_one, norms_two, up_kept, up_sent
    )
    grad_up, grad_out, grad_norm = split_up(scatter(up_kept, up_sent), width)
    grad_mixed = attention_back(projected, grad_context, seg_col, seg_row, log_sums)
    grad_qkv = scatter(*rows_grad(core, rows, grad_mixed, slab))
    grad_tokens = tokens_grad(grad_mixed, w_first, grad_first_in)
    return (
        to_positions(result),
        to_positions(grad_tokens).astype(jnp.float32),
        grad_qkv,
        grad_out,
        grad_up,
        grad_down,
        grad_norm,
    )


def solution(mesh):
    sizes = tuple(mesh.shape[name] for name in ALL)
    body = body_lines if sizes == (8, 2, 2) else body_any
    placed = (
        P("dp", ("blk", "head"), None),
        P("dp", None),
        P(("dp", "blk", "head"), None),
        P(("dp", "blk", "head"), None),
        P(("dp", "blk", "head"), None),
        P(("dp", "blk", "head"), None),
        P(("dp", "blk", "head"), None),
        P("dp", ("blk", "head"), None),
    )
    return jax.shard_map(
        body,
        mesh=mesh,
        in_specs=placed,
        out_specs=(
            P("dp", ("blk", "head"), None),
            P("dp", ("blk", "head"), None),
            P(("dp", "blk", "head"), None),
            P(("dp", "blk", "head"), None),
            P(("dp", "blk", "head"), None),
            P(("dp", "blk", "head"), None),
            P(("dp", "blk", "head"), None),
        ),
        check_vma=False,
    )
```

```python
import functools

import jax
import jax.numpy as jnp
from jax import lax
from jax.experimental import pallas as pl
from jax.experimental.pallas import tpu as pltpu
from jax.sharding import PartitionSpec as P

HEAD_DIM = 64
ALL = ("dp", "blk", "head")
GROUP = ("blk", "head")
LINES = [[0, 2, 4, 6], [1, 3, 5, 7]]
epsilon = 1e-12


def segments_of(doc_lengths, length):
    doc_ends = jnp.cumsum(doc_lengths, axis=-1, dtype=jnp.int32)
    places = jnp.arange(length, dtype=jnp.int32)
    passed = jnp.sum(
        (doc_ends[..., None, :] <= places[:, None]).astype(jnp.int32), axis=-1, dtype=jnp.int32
    )
    return jnp.where(places < doc_ends[..., -1:], passed + 1, 0)


def run(kernel, operands, after=(), in_specs=(), scalars=0, grid=(1,), out_specs=None, scratch_shapes=(), **rest):
    count = len(operands)

    def body(*refs):
        kernel(*refs[:count], *refs[count + len(after) :])

    specs = list(in_specs) + [pl.BlockSpec(memory_space=pl.ANY)] * len(after)
    spec = pltpu.PrefetchScalarGridSpec(
        num_scalar_prefetch=scalars,
        grid=grid,
        in_specs=specs,
        out_specs=out_specs,
        scratch_shapes=scratch_shapes,
    )
    return pl.pallas_call(body, grid_spec=spec, **rest)(*operands, *after)


MIB = 2**20
NO_COST = pl.CostEstimate(flops=1, bytes_accessed=1, transcendentals=0)
LAST = (((1,), (1,)), ((), ()))
FIRST = (((0,), (0,)), ((), ()))


def grant(mib):
    return pltpu.CompilerParams(vmem_limit_bytes=mib * MIB)


def dot(left, right, form=(((1,), (0,)), ((), ()))):
    return lax.dot_general(left, right, form, preferred_element_type=jnp.float32)


def whole(shape):
    return pl.BlockSpec(shape, lambda *_: (0,) * len(shape))


HBM = pl.BlockSpec(memory_space=pltpu.HBM)
SCALARS = pl.BlockSpec(memory_space=pltpu.SMEM)


def attn_fwd_kernel(q_ref, k_ref, v_ref, segc_ref, segr_ref, out_ref, lse_ref):
    length = q_ref.shape[0]
    scaled = q_ref[...] * jnp.bfloat16(HEAD_DIM ** (-0.5))
    key_pair = k_ref[...]
    value_t = v_ref[...].T
    lanes = lax.broadcasted_iota(jnp.int32, key_pair.shape, 1)
    allowed = segc_ref[...] == segr_ref[...]
    parts = []
    for h in range(2):
        own = (lanes >= h * HEAD_DIM) & (lanes < (h + 1) * HEAD_DIM)
        keys = jnp.where(own, key_pair, jnp.zeros_like(key_pair))
        scores = lax.dot_general(
            keys, scaled, (((1,), (1,)), ((), ())), preferred_element_type=jnp.float32
        )
        scores = jnp.where(allowed, scores, -1e30)
        largest = jnp.max(scores, axis=0, keepdims=True)
        powers = jnp.exp(scores - largest)
        totals = jnp.sum(powers, axis=0, keepdims=True)
        probs = (powers * (1.0 / totals)).astype(jnp.bfloat16)
        parts.append(
            jnp.dot(
                value_t[h * HEAD_DIM : (h + 1) * HEAD_DIM], probs, preferred_element_type=jnp.float32
            )
        )
        lse_ref[0, h : h + 1, :] = largest + jnp.log(totals)
    live = (segc_ref[...] != 0).astype(jnp.float32)
    context = jnp.concatenate(parts, axis=0).T * live
    out_ref[...] = context.astype(jnp.bfloat16)


def attn_bwd_kernel(
    q_ref, k_ref, v_ref, g_ref, segc_ref, segr_ref, lse_ref, *refs
):
    out_ref = refs[-1]
    scaled = q_ref[...] * jnp.bfloat16(HEAD_DIM ** (-0.5))
    key_pair = k_ref[...]
    value_pair = v_ref[...]
    key_t = key_pair.T
    grads = jnp.where(segc_ref[...] != 0, g_ref[...], jnp.zeros_like(g_ref[...]))
    lanes = lax.broadcasted_iota(jnp.int32, key_pair.shape, 1)
    allowed = segc_ref[...] == segr_ref[...]
    contract = (((1,), (1,)), ((), ()))
    dq_parts = []
    dk = None
    dv = None
    for h in range(2):
        own = (lanes >= h * HEAD_DIM) & (lanes < (h + 1) * HEAD_DIM)
        zero = jnp.zeros_like(key_pair)
        keys = jnp.where(own, key_pair, zero)
        values = jnp.where(own, value_pair, zero)
        queries = jnp.where(own, scaled, zero)
        grad_own = jnp.where(own, grads, zero)
        scores = lax.dot_general(keys, scaled, contract, preferred_element_type=jnp.float32)
        scores = jnp.where(allowed, scores, -1e30)
        probs = jnp.exp(scores - lse_ref[0, h : h + 1, :])
        grad_probs = lax.dot_general(values, grads, contract, preferred_element_type=jnp.float32)
        inner = jnp.sum(probs * grad_probs, axis=0, keepdims=True)
        grad_scores = (probs * (grad_probs - inner)).astype(jnp.bfloat16)
        dv_h = jnp.dot(probs.astype(jnp.bfloat16), grad_own, preferred_element_type=jnp.float32)
        dk_h = jnp.dot(grad_scores, queries, preferred_element_type=jnp.float32)
        dv = dv_h if dv is None else dv + dv_h
        dk = dk_h if dk is None else dk + dk_h
        dq_parts.append(
            jnp.dot(
                key_t[h * HEAD_DIM : (h + 1) * HEAD_DIM],
                grad_scores,
                preferred_element_type=jnp.float32,
            )
        )
    dq = jnp.concatenate(dq_parts, axis=0).T * (HEAD_DIM ** (-0.5))
    out_ref[0] = dq.astype(jnp.bfloat16)
    out_ref[1] = dk.astype(jnp.bfloat16)
    out_ref[2] = dv.astype(jnp.bfloat16)


def attention(projected, seg_col, seg_row, after=()):
    length, width3 = projected.shape
    width = width3 // 3
    pairs = width // (2 * HEAD_DIM)
    lane = 2 * HEAD_DIM
    col = lambda base: pl.BlockSpec((length, lane), lambda i: (0, base * pairs + i))
    return run(
        attn_fwd_kernel,
        (projected, projected, projected, seg_col, seg_row,),
        after,
        grid=(pairs,),
        in_specs=[
            col(0),
            col(1),
            col(2),
            pl.BlockSpec((length, 1), lambda i: (0, 0)),
            pl.BlockSpec((1, length), lambda i: (0, 0)),
        ],
        out_specs=[
            pl.BlockSpec((length, lane), lambda i: (0, i)),
            pl.BlockSpec((1, 2, length), lambda i: (i, 0, 0)),
        ],
        out_shape=[
            jax.ShapeDtypeStruct((length, width3 // 3), jnp.bfloat16),
            jax.ShapeDtypeStruct((pairs, 2, length), jnp.float32),
        ],
        compiler_params=grant(56),
        cost_estimate=NO_COST,
    )


def attention_back(projected, grad_context, seg_col, seg_row, lse, first=0, count=None, into=None, after=()):
    length, width3 = projected.shape
    width = width3 // 3
    pairs = width // (2 * HEAD_DIM)
    count = count or pairs
    lane = 2 * HEAD_DIM
    col = lambda base: pl.BlockSpec((length, lane), lambda i: (0, base * pairs + first + i))
    into = () if into is None else (into,)
    return run(
        attn_bwd_kernel,
        (projected, projected, projected, grad_context, seg_col, seg_row, lse, *into,),
        after,
        grid=(count,),
        in_specs=[
            col(0),
            col(1),
            col(2),
            col(0),
            pl.BlockSpec((length, 1), lambda i: (0, 0)),
            pl.BlockSpec((1, length), lambda i: (0, 0)),
            pl.BlockSpec((1, 2, length), lambda i: (first + i, 0, 0)),
        ]
        + [HBM] * len(into),
        out_specs=pl.BlockSpec((3, length, lane), lambda i: (0, 0, first + i)),
        out_shape=jax.ShapeDtypeStruct((3, length, width), jnp.bfloat16),
        input_output_aliases={7: 0} if into else {},
        compiler_params=grant(20),
        cost_estimate=NO_COST,
    )


def start_slabs(table_ref, sources, full_ref, sem):
    copies = []
    for source in sources:
        outer, inner, rows, _ = source.shape
        for o in range(outer):
            for i in range(inner):
                start = pl.multiple_of(table_ref[len(copies)], rows)
                copies.append(
                    pltpu.make_async_copy(source.at[o, i], full_ref.at[pl.ds(start, rows)], sem)
                )
                copies[-1].start()
    return copies


def project_kernel(count, table_ref, x_ref, *refs):
    sources, (out_ref, norms_ref, kept_ref, full_ref, sem, back_sem) = refs[:count], refs[count:]
    for copy in start_slabs(table_ref, sources, full_ref, sem):
        copy.wait()
    back = pltpu.make_async_copy(full_ref, kept_ref, back_sem)
    back.start()
    norms_ref[...] = full_ref[:, -128:].astype(jnp.float32).T[:8]
    x = x_ref[...]
    step = 512
    for j in range(out_ref.shape[1] // step):
        here = slice(j * step, (j + 1) * step)
        out_ref[:, here] = dot(x, full_ref[:, here]).astype(jnp.bfloat16)
    back.wait()


def project(x, table, buffers, columns, after=()):
    total, full_columns = x.shape[1], buffers[0].shape[3]
    return run(
        functools.partial(project_kernel, len(buffers)),
        (table, x, *buffers,),
        after,
        in_specs=[SCALARS, whole(x.shape)] + [HBM] * len(buffers),
        out_specs=[whole((x.shape[0], columns)), whole((8, total)), HBM],
        out_shape=[
            jax.ShapeDtypeStruct((x.shape[0], columns), jnp.bfloat16),
            jax.ShapeDtypeStruct((8, total), jnp.float32),
            jax.ShapeDtypeStruct((total, full_columns), jnp.bfloat16),
        ],
        grid=(1,),
        scratch_shapes=[
            pltpu.VMEM((total, full_columns), jnp.bfloat16),
            pltpu.SemaphoreType.DMA,
            pltpu.SemaphoreType.DMA,
        ],
        compiler_params=grant(56),
        cost_estimate=NO_COST,
    )


def normalise(hidden):
    average = jnp.mean(hidden, axis=-1, keepdims=True)
    centred = hidden - average
    spread = jnp.mean(centred * centred, axis=-1, keepdims=True)
    scale = lax.rsqrt(spread + epsilon)
    return centred * scale, scale


def norm_back(grad, xhat, scale, gain):
    inner = grad * gain
    return scale * (
        inner
        - jnp.mean(inner, axis=-1, keepdims=True)
        - xhat * jnp.mean(inner * xhat, axis=-1, keepdims=True)
    )


def branch_kernel(context_ref, w_ref, tokens_ref, norm_ref, xhat_ref, scale_ref, low_ref):
    step = 128
    for j in range(context_ref.shape[0] // step):
        here = slice(j * step, (j + 1) * step)
        first_in = tokens_ref[here].astype(jnp.float32) + dot(context_ref[here], w_ref[...])
        xhat, scale = normalise(first_in)
        xhat_ref[here] = xhat
        scale_ref[here] = scale
        low_ref[here] = (xhat * norm_ref[0:1] + norm_ref[1:2]).astype(jnp.bfloat16)


def branch(context, w_first, tokens, norm_rows, after=()):
    rows, width = context.shape
    return run(
        branch_kernel,
        (context, w_first, tokens, norm_rows,),
        after,
        grid=(1,),
        in_specs=[
            whole((rows, width)),
            pl.BlockSpec((width, width), lambda i: (0, 3)),
            whole((rows, width)),
            whole(norm_rows.shape),
        ],
        out_specs=[whole((rows, width)), whole((rows, 1)), whole((rows, width))],
        out_shape=[
            jax.ShapeDtypeStruct((rows, width), jnp.float32),
            jax.ShapeDtypeStruct((rows, 1), jnp.float32),
            jax.ShapeDtypeStruct((rows, width), jnp.bfloat16),
        ],
        compiler_params=grant(56),
        cost_estimate=NO_COST,
    )


def up_kernel(count, table_ref, x_ref, *refs):
    sources, (act_ref, slope_ref, kept_ref, full_ref, sem, back_sem) = refs[:count], refs[count:]
    for copy in start_slabs(table_ref, sources, full_ref, sem):
        copy.wait()
    back = pltpu.make_async_copy(full_ref, kept_ref, back_sem)
    back.start()
    x = x_ref[...]
    step = 256
    for j in range(act_ref.shape[1] // step):
        here = slice(j * step, (j + 1) * step)
        pre = dot(x, full_ref[:, here])
        below = 0.5 + 0.5 * lax.erf(pre * 0.7071067811865476)
        bell = jnp.exp(pre * pre * -0.5) * 0.3989422804014327
        act_ref[:, here] = (pre * below).astype(jnp.bfloat16)
        slope_ref[:, here] = (below + pre * bell).astype(jnp.bfloat16)
    back.wait()


def up_gelu(x, table, buffers, after=()):
    total, columns = x.shape[1], buffers[0].shape[3]
    rows = x.shape[0]
    return run(
        functools.partial(up_kernel, len(buffers)),
        (table, x, *buffers,),
        after,
        in_specs=[SCALARS, whole(x.shape)] + [HBM] * len(buffers),
        out_specs=[whole((rows, columns)), whole((rows, columns)), HBM],
        out_shape=[
            jax.ShapeDtypeStruct((rows, columns), jnp.bfloat16),
            jax.ShapeDtypeStruct((rows, columns), jnp.bfloat16),
            jax.ShapeDtypeStruct((total, columns), jnp.bfloat16),
        ],
        grid=(1,),
        scratch_shapes=[
            pltpu.VMEM((total, columns), jnp.bfloat16),
            pltpu.SemaphoreType.DMA,
            pltpu.SemaphoreType.DMA,
        ],
        compiler_params=grant(56),
        cost_estimate=NO_COST,
    )


def down_kernel(count, table_ref, act_ref, xhat_ref, norm_ref, up_ref, *refs):
    sources = refs[:count]
    out_ref, second_ref, ff_ref, norms_ref, kept_ref, full_ref, sem, back_sem = refs[count:]
    step = pl.program_id(0)
    back = pltpu.make_async_copy(full_ref, kept_ref, back_sem)

    @pl.when(step == 0)
    def _():
        for copy in start_slabs(table_ref, sources, full_ref, sem):
            copy.wait()
        back.start()
        norms_ref[...] = jnp.zeros_like(norms_ref)

    first_out = xhat_ref[...] * norm_ref[0:1] + norm_ref[1:2]
    xhat, scale = normalise(first_out + dot(act_ref[...], full_ref[...]))
    out_ref[...] = (xhat * norm_ref[2:3] + norm_ref[3:4]).astype(jnp.bfloat16)
    upstream = up_ref[...].astype(jnp.float32)
    grad = norm_back(upstream, xhat, scale, norm_ref[2:3])
    second_ref[...] = grad
    ff_ref[...] = grad.astype(jnp.bfloat16)
    norms_ref[0:1] += jnp.sum(upstream * xhat, axis=0, keepdims=True)
    norms_ref[1:2] += jnp.sum(upstream, axis=0, keepdims=True)

    @pl.when(step == pl.num_programs(0) - 1)
    def _():
        back.wait()


def down_norm(act, table, buffers, xhat, norm_rows, upstream, after=()):
    rows, inner = act.shape
    width = xhat.shape[1]
    step = 128
    block = pl.BlockSpec((step, width), lambda i: (i, 0))
    return run(
        functools.partial(down_kernel, len(buffers)),
        (table, act, xhat, norm_rows, upstream, *buffers),
        after,
        grid=(rows // step,),
        in_specs=[
            SCALARS,
            pl.BlockSpec((step, inner), lambda i: (i, 0)),
            block,
            whole(norm_rows.shape),
            block,
        ]
        + [HBM] * len(buffers),
        out_specs=[block] * 3 + [whole((2, width)), HBM],
        out_shape=[
            jax.ShapeDtypeStruct((rows, width), jnp.bfloat16),
            jax.ShapeDtypeStruct((rows, width), jnp.float32),
            jax.ShapeDtypeStruct((rows, width), jnp.bfloat16),
            jax.ShapeDtypeStruct((2, width), jnp.float32),
            jax.ShapeDtypeStruct((inner, width), jnp.bfloat16),
        ],
        scratch_shapes=[
            pltpu.VMEM((inner, width), jnp.bfloat16),
            pltpu.SemaphoreType.DMA,
            pltpu.SemaphoreType.DMA,
        ],
        compiler_params=grant(56),
        cost_estimate=NO_COST,
    )


def share(core, value, kept_ref, sent_ref, columns):
    places, rows, _ = kept_ref.shape
    value = value.astype(jnp.bfloat16).reshape(places, 2, rows, value.shape[1])
    low, high = value[:, 0], value[:, 1]
    kept_ref[:, :, columns] = jnp.where(core == 0, low, high)
    sent_ref[:, :, columns] = jnp.where(core == 0, high, low)


def rows_grad_kernel(core_ref, left_ref, right_ref, *refs):
    kept_ref, sent_ref, turned_ref = refs[-3:]

    @pl.when(pl.program_id(0) == 0)
    def _():
        turned_ref[...] = left_ref[...].T

    right = right_ref[...].reshape(right_ref.shape[-2:])
    share(core_ref[0], dot(turned_ref[...], right), kept_ref, sent_ref, slice(None))


def rows_grad(core, left, right, rows, into=None, after=()):
    tokens, width = left.shape
    places = width // rows // 2
    step = 512
    each = right.shape[-1] // step
    steps = right.size // tokens // step
    if right.ndim == 3:
        block = pl.BlockSpec((1, tokens, step), lambda i: (i // each, 0, i % each))
    else:
        block = pl.BlockSpec((tokens, step), lambda i: (0, i))
    out = pl.BlockSpec((places, rows, step), lambda i: (0, 0, i))
    into = tuple(into) if into else ()
    columns = into[0].shape[2] if into else steps * step
    return run(
        rows_grad_kernel,
        (core, left, right, *into,),
        after,
        grid=(steps,),
        in_specs=[SCALARS, whole((tokens, width)), block] + [HBM] * len(into),
        out_specs=[out, out],
        out_shape=[jax.ShapeDtypeStruct((places, rows, columns), jnp.bfloat16)] * 2,
        input_output_aliases={3: 0, 4: 1} if into else {},
        scratch_shapes=[pltpu.VMEM((width, tokens), jnp.bfloat16)],
        compiler_params=grant(56),
        cost_estimate=NO_COST,
    )


def ffn_back_kernel(
    core_ref,
    act_ref,
    slope_ref,
    w_down_ref,
    w_up_ref,
    grad_ref,
    low_ref,
    second_ref,
    xhat_ref,
    scale_ref,
    norm_ref,
    down_kept_ref,
    down_sent_ref,
    up_kept_ref,
    up_sent_ref,
    in_ref,
    branch_ref,
    norms_ref,
    turned_ref,
    sum_ref,
):
    step = pl.program_id(0)
    core = core_ref[0]

    @pl.when(step == 0)
    def _():
        turned_ref[...] = low_ref[...].T
        sum_ref[...] = second_ref[...]

    grad = grad_ref[...]
    back = dot(grad, w_down_ref[...], LAST) * slope_ref[...].astype(jnp.float32)
    back = back.astype(jnp.bfloat16)
    share(core, dot(act_ref[...].T, grad), down_kept_ref, down_sent_ref, slice(None))
    share(core, dot(turned_ref[...], back), up_kept_ref, up_sent_ref, slice(None))
    sum_ref[...] += dot(back, w_up_ref[...], LAST)

    @pl.when(step == pl.num_programs(0) - 1)
    def _():
        gain_sum = shift_sum = 0.0
        chunk = 128
        for j in range(sum_ref.shape[0] // chunk):
            here = slice(j * chunk, (j + 1) * chunk)
            first, xhat = sum_ref[here], xhat_ref[here]
            back = norm_back(first, xhat, scale_ref[here], norm_ref[0:1])
            in_ref[here] = back
            branch_ref[here] = back.astype(jnp.bfloat16)
            gain_sum = gain_sum + jnp.sum(first * xhat, axis=0, keepdims=True)
            shift_sum = shift_sum + jnp.sum(first, axis=0, keepdims=True)
        norms_ref[0:1] = gain_sum
        norms_ref[1:2] = shift_sum


def ffn_back(core, act, slope, w_down, w_up, grad, low, second, xhat, scale, norm_rows, rows, ff_rows):
    tokens, inner = act.shape
    width = grad.shape[1]
    step = 512
    places = width // rows // 2
    ff_places = inner // ff_rows // 2
    here = step // ff_rows // 2
    columns = pl.BlockSpec((tokens, step), lambda i: (0, i))
    down_out = pl.BlockSpec((here, ff_rows, width), lambda i: (i, 0, 0))
    up_out = pl.BlockSpec((places, rows, step), lambda i: (0, 0, i))
    down_shape = jax.ShapeDtypeStruct((ff_places, ff_rows, width), jnp.bfloat16)
    up_shape = jax.ShapeDtypeStruct((places, rows, inner + width + 128), jnp.bfloat16)
    return run(
        ffn_back_kernel,
        (core, act, slope, w_down, w_up, grad, low, second, xhat, scale, norm_rows),
        grid=(inner // step,),
        in_specs=[
            SCALARS,
            columns,
            columns,
            pl.BlockSpec((step, width), lambda i: (i, 0)),
            pl.BlockSpec((width, step), lambda i: (0, i)),
            whole((tokens, width)),
            whole((tokens, width)),
            whole((tokens, width)),
            whole((tokens, width)),
            whole((tokens, 1)),
            whole(norm_rows.shape),
        ],
        out_specs=[down_out, down_out, up_out, up_out]
        + [whole((tokens, width))] * 2
        + [whole((2, width))],
        out_shape=[
            down_shape,
            down_shape,
            up_shape,
            up_shape,
            jax.ShapeDtypeStruct((tokens, width), jnp.float32),
            jax.ShapeDtypeStruct((tokens, width), jnp.bfloat16),
            jax.ShapeDtypeStruct((2, width), jnp.float32),
        ],
        scratch_shapes=[
            pltpu.VMEM((width, tokens), jnp.bfloat16),
            pltpu.VMEM((tokens, width), jnp.float32),
        ],
        compiler_params=grant(56),
        cost_estimate=NO_COST,
    )


def out_grad_kernel(
    core_ref,
    context_ref,
    grad_ref,
    w_ref,
    one_ref,
    two_ref,
    kept_in,
    sent_in,
    back_ref,
    kept_hbm,
    sent_hbm,
    kept_ref,
    sent_ref,
    sems,
):
    core = core_ref[0]
    width = w_ref.shape[0]
    grad = grad_ref[...]
    turned = context_ref[...].T
    step = 256
    for j in range(width // step):
        here = slice(j * step, (j + 1) * step)
        share(core, dot(turned, grad[:, here]), kept_ref, sent_ref, here)
    norms = jnp.concatenate([one_ref[...], two_ref[...], jnp.zeros((124, width), jnp.float32)], 0)
    share(core, norms.T, kept_ref, sent_ref, slice(width, width + 128))
    last = pl.ds(kept_hbm.shape[2] - width - 128, width + 128)
    copies = [
        pltpu.make_async_copy(kept_ref, kept_hbm.at[:, :, last], sems.at[0]),
        pltpu.make_async_copy(sent_ref, sent_hbm.at[:, :, last], sems.at[1]),
    ]
    for copy in copies:
        copy.start()
    for j in range(width // step):
        here = slice(j * step, (j + 1) * step)
        back_ref[:, here] = dot(grad, w_ref[here], LAST).astype(jnp.bfloat16)
    for copy in copies:
        copy.wait()


def out_grad(core, context, grad, w_first, norms_one, norms_two, kept, sent, after=()):
    tokens, width = context.shape
    part = pltpu.VMEM(kept.shape[:2] + (width + 128,), jnp.bfloat16)
    out = kept.shape
    return run(
        out_grad_kernel,
        (core, context, grad, w_first, norms_one, norms_two, kept, sent),
        after,
        grid=(1,),
        in_specs=[
            SCALARS,
            whole((tokens, width)),
            whole((tokens, width)),
            pl.BlockSpec((width, width), lambda i: (0, 3)),
            whole((2, width)),
            whole((2, width)),
            HBM,
            HBM,
        ],
        out_specs=[whole((tokens, width)), HBM, HBM],
        out_shape=[
            jax.ShapeDtypeStruct((tokens, width), jnp.bfloat16),
            jax.ShapeDtypeStruct(out, jnp.bfloat16),
            jax.ShapeDtypeStruct(out, jnp.bfloat16),
        ],
        input_output_aliases={6: 1, 7: 2},
        scratch_shapes=[part, part, pltpu.SemaphoreType.DMA((2,))],
        compiler_params=grant(56),
        cost_estimate=NO_COST,
    )


def tokens_grad_kernel(grad_ref, w_ref, first_ref, out_ref, sum_ref):
    step = pl.program_id(0)

    @pl.when(step == 0)
    def _():
        sum_ref[...] = first_ref[...]

    sum_ref[...] += dot(grad_ref[0], w_ref[...], LAST)

    @pl.when(step == pl.num_programs(0) - 1)
    def _():
        out_ref[...] = sum_ref[...].astype(jnp.bfloat16)


def tokens_grad(grad_mixed, w_first, first, after=()):
    count, tokens, width = grad_mixed.shape
    return run(
        tokens_grad_kernel,
        (grad_mixed, w_first, first,),
        after,
        grid=(count,),
        in_specs=[
            pl.BlockSpec((1, tokens, width), lambda i: (i, 0, 0)),
            pl.BlockSpec((width, width), lambda i: (0, i)),
            whole((tokens, width)),
        ],
        out_specs=whole((tokens, width)),
        out_shape=jax.ShapeDtypeStruct((tokens, width), jnp.bfloat16),
        scratch_shapes=[pltpu.VMEM((tokens, width), jnp.float32)],
        compiler_params=grant(56),
        cost_estimate=NO_COST,
    )


def fold_kernel(place_ref, kept_ref, came_ref, a_own_ref, a_out_ref, b_own_ref, b_out_ref):
    x, y = place_ref[0], place_ref[1]
    half = a_own_ref.shape[2]
    part = lambda ref, i, j, rows: ref[0, i, j, rows].astype(jnp.float32)
    low, high = pl.ds(0, half), pl.ds(half, half)
    for i in range(2):
        both = lambda a, b, rows: (part(kept_ref, a, b, rows) + part(came_ref, a, b, rows)).astype(
            jnp.bfloat16
        )
        a_own_ref[0, i] = both(i, y, low)
        a_out_ref[0, i] = both(i, 1 - y, low)
        b_own_ref[0, i] = both(x, i, high)
        b_out_ref[0, i] = both(1 - x, i, high)


def fold_plane_kernel(place_ref, *refs):
    for i in range(2):
        own_ref, came_ref = refs[2 * i], refs[2 * i + 1]
        keep_ref, out_ref = refs[4 + 2 * i], refs[5 + 2 * i]
        place = place_ref[i]
        for ref, index in ((keep_ref, place), (out_ref, 1 - place)):
            total = own_ref[0, index].astype(jnp.float32) + came_ref[0, index].astype(jnp.float32)
            ref[0] = total.astype(jnp.bfloat16)


def fold_plane(place, a_own, a_came, b_own, b_came, after=()):
    zs, both, rows, columns = a_own.shape
    block = pl.BlockSpec((1, both, rows, columns), lambda i: (i, 0, 0, 0))
    out = pl.BlockSpec((1, rows, columns), lambda i: (i, 0, 0))
    return run(
        fold_plane_kernel,
        (place, a_own, a_came, b_own, b_came),
        after,
        grid=(zs,),
        in_specs=[SCALARS] + [block] * 4,
        out_specs=[out] * 4,
        out_shape=[jax.ShapeDtypeStruct((zs, rows, columns), jnp.bfloat16)] * 4,
        compiler_params=grant(20),
        cost_estimate=NO_COST,
    )


def fold(place, kept, came, after=()):
    zs, xs, ys, rows, columns = kept.shape
    out = pl.BlockSpec((1, 2, rows // 2, columns), lambda i: (i, 0, 0, 0))
    block = pl.BlockSpec((1, xs, ys, rows, columns), lambda i: (i, 0, 0, 0, 0))
    return run(
        fold_kernel,
        (place, kept, came,),
        after,
        grid=(zs,),
        in_specs=[SCALARS, block, block],
        out_specs=[out] * 4,
        out_shape=[jax.ShapeDtypeStruct((zs, 2, rows // 2, columns), jnp.bfloat16)] * 4,
        compiler_params=grant(20),
        cost_estimate=NO_COST,
    )


def gate(values, after=(), room=None):
    return run(
        lambda *refs: None,
        values,
        after,
        in_specs=[pl.BlockSpec(memory_space=pl.ANY)] * len(values),
        out_specs=[pl.BlockSpec(memory_space=pl.ANY)] * len(values),
        out_shape=[jax.ShapeDtypeStruct(v.shape, v.dtype) for v in values],
        input_output_aliases={i: i for i in range(len(values))},
        compiler_params=grant(room) if room else None,
    )


def routes(move):
    pairs = []
    for place in range(32):
        z, x, y, c = place // 8, place // 4 % 2, place // 2 % 2, place % 2
        target = move(z, x, y, c)
        if target is not None:
            tz, tx, ty, tc = target
            pairs.append((place, tz * 8 + tx * 4 + ty * 2 + tc))
    return pairs


ROUTE_X = routes(lambda z, x, y, c: (z, 1 - x, y, c))
ROUTE_Y = routes(lambda z, x, y, c: (z, x, 1 - y, c))
ROUTE_C = routes(lambda z, x, y, c: (z, x, y, 1 - c))


def send(value, route):
    return lax.ppermute(value, ALL, route)


def coordinates():
    dp = lax.axis_index("dp")
    return dp // 2, dp % 2, lax.axis_index("blk"), lax.axis_index("head")


def copy_kernel(in_ref, out_ref):
    out_ref[...] = in_ref[...]


def copy_after(value, after):
    return run(
        copy_kernel,
        (value,),
        after,
        in_specs=[whole(value.shape)],
        out_specs=whole(value.shape),
        out_shape=jax.ShapeDtypeStruct(value.shape, value.dtype),
        cost_estimate=NO_COST,
    )


def side_kernel(left_ref, right_ref, out_ref):
    middle = left_ref.shape[1]
    out_ref[:, :middle] = left_ref[...]
    out_ref[:, middle:] = right_ref[...]


def side_by_side(left, right, after):
    blocks, first, columns = left.shape
    both = first + right.shape[1]
    return run(
        side_kernel,
        (left, right),
        after,
        grid=(blocks,),
        in_specs=[
            pl.BlockSpec((1,) + left.shape[1:], lambda i: (i, 0, 0)),
            pl.BlockSpec((1,) + right.shape[1:], lambda i: (i, 0, 0)),
        ],
        out_specs=pl.BlockSpec((1, both, columns), lambda i: (i, 0, 0)),
        out_shape=jax.ShapeDtypeStruct((blocks, both, columns), left.dtype),
        cost_estimate=NO_COST,
    )


def sum_of(values):
    total = None
    for value in values:
        value = value.astype(jnp.float32)
        total = value if total is None else total + value
    return total


def slot_rows(buffers, rows):
    z, x, y, c = coordinates()
    tables = []
    for value, part, axis, dx, dy, dc in buffers:
        js = jnp.arange(value.shape[0])[:, None]
        zs = jnp.arange(4)[None, :]
        sx = (x ^ dx ^ js) if axis == 0 else x ^ dx
        sy = (y ^ dy ^ js) if axis == 1 else y ^ dy
        device = ((zs * 2 + sx) * 2 + sy) * 2 + (c ^ dc)
        tables.append((device * rows + part * (rows // 2)).reshape(-1))
    return jnp.concatenate(tables).astype(jnp.int32)


def pick(value, index, axis):
    return lax.dynamic_index_in_dim(value, index, axis, keepdims=False)


def fold_cores(kept, came, after):
    z, x, y, c = coordinates()
    shape = (4, 2, 2) + kept.shape[1:]
    return fold(jnp.stack([x, y]), kept.reshape(shape), came.reshape(shape), after)


def natural(kept, sent):
    return jnp.stack([kept, sent], axis=1).reshape(-1, kept.shape[2])


def joined_shards(qkv_weight, out_weight, norm_params):
    norm_wide = jnp.pad(norm_params, ((0, 0), (0, 128 - norm_params.shape[1])))
    return jnp.concatenate([qkv_weight, out_weight, norm_wide], axis=1)


def split_up(grad, width):
    inner = grad.shape[1] - width - 128
    last = inner + width
    return tuple(
        part.astype(jnp.float32)
        for part in (grad[:, :inner], grad[:, inner:last], grad[:, last : last + 4])
    )


def buffers_of(a2, ay, b2, bx):
    return [(a2, 0, 0, 0, 0), (ay, 0, 0, 0, 1), (b2, 1, 1, 0, 0), (bx, 1, 1, 1, 0)]


def with_partner(shard, own, partner):
    buffers = [b + (0,) for b in own]
    buffers += [(v,) + b[1:] + (1,) for v, b in zip(partner, own)]
    return slot_rows(buffers, shard.shape[0]), [b[0] for b in buffers]


def body_lines(
    tokens, doc_lengths, qkv_weight, out_weight, up_weight, down_weight, norm_params, out_cotangent
):
    seqs_here, local_len, width = tokens.shape
    full_len = local_len * 4
    z, x, y, c = coordinates()
    place = y * 2 + c
    core = c.reshape(1)
    slab, ff_slab = up_weight.shape[0], down_weight.shape[0]
    exchange = lambda v: lax.all_to_all(v, GROUP, split_axis=0, concat_axis=0, tiled=True)
    to_sequence = lambda v: exchange(v).reshape(full_len, width)
    to_positions = lambda v: exchange(v.reshape(seqs_here, local_len, width))
    own_lengths = lax.dynamic_slice_in_dim(doc_lengths, place, 1, 0)
    seg_row = segments_of(own_lengths, full_len)
    seg_col = seg_row.reshape(full_len, 1)
    first_own, up_own = joined_shards(qkv_weight, out_weight, norm_params), up_weight
    half, ff_half = slab // 2, ff_slab // 2
    line = lambda v: lax.all_gather(v, "dp", axis_index_groups=LINES)

    first_line = line(first_own)
    down_a, down_b = down_weight[:ff_half], down_weight[ff_half:]
    down_ax, down_by = send(down_a, ROUTE_X), send(down_b, ROUTE_Y)
    both = exchange(side_by_side(tokens, out_cotangent, (first_own, down_ax, down_by)))
    rows, upstream = (
        v.reshape(full_len, width) for v in (both[:, :local_len], both[:, local_len:])
    )
    down_own = jnp.stack([down_a, down_ax, down_b, down_by])

    a, b = gate(
        (first_line[:, :half], first_line[:, half:]),
        (down_own, seg_row, seg_col),
    )
    up_shard = copy_after(up_own, (a,))
    ax, by = send(a, ROUTE_X), send(b, ROUTE_Y)
    up_line = line(up_shard)

    a2, b2 = gate((jnp.stack([a, ax]), jnp.stack([b, by])), (rows, upstream))
    ay, bx = send(a2, ROUTE_Y), send(b2, ROUTE_X)
    a2c, b2c = send(a2, ROUTE_C), send(b2, ROUTE_C)

    ay, bx, up_a, up_b, down_own, a2c, b2c = gate(
        (ay, bx, up_line[:, :half], up_line[:, half:], down_own, a2c, b2c)
    )
    ayc, bxc = send(ay, ROUTE_C), send(bx, ROUTE_C)
    up_ax, up_by = send(up_a, ROUTE_X), send(up_b, ROUTE_Y)
    down_line = line(down_own)
    table, buffers = with_partner(
        first_own, buffers_of(a2, ay, b2, bx), (a2c, ayc, b2c, bxc)
    )
    projected, norm_rows, w_first = project(rows, table, buffers, 3 * width)

    up_ax, up_by, projected = gate((up_ax, up_by, projected))
    up_a2, up_b2 = jnp.stack([up_a, up_ax]), jnp.stack([up_b, up_by])
    up_ay, up_bx = send(up_a2, ROUTE_Y), send(up_b2, ROUTE_X)
    up_a2c, up_b2c = send(up_a2, ROUTE_C), send(up_b2, ROUTE_C)
    context, log_sums = attention(projected, seg_col, seg_row)

    up_ay, up_bx, up_a2c, up_b2c, down_line, context = gate(
        (up_ay, up_bx, up_a2c, up_b2c, down_line, context)
    )
    down_a2, down_b2 = jnp.swapaxes(down_line[:, :2], 0, 1), jnp.swapaxes(down_line[:, 2:], 0, 1)
    down_ay, down_bx = send(down_a2, ROUTE_Y), send(down_b2, ROUTE_X)
    down_a2c, down_b2c = send(down_a2, ROUTE_C), send(down_b2, ROUTE_C)
    up_ayc, up_bxc = send(up_ay, ROUTE_C), send(up_bx, ROUTE_C)
    xhat, scale, first_low = branch(context, w_first, rows, norm_rows)
    table, buffers = with_partner(
        up_own, buffers_of(up_a2, up_ay, up_b2, up_bx), (up_a2c, up_ayc, up_b2c, up_bxc)
    )
    act, slope, w_up = up_gelu(first_low, table, buffers)

    down_ay, down_bx, down_a2c, down_b2c, act = gate((down_ay, down_bx, down_a2c, down_b2c, act))
    down_ayc, down_bxc = send(down_ay, ROUTE_C), send(down_bx, ROUTE_C)
    table, buffers = with_partner(
        down_weight,
        buffers_of(down_a2, down_ay, down_b2, down_bx),
        (down_a2c, down_ayc, down_b2c, down_bxc),
    )
    result, grad_second, grad_ff, norms_two, w_down = down_norm(
        act, table, buffers, xhat, norm_rows, upstream
    )

    low = lambda *v: sum_of(v).astype(jnp.bfloat16)
    place_xy = jnp.stack([x, y])
    layer_out = to_positions(result)
    down_kept, down_sent, up_kept, up_sent, grad_first_in, grad_branch, norms_one = ffn_back(
        core,
        act,
        slope,
        w_down,
        w_up,
        grad_ff,
        first_low,
        grad_second,
        xhat,
        scale,
        norm_rows,
        slab,
        ff_slab,
    )

    down_sent, grad_branch = gate((down_sent, grad_branch), (layer_out,))
    down_came = send(down_sent, ROUTE_C)
    grad_context, up_kept, up_sent = out_grad(
        core, context, grad_branch, w_first, norms_one, norms_two, up_kept, up_sent
    )

    da_own, da_out, db_own, db_out = fold_cores(down_kept, down_came, (grad_context,))
    da_out, db_out, up_sent, grad_context = gate((da_out, db_out, up_sent, grad_context), (), 1)
    da_in, db_in = send(da_out, ROUTE_Y), send(db_out, ROUTE_X)
    up_came = send(up_sent, ROUTE_C)
    grad_mixed = attention_back(projected, grad_context, seg_col, seg_row, log_sums)

    ua_own, ua_out, ub_own, ub_out = fold_cores(up_kept, up_came, (grad_mixed, da_in, db_in))
    down_blocks = jnp.concatenate([low(da_own, da_in), low(db_own, db_in)], axis=1)
    ua_out, ub_out, down_blocks, grad_mixed = gate((ua_out, ub_out, down_blocks, grad_mixed), (), 1)
    ua_in, ub_in = send(ua_out, ROUTE_Y), send(ub_out, ROUTE_X)
    down_sum = lax.psum_scatter(
        down_blocks, "dp", scatter_dimension=0, axis_index_groups=LINES, tiled=False
    )
    last_kept, last_sent = rows_grad(core, rows, grad_mixed, slab)
    grad_tokens = tokens_grad(grad_mixed, w_first, grad_first_in, (last_sent,))

    ua_own, ua_out, ub_own, ub_out = fold_plane(
        place_xy, ua_own, ua_in, ub_own, ub_in, (grad_tokens,)
    )
    ua_out, ub_out, last_sent = gate((ua_out, ub_out, last_sent), (), 1)
    ua_in2, ub_in2 = send(ua_out, ROUTE_X), send(ub_out, ROUTE_Y)
    last_came = send(last_sent, ROUTE_C)

    la_own, la_out, lb_own, lb_out = fold_cores(last_kept, last_came, (ua_in2, ub_in2))
    up_blocks = jnp.concatenate([low(ua_own, ua_in2), low(ub_own, ub_in2)], axis=1)
    up_blocks, la_out, lb_out, down_sum = gate((up_blocks, la_out, lb_out, down_sum), (), 1)
    up_sum = lax.psum_scatter(
        up_blocks, "dp", scatter_dimension=0, axis_index_groups=LINES, tiled=False
    )
    la_in, lb_in = send(la_out, ROUTE_Y), send(lb_out, ROUTE_X)
    da_in = send(pick(down_sum[:2], 1 - x, 0), ROUTE_X)
    db_in = send(pick(down_sum[2:], 1 - y, 0), ROUTE_Y)

    la_own, la_out, lb_own, lb_out = fold_plane(
        place_xy, la_own, la_in, lb_own, lb_in, (da_in, db_in)
    )
    la_out, lb_out, grad_tokens = gate((la_out, lb_out, grad_tokens), (), 1)
    la_in2, lb_in2 = send(la_out, ROUTE_X), send(lb_out, ROUTE_Y)
    grad_down = jnp.concatenate(
        [sum_of([pick(down_sum[:2], x, 0), da_in]), sum_of([pick(down_sum[2:], y, 0), db_in])],
        axis=0,
    )

    last_blocks = jnp.concatenate([low(la_own, la_in2), low(lb_own, lb_in2)], axis=1)
    last_blocks, grad_tokens, up_sum = gate((last_blocks, grad_tokens, up_sum), (), 1)
    input_grad = to_positions(grad_tokens)
    last_sum = lax.psum_scatter(
        last_blocks, "dp", scatter_dimension=0, axis_index_groups=LINES, tiled=False
    )
    grad_qkv = last_sum.astype(jnp.float32)
    grad_up, grad_out, grad_norm = split_up(up_sum, width)
    return (
        layer_out,
        input_grad.astype(jnp.float32),
        grad_qkv,
        grad_out,
        grad_up,
        grad_down,
        grad_norm,
    )


def body_any(
    tokens, doc_lengths, qkv_weight, out_weight, up_weight, down_weight, norm_params, out_cotangent
):
    seqs_here, local_len, width = tokens.shape
    ff = up_weight.shape[1]
    full_len = local_len * lax.axis_size("blk") * lax.axis_size("head")
    place = lax.axis_index("blk") * lax.axis_size("head") + lax.axis_index("head")
    core = jnp.zeros((1,), jnp.int32)
    slab, ff_slab = width // 32, ff // 32
    exchange = lambda v: lax.all_to_all(v, GROUP, split_axis=0, concat_axis=0, tiled=True)
    to_sequence = lambda v: exchange(v).reshape(full_len, width)
    to_positions = lambda v: exchange(v.reshape(seqs_here, local_len, width))

    def gather(shard):
        return core, [lax.all_gather(shard, ALL, axis=0, tiled=True)[None, None]]

    def scatter(kept, sent):
        total = lax.psum_scatter(natural(kept, sent), ALL, scatter_dimension=0, tiled=True)
        return total.astype(jnp.float32)

    rows = to_sequence(tokens)
    upstream = to_sequence(out_cotangent)
    own_lengths = lax.dynamic_slice_in_dim(doc_lengths, place, 1, 0)
    seg_row = segments_of(own_lengths, full_len)
    seg_col = seg_row.reshape(full_len, 1)
    first_slots = gather(joined_shards(qkv_weight, out_weight, norm_params))
    projected, norm_rows, w_first = project(rows, *first_slots, 3 * width)
    context, log_sums = attention(projected, seg_col, seg_row)
    xhat, scale, first_low = branch(context, w_first, rows, norm_rows)
    act, slope, w_up = up_gelu(first_low, *gather(up_weight))
    result, grad_second, grad_ff, norms_two, w_down = down_norm(
        act, *gather(down_weight), xhat, norm_rows, upstream
    )
    down_kept, down_sent, up_kept, up_sent, grad_first_in, grad_branch, norms_one = ffn_back(
        core,
        act,
        slope,
        w_down,
        w_up,
        grad_ff,
        first_low,
        grad_second,
        xhat,
        scale,
        norm_rows,
        slab,
        ff_slab,
    )
    grad_down = scatter(down_kept, down_sent)
    grad_context, up_kept, up_sent = out_grad(
        core, context, grad_branch, w_first, norms_one, norms_two, up_kept, up_sent
    )
    grad_up, grad_out, grad_norm = split_up(scatter(up_kept, up_sent), width)
    grad_mixed = attention_back(projected, grad_context, seg_col, seg_row, log_sums)
    grad_qkv = scatter(*rows_grad(core, rows, grad_mixed, slab))
    grad_tokens = tokens_grad(grad_mixed, w_first, grad_first_in)
    return (
        to_positions(result),
        to_positions(grad_tokens).astype(jnp.float32),
        grad_qkv,
        grad_out,
        grad_up,
        grad_down,
        grad_norm,
    )


def solution(mesh):
    sizes = tuple(mesh.shape[name] for name in ALL)
    body = body_lines if sizes == (8, 2, 2) else body_any
    placed = (
        P("dp", ("blk", "head"), None),
        P("dp", None),
        P(("dp", "blk", "head"), None),
        P(("dp", "blk", "head"), None),
        P(("dp", "blk", "head"), None),
        P(("dp", "blk", "head"), None),
        P(("dp", "blk", "head"), None),
        P("dp", ("blk", "head"), None),
    )
    return jax.shard_map(
        body,
        mesh=mesh,
        in_specs=placed,
        out_specs=(
            P("dp", ("blk", "head"), None),
            P("dp", ("blk", "head"), None),
            P(("dp", "blk", "head"), None),
            P(("dp", "blk", "head"), None),
            P(("dp", "blk", "head"), None),
            P(("dp", "blk", "head"), None),
            P(("dp", "blk", "head"), None),
        ),
        check_vma=False,
    )
```

```python
import functools

import jax
import jax.numpy as jnp
from jax import lax
from jax.experimental import pallas as pl
from jax.experimental.pallas import tpu as pltpu
from jax.sharding import PartitionSpec as P

HEAD_DIM = 64
ALL = ("dp", "blk", "head")
GROUP = ("blk", "head")
LINES = [[0, 2, 4, 6], [1, 3, 5, 7]]
epsilon = 1e-12


def segments_of(doc_lengths, length):
    doc_ends = jnp.cumsum(doc_lengths, axis=-1, dtype=jnp.int32)
    places = jnp.arange(length, dtype=jnp.int32)
    passed = jnp.sum(
        (doc_ends[..., None, :] <= places[:, None]).astype(jnp.int32), axis=-1, dtype=jnp.int32
    )
    return jnp.where(places < doc_ends[..., -1:], passed + 1, 0)


def run(kernel, operands, after=(), in_specs=(), scalars=0, grid=(1,), out_specs=None, scratch_shapes=(), **rest):
    count = len(operands)

    def body(*refs):
        kernel(*refs[:count], *refs[count + len(after) :])

    specs = list(in_specs) + [pl.BlockSpec(memory_space=pl.ANY)] * len(after)
    spec = pltpu.PrefetchScalarGridSpec(
        num_scalar_prefetch=scalars,
        grid=grid,
        in_specs=specs,
        out_specs=out_specs,
        scratch_shapes=scratch_shapes,
    )
    return pl.pallas_call(body, grid_spec=spec, **rest)(*operands, *after)


MIB = 2**20
NO_COST = pl.CostEstimate(flops=1, bytes_accessed=1, transcendentals=0)
LAST = (((1,), (1,)), ((), ()))
FIRST = (((0,), (0,)), ((), ()))


def grant(mib):
    return pltpu.CompilerParams(vmem_limit_bytes=mib * MIB)


def dot(left, right, form=(((1,), (0,)), ((), ()))):
    return lax.dot_general(left, right, form, preferred_element_type=jnp.float32)


def whole(shape):
    return pl.BlockSpec(shape, lambda *_: (0,) * len(shape))


HBM = pl.BlockSpec(memory_space=pltpu.HBM)
SCALARS = pl.BlockSpec(memory_space=pltpu.SMEM)


def attn_fwd_kernel(q_ref, k_ref, v_ref, segc_ref, segr_ref, out_ref, lse_ref):
    length = q_ref.shape[0]
    scaled = q_ref[...] * jnp.bfloat16(HEAD_DIM ** (-0.5))
    key_pair = k_ref[...]
    value_t = v_ref[...].T
    lanes = lax.broadcasted_iota(jnp.int32, key_pair.shape, 1)
    allowed = segc_ref[...] == segr_ref[...]
    parts = []
    for h in range(2):
        own = (lanes >= h * HEAD_DIM) & (lanes < (h + 1) * HEAD_DIM)
        keys = jnp.where(own, key_pair, jnp.zeros_like(key_pair))
        scores = lax.dot_general(
            keys, scaled, (((1,), (1,)), ((), ())), preferred_element_type=jnp.float32
        )
        scores = jnp.where(allowed, scores, -1e30)
        largest = jnp.max(scores, axis=0, keepdims=True)
        powers = jnp.exp(scores - largest)
        totals = jnp.sum(powers, axis=0, keepdims=True)
        probs = (powers * (1.0 / totals)).astype(jnp.bfloat16)
        parts.append(
            jnp.dot(
                value_t[h * HEAD_DIM : (h + 1) * HEAD_DIM], probs, preferred_element_type=jnp.float32
            )
        )
        lse_ref[0, h : h + 1, :] = largest + jnp.log(totals)
    live = (segc_ref[...] != 0).astype(jnp.float32)
    context = jnp.concatenate(parts, axis=0).T * live
    out_ref[...] = context.astype(jnp.bfloat16)


def attn_bwd_kernel(
    q_ref, k_ref, v_ref, g_ref, segc_ref, segr_ref, lse_ref, *refs
):
    out_ref = refs[-1]
    scaled = q_ref[...] * jnp.bfloat16(HEAD_DIM ** (-0.5))
    key_pair = k_ref[...]
    value_pair = v_ref[...]
    key_t = key_pair.T
    grads = jnp.where(segc_ref[...] != 0, g_ref[...], jnp.zeros_like(g_ref[...]))
    lanes = lax.broadcasted_iota(jnp.int32, key_pair.shape, 1)
    allowed = segc_ref[...] == segr_ref[...]
    contract = (((1,), (1,)), ((), ()))
    dq_parts = []
    dk = None
    dv = None
    for h in range(2):
        own = (lanes >= h * HEAD_DIM) & (lanes < (h + 1) * HEAD_DIM)
        zero = jnp.zeros_like(key_pair)
        keys = jnp.where(own, key_pair, zero)
        values = jnp.where(own, value_pair, zero)
        queries = jnp.where(own, scaled, zero)
        grad_own = jnp.where(own, grads, zero)
        scores = lax.dot_general(keys, scaled, contract, preferred_element_type=jnp.float32)
        scores = jnp.where(allowed, scores, -1e30)
        probs = jnp.exp(scores - lse_ref[0, h : h + 1, :])
        grad_probs = lax.dot_general(values, grads, contract, preferred_element_type=jnp.float32)
        inner = jnp.sum(probs * grad_probs, axis=0, keepdims=True)
        grad_scores = (probs * (grad_probs - inner)).astype(jnp.bfloat16)
        dv_h = jnp.dot(probs.astype(jnp.bfloat16), grad_own, preferred_element_type=jnp.float32)
        dk_h = jnp.dot(grad_scores, queries, preferred_element_type=jnp.float32)
        dv = dv_h if dv is None else dv + dv_h
        dk = dk_h if dk is None else dk + dk_h
        dq_parts.append(
            jnp.dot(
                key_t[h * HEAD_DIM : (h + 1) * HEAD_DIM],
                grad_scores,
                preferred_element_type=jnp.float32,
            )
        )
    dq = jnp.concatenate(dq_parts, axis=0).T * (HEAD_DIM ** (-0.5))
    out_ref[0] = dq.astype(jnp.bfloat16)
    out_ref[1] = dk.astype(jnp.bfloat16)
    out_ref[2] = dv.astype(jnp.bfloat16)


def attention(projected, seg_col, seg_row, after=()):
    length, width3 = projected.shape
    width = width3 // 3
    pairs = width // (2 * HEAD_DIM)
    lane = 2 * HEAD_DIM
    col = lambda base: pl.BlockSpec((length, lane), lambda i: (0, base * pairs + i))
    return run(
        attn_fwd_kernel,
        (projected, projected, projected, seg_col, seg_row,),
        after,
        grid=(pairs,),
        in_specs=[
            col(0),
            col(1),
            col(2),
            pl.BlockSpec((length, 1), lambda i: (0, 0)),
            pl.BlockSpec((1, length), lambda i: (0, 0)),
        ],
        out_specs=[
            pl.BlockSpec((length, lane), lambda i: (0, i)),
            pl.BlockSpec((1, 2, length), lambda i: (i, 0, 0)),
        ],
        out_shape=[
            jax.ShapeDtypeStruct((length, width3 // 3), jnp.bfloat16),
            jax.ShapeDtypeStruct((pairs, 2, length), jnp.float32),
        ],
        compiler_params=grant(56),
        cost_estimate=NO_COST,
    )


def attention_back(projected, grad_context, seg_col, seg_row, lse, first=0, count=None, into=None, after=()):
    length, width3 = projected.shape
    width = width3 // 3
    pairs = width // (2 * HEAD_DIM)
    count = count or pairs
    lane = 2 * HEAD_DIM
    col = lambda base: pl.BlockSpec((length, lane), lambda i: (0, base * pairs + first + i))
    into = () if into is None else (into,)
    return run(
        attn_bwd_kernel,
        (projected, projected, projected, grad_context, seg_col, seg_row, lse, *into,),
        after,
        grid=(count,),
        in_specs=[
            col(0),
            col(1),
            col(2),
            col(0),
            pl.BlockSpec((length, 1), lambda i: (0, 0)),
            pl.BlockSpec((1, length), lambda i: (0, 0)),
            pl.BlockSpec((1, 2, length), lambda i: (first + i, 0, 0)),
        ]
        + [HBM] * len(into),
        out_specs=pl.BlockSpec((3, length, lane), lambda i: (0, 0, first + i)),
        out_shape=jax.ShapeDtypeStruct((3, length, width), jnp.bfloat16),
        input_output_aliases={7: 0} if into else {},
        compiler_params=grant(20),
        cost_estimate=NO_COST,
    )


def start_slabs(table_ref, sources, full_ref, sem):
    copies = []
    for source in sources:
        outer, inner, rows, _ = source.shape
        for o in range(outer):
            for i in range(inner):
                start = pl.multiple_of(table_ref[len(copies)], rows)
                copies.append(
                    pltpu.make_async_copy(source.at[o, i], full_ref.at[pl.ds(start, rows)], sem)
                )
                copies[-1].start()
    return copies


def project_kernel(count, table_ref, x_ref, *refs):
    sources, (out_ref, kept_ref, full_ref, sem, back_sem) = refs[:count], refs[count:]
    for copy in start_slabs(table_ref, sources, full_ref, sem):
        copy.wait()
    back = pltpu.make_async_copy(full_ref, kept_ref, back_sem)
    back.start()
    x = x_ref[...]
    step = 512
    for j in range(out_ref.shape[1] // step):
        here = slice(j * step, (j + 1) * step)
        out_ref[:, here] = dot(x, full_ref[:, here]).astype(jnp.bfloat16)
    back.wait()


def project(x, table, buffers, columns, after=()):
    total, full_columns = x.shape[1], buffers[0].shape[3]
    return run(
        functools.partial(project_kernel, len(buffers)),
        (table, x, *buffers,),
        after,
        in_specs=[SCALARS, whole(x.shape)] + [HBM] * len(buffers),
        out_specs=[whole((x.shape[0], columns)), HBM],
        out_shape=[
            jax.ShapeDtypeStruct((x.shape[0], columns), jnp.bfloat16),
            jax.ShapeDtypeStruct((total, full_columns), jnp.bfloat16),
        ],
        grid=(1,),
        scratch_shapes=[
            pltpu.VMEM((total, full_columns), jnp.bfloat16),
            pltpu.SemaphoreType.DMA,
            pltpu.SemaphoreType.DMA,
        ],
        compiler_params=grant(56),
        cost_estimate=NO_COST,
    )


def normalise(hidden):
    average = jnp.mean(hidden, axis=-1, keepdims=True)
    centred = hidden - average
    spread = jnp.mean(centred * centred, axis=-1, keepdims=True)
    scale = lax.rsqrt(spread + epsilon)
    return centred * scale, scale


def norm_back(grad, xhat, scale, gain):
    inner = grad * gain
    return scale * (
        inner
        - jnp.mean(inner, axis=-1, keepdims=True)
        - xhat * jnp.mean(inner * xhat, axis=-1, keepdims=True)
    )


def middle_kernel(count, table_ref, context_ref, tokens_ref, *refs):
    sources = refs[:count]
    (xhat_ref, scale_ref, low_ref, norms_ref, act_ref, slope_ref, kept_ref) = refs[count : count + 7]
    full_ref, sem, back_sem = refs[count + 7 :]
    for copy in start_slabs(table_ref, sources, full_ref, sem):
        copy.wait()
    back = pltpu.make_async_copy(full_ref, kept_ref, back_sem)
    back.start()
    inner, width = act_ref.shape[1], context_ref.shape[1]
    norms = full_ref[:, -128:].astype(jnp.float32).T[:8]
    norms_ref[...] = norms
    step = 128
    for j in range(context_ref.shape[0] // step):
        here = slice(j * step, (j + 1) * step)
        first_in = tokens_ref[here].astype(jnp.float32) + dot(
            context_ref[here], full_ref[:, inner : inner + width]
        )
        xhat, scale = normalise(first_in)
        xhat_ref[here] = xhat
        scale_ref[here] = scale
        low_ref[here] = (xhat * norms[0:1] + norms[1:2]).astype(jnp.bfloat16)
    x = low_ref[...]
    step = 256
    for j in range(inner // step):
        here = slice(j * step, (j + 1) * step)
        pre = dot(x, full_ref[:, here])
        below = 0.5 + 0.5 * lax.erf(pre * 0.7071067811865476)
        bell = jnp.exp(pre * pre * -0.5) * 0.3989422804014327
        act_ref[:, here] = (pre * below).astype(jnp.bfloat16)
        slope_ref[:, here] = (below + pre * bell).astype(jnp.bfloat16)
    back.wait()


def middle(context, tokens, table, buffers, after=()):
    rows, width = context.shape
    columns = buffers[0].shape[3]
    inner = columns - width - 128
    return run(
        functools.partial(middle_kernel, len(buffers)),
        (table, context, tokens, *buffers),
        after,
        in_specs=[SCALARS, whole((rows, width)), whole((rows, width))] + [HBM] * len(buffers),
        out_specs=[
            whole((rows, width)),
            whole((rows, 1)),
            whole((rows, width)),
            whole((8, width)),
            whole((rows, inner)),
            whole((rows, inner)),
            HBM,
        ],
        out_shape=[
            jax.ShapeDtypeStruct((rows, width), jnp.float32),
            jax.ShapeDtypeStruct((rows, 1), jnp.float32),
            jax.ShapeDtypeStruct((rows, width), jnp.bfloat16),
            jax.ShapeDtypeStruct((8, width), jnp.float32),
            jax.ShapeDtypeStruct((rows, inner), jnp.bfloat16),
            jax.ShapeDtypeStruct((rows, inner), jnp.bfloat16),
            jax.ShapeDtypeStruct((width, columns), jnp.bfloat16),
        ],
        scratch_shapes=[
            pltpu.VMEM((width, columns), jnp.bfloat16),
            pltpu.SemaphoreType.DMA,
            pltpu.SemaphoreType.DMA,
        ],
        compiler_params=grant(56),
        cost_estimate=NO_COST,
    )


def down_kernel(count, table_ref, act_ref, xhat_ref, norm_ref, up_ref, *refs):
    sources = refs[:count]
    out_ref, second_ref, ff_ref, norms_ref, kept_ref, full_ref, sem, back_sem = refs[count:]
    step = pl.program_id(0)
    back = pltpu.make_async_copy(full_ref, kept_ref, back_sem)

    @pl.when(step == 0)
    def _():
        for copy in start_slabs(table_ref, sources, full_ref, sem):
            copy.wait()
        back.start()
        norms_ref[...] = jnp.zeros_like(norms_ref)

    first_out = xhat_ref[...] * norm_ref[0:1] + norm_ref[1:2]
    xhat, scale = normalise(first_out + dot(act_ref[...], full_ref[...]))
    out_ref[...] = (xhat * norm_ref[2:3] + norm_ref[3:4]).astype(jnp.bfloat16)
    upstream = up_ref[...].astype(jnp.float32)
    grad = norm_back(upstream, xhat, scale, norm_ref[2:3])
    second_ref[...] = grad
    ff_ref[...] = grad.astype(jnp.bfloat16)
    norms_ref[0:1] += jnp.sum(upstream * xhat, axis=0, keepdims=True)
    norms_ref[1:2] += jnp.sum(upstream, axis=0, keepdims=True)

    @pl.when(step == pl.num_programs(0) - 1)
    def _():
        back.wait()


def down_norm(act, table, buffers, xhat, norm_rows, upstream, after=()):
    rows, inner = act.shape
    width = xhat.shape[1]
    step = 128
    block = pl.BlockSpec((step, width), lambda i: (i, 0))
    return run(
        functools.partial(down_kernel, len(buffers)),
        (table, act, xhat, norm_rows, upstream, *buffers),
        after,
        grid=(rows // step,),
        in_specs=[
            SCALARS,
            pl.BlockSpec((step, inner), lambda i: (i, 0)),
            block,
            whole(norm_rows.shape),
            block,
        ]
        + [HBM] * len(buffers),
        out_specs=[block] * 3 + [whole((2, width)), HBM],
        out_shape=[
            jax.ShapeDtypeStruct((rows, width), jnp.bfloat16),
            jax.ShapeDtypeStruct((rows, width), jnp.float32),
            jax.ShapeDtypeStruct((rows, width), jnp.bfloat16),
            jax.ShapeDtypeStruct((2, width), jnp.float32),
            jax.ShapeDtypeStruct((inner, width), jnp.bfloat16),
        ],
        scratch_shapes=[
            pltpu.VMEM((inner, width), jnp.bfloat16),
            pltpu.SemaphoreType.DMA,
            pltpu.SemaphoreType.DMA,
        ],
        compiler_params=grant(56),
        cost_estimate=NO_COST,
    )


def share(core, value, kept_ref, sent_ref, columns):
    places, rows, _ = kept_ref.shape
    value = value.astype(jnp.bfloat16).reshape(places, 2, rows, value.shape[1])
    low, high = value[:, 0], value[:, 1]
    kept_ref[:, :, columns] = jnp.where(core == 0, low, high)
    sent_ref[:, :, columns] = jnp.where(core == 0, high, low)


def rows_grad_kernel(core_ref, left_ref, right_ref, *refs):
    kept_ref, sent_ref, turned_ref = refs[-3:]

    @pl.when(pl.program_id(0) == 0)
    def _():
        turned_ref[...] = left_ref[...].T

    right = right_ref[...].reshape(right_ref.shape[-2:])
    share(core_ref[0], dot(turned_ref[...], right), kept_ref, sent_ref, slice(None))


def rows_grad(core, left, right, rows, into=None, after=()):
    tokens, width = left.shape
    places = width // rows // 2
    step = 512
    each = right.shape[-1] // step
    steps = right.size // tokens // step
    if right.ndim == 3:
        block = pl.BlockSpec((1, tokens, step), lambda i: (i // each, 0, i % each))
    else:
        block = pl.BlockSpec((tokens, step), lambda i: (0, i))
    out = pl.BlockSpec((places, rows, step), lambda i: (0, 0, i))
    into = tuple(into) if into else ()
    columns = into[0].shape[2] if into else steps * step
    return run(
        rows_grad_kernel,
        (core, left, right, *into,),
        after,
        grid=(steps,),
        in_specs=[SCALARS, whole((tokens, width)), block] + [HBM] * len(into),
        out_specs=[out, out],
        out_shape=[jax.ShapeDtypeStruct((places, rows, columns), jnp.bfloat16)] * 2,
        input_output_aliases={3: 0, 4: 1} if into else {},
        scratch_shapes=[pltpu.VMEM((width, tokens), jnp.bfloat16)],
        compiler_params=grant(56),
        cost_estimate=NO_COST,
    )


def ffn_back_kernel(
    core_ref,
    act_ref,
    slope_ref,
    w_down_ref,
    w_up_ref,
    grad_ref,
    low_ref,
    second_ref,
    xhat_ref,
    scale_ref,
    norm_ref,
    down_kept_ref,
    down_sent_ref,
    up_kept_ref,
    up_sent_ref,
    in_ref,
    branch_ref,
    norms_ref,
    turned_ref,
    sum_ref,
):
    step = pl.program_id(0)
    core = core_ref[0]

    @pl.when(step == 0)
    def _():
        turned_ref[...] = low_ref[...].T
        sum_ref[...] = second_ref[...]

    grad = grad_ref[...]
    back = dot(grad, w_down_ref[...], LAST) * slope_ref[...].astype(jnp.float32)
    back = back.astype(jnp.bfloat16)
    share(core, dot(act_ref[...].T, grad), down_kept_ref, down_sent_ref, slice(None))
    share(core, dot(turned_ref[...], back), up_kept_ref, up_sent_ref, slice(None))
    sum_ref[...] += dot(back, w_up_ref[...], LAST)

    @pl.when(step == pl.num_programs(0) - 1)
    def _():
        gain_sum = shift_sum = 0.0
        chunk = 128
        for j in range(sum_ref.shape[0] // chunk):
            here = slice(j * chunk, (j + 1) * chunk)
            first, xhat = sum_ref[here], xhat_ref[here]
            back = norm_back(first, xhat, scale_ref[here], norm_ref[0:1])
            in_ref[here] = back
            branch_ref[here] = back.astype(jnp.bfloat16)
            gain_sum = gain_sum + jnp.sum(first * xhat, axis=0, keepdims=True)
            shift_sum = shift_sum + jnp.sum(first, axis=0, keepdims=True)
        norms_ref[0:1] = gain_sum
        norms_ref[1:2] = shift_sum


def ffn_back(core, act, slope, w_down, w_up, grad, low, second, xhat, scale, norm_rows, rows, ff_rows):
    tokens, inner = act.shape
    width = grad.shape[1]
    step = 512
    places = width // rows // 2
    ff_places = inner // ff_rows // 2
    here = step // ff_rows // 2
    columns = pl.BlockSpec((tokens, step), lambda i: (0, i))
    down_out = pl.BlockSpec((here, ff_rows, width), lambda i: (i, 0, 0))
    up_out = pl.BlockSpec((places, rows, step), lambda i: (0, 0, i))
    down_shape = jax.ShapeDtypeStruct((ff_places, ff_rows, width), jnp.bfloat16)
    up_shape = jax.ShapeDtypeStruct((places, rows, inner + width + 128), jnp.bfloat16)
    return run(
        ffn_back_kernel,
        (core, act, slope, w_down, w_up, grad, low, second, xhat, scale, norm_rows),
        grid=(inner // step,),
        in_specs=[
            SCALARS,
            columns,
            columns,
            pl.BlockSpec((step, width), lambda i: (i, 0)),
            pl.BlockSpec((width, step), lambda i: (0, i)),
            whole((tokens, width)),
            whole((tokens, width)),
            whole((tokens, width)),
            whole((tokens, width)),
            whole((tokens, 1)),
            whole(norm_rows.shape),
        ],
        out_specs=[down_out, down_out, up_out, up_out]
        + [whole((tokens, width))] * 2
        + [whole((2, width))],
        out_shape=[
            down_shape,
            down_shape,
            up_shape,
            up_shape,
            jax.ShapeDtypeStruct((tokens, width), jnp.float32),
            jax.ShapeDtypeStruct((tokens, width), jnp.bfloat16),
            jax.ShapeDtypeStruct((2, width), jnp.float32),
        ],
        scratch_shapes=[
            pltpu.VMEM((width, tokens), jnp.bfloat16),
            pltpu.VMEM((tokens, width), jnp.float32),
        ],
        compiler_params=grant(56),
        cost_estimate=NO_COST,
    )


def out_grad_kernel(
    core_ref,
    context_ref,
    grad_ref,
    w_ref,
    one_ref,
    two_ref,
    kept_in,
    sent_in,
    back_ref,
    kept_hbm,
    sent_hbm,
    kept_ref,
    sent_ref,
    sems,
):
    core = core_ref[0]
    width = w_ref.shape[0]
    grad = grad_ref[...]
    turned = context_ref[...].T
    step = 256
    for j in range(width // step):
        here = slice(j * step, (j + 1) * step)
        share(core, dot(turned, grad[:, here]), kept_ref, sent_ref, here)
    norms = jnp.concatenate([one_ref[...], two_ref[...], jnp.zeros((124, width), jnp.float32)], 0)
    share(core, norms.T, kept_ref, sent_ref, slice(width, width + 128))
    last = pl.ds(kept_hbm.shape[2] - width - 128, width + 128)
    copies = [
        pltpu.make_async_copy(kept_ref, kept_hbm.at[:, :, last], sems.at[0]),
        pltpu.make_async_copy(sent_ref, sent_hbm.at[:, :, last], sems.at[1]),
    ]
    for copy in copies:
        copy.start()
    for j in range(width // step):
        here = slice(j * step, (j + 1) * step)
        back_ref[:, here] = dot(grad, w_ref[here], LAST).astype(jnp.bfloat16)
    for copy in copies:
        copy.wait()


def out_grad(core, context, grad, w_up, norms_one, norms_two, kept, sent, after=()):
    tokens, width = context.shape
    part = pltpu.VMEM(kept.shape[:2] + (width + 128,), jnp.bfloat16)
    out = kept.shape
    return run(
        out_grad_kernel,
        (core, context, grad, w_up, norms_one, norms_two, kept, sent),
        after,
        grid=(1,),
        in_specs=[
            SCALARS,
            whole((tokens, width)),
            whole((tokens, width)),
            pl.BlockSpec((width, width), lambda i: (0, w_up.shape[1] // width - 1)),
            whole((2, width)),
            whole((2, width)),
            HBM,
            HBM,
        ],
        out_specs=[whole((tokens, width)), HBM, HBM],
        out_shape=[
            jax.ShapeDtypeStruct((tokens, width), jnp.bfloat16),
            jax.ShapeDtypeStruct(out, jnp.bfloat16),
            jax.ShapeDtypeStruct(out, jnp.bfloat16),
        ],
        input_output_aliases={6: 1, 7: 2},
        scratch_shapes=[part, part, pltpu.SemaphoreType.DMA((2,))],
        compiler_params=grant(56),
        cost_estimate=NO_COST,
    )


def tokens_grad_kernel(grad_ref, w_ref, first_ref, out_ref, sum_ref):
    step = pl.program_id(0)

    @pl.when(step == 0)
    def _():
        sum_ref[...] = first_ref[...]

    sum_ref[...] += dot(grad_ref[0], w_ref[...], LAST)

    @pl.when(step == pl.num_programs(0) - 1)
    def _():
        out_ref[...] = sum_ref[...].astype(jnp.bfloat16)


def tokens_grad(grad_mixed, w_first, first, after=()):
    count, tokens, width = grad_mixed.shape
    return run(
        tokens_grad_kernel,
        (grad_mixed, w_first, first,),
        after,
        grid=(count,),
        in_specs=[
            pl.BlockSpec((1, tokens, width), lambda i: (i, 0, 0)),
            pl.BlockSpec((width, width), lambda i: (0, i)),
            whole((tokens, width)),
        ],
        out_specs=whole((tokens, width)),
        out_shape=jax.ShapeDtypeStruct((tokens, width), jnp.bfloat16),
        scratch_shapes=[pltpu.VMEM((tokens, width), jnp.float32)],
        compiler_params=grant(56),
        cost_estimate=NO_COST,
    )


def fold_kernel(place_ref, kept_ref, came_ref, a_own_ref, a_out_ref, b_own_ref, b_out_ref):
    x, y = place_ref[0], place_ref[1]
    half = a_own_ref.shape[2]
    part = lambda ref, i, j, rows: ref[0, i, j, rows].astype(jnp.float32)
    low, high = pl.ds(0, half), pl.ds(half, half)
    for i in range(2):
        both = lambda a, b, rows: (part(kept_ref, a, b, rows) + part(came_ref, a, b, rows)).astype(
            jnp.bfloat16
        )
        a_own_ref[0, i] = both(i, y, low)
        a_out_ref[0, i] = both(i, 1 - y, low)
        b_own_ref[0, i] = both(x, i, high)
        b_out_ref[0, i] = both(1 - x, i, high)


def fold_plane_kernel(place_ref, *refs):
    for i in range(2):
        own_ref, came_ref = refs[2 * i], refs[2 * i + 1]
        keep_ref, out_ref = refs[4 + 2 * i], refs[5 + 2 * i]
        place = place_ref[i]
        for ref, index in ((keep_ref, place), (out_ref, 1 - place)):
            total = own_ref[0, index].astype(jnp.float32) + came_ref[0, index].astype(jnp.float32)
            ref[0] = total.astype(jnp.bfloat16)


def fold_plane(place, a_own, a_came, b_own, b_came, after=()):
    zs, both, rows, columns = a_own.shape
    block = pl.BlockSpec((1, both, rows, columns), lambda i: (i, 0, 0, 0))
    out = pl.BlockSpec((1, rows, columns), lambda i: (i, 0, 0))
    return run(
        fold_plane_kernel,
        (place, a_own, a_came, b_own, b_came),
        after,
        grid=(zs,),
        in_specs=[SCALARS] + [block] * 4,
        out_specs=[out] * 4,
        out_shape=[jax.ShapeDtypeStruct((zs, rows, columns), jnp.bfloat16)] * 4,
        compiler_params=grant(20),
        cost_estimate=NO_COST,
    )


def fold(place, kept, came, after=()):
    zs, xs, ys, rows, columns = kept.shape
    out = pl.BlockSpec((1, 2, rows // 2, columns), lambda i: (i, 0, 0, 0))
    block = pl.BlockSpec((1, xs, ys, rows, columns), lambda i: (i, 0, 0, 0, 0))
    return run(
        fold_kernel,
        (place, kept, came,),
        after,
        grid=(zs,),
        in_specs=[SCALARS, block, block],
        out_specs=[out] * 4,
        out_shape=[jax.ShapeDtypeStruct((zs, 2, rows // 2, columns), jnp.bfloat16)] * 4,
        compiler_params=grant(20),
        cost_estimate=NO_COST,
    )


def gate(values, after=(), room=None):
    return run(
        lambda *refs: None,
        values,
        after,
        in_specs=[pl.BlockSpec(memory_space=pl.ANY)] * len(values),
        out_specs=[pl.BlockSpec(memory_space=pl.ANY)] * len(values),
        out_shape=[jax.ShapeDtypeStruct(v.shape, v.dtype) for v in values],
        input_output_aliases={i: i for i in range(len(values))},
        compiler_params=grant(room) if room else None,
    )


def routes(move):
    pairs = []
    for place in range(32):
        z, x, y, c = place // 8, place // 4 % 2, place // 2 % 2, place % 2
        target = move(z, x, y, c)
        if target is not None:
            tz, tx, ty, tc = target
            pairs.append((place, tz * 8 + tx * 4 + ty * 2 + tc))
    return pairs


ROUTE_X = routes(lambda z, x, y, c: (z, 1 - x, y, c))
ROUTE_Y = routes(lambda z, x, y, c: (z, x, 1 - y, c))
ROUTE_C = routes(lambda z, x, y, c: (z, x, y, 1 - c))


def send(value, route):
    return lax.ppermute(value, ALL, route)


def coordinates():
    dp = lax.axis_index("dp")
    return dp // 2, dp % 2, lax.axis_index("blk"), lax.axis_index("head")


def side_kernel(left_ref, right_ref, out_ref):
    middle = left_ref.shape[1]
    out_ref[:, :middle] = left_ref[...]
    out_ref[:, middle:] = right_ref[...]


def side_by_side(left, right, after):
    blocks, first, columns = left.shape
    both = first + right.shape[1]
    return run(
        side_kernel,
        (left, right),
        after,
        grid=(blocks,),
        in_specs=[
            pl.BlockSpec((1,) + left.shape[1:], lambda i: (i, 0, 0)),
            pl.BlockSpec((1,) + right.shape[1:], lambda i: (i, 0, 0)),
        ],
        out_specs=pl.BlockSpec((1, both, columns), lambda i: (i, 0, 0)),
        out_shape=jax.ShapeDtypeStruct((blocks, both, columns), left.dtype),
        cost_estimate=NO_COST,
    )


def sum_of(values):
    total = None
    for value in values:
        value = value.astype(jnp.float32)
        total = value if total is None else total + value
    return total


def slot_rows(buffers, rows):
    z, x, y, c = coordinates()
    tables = []
    for value, part, axis, dx, dy, dc in buffers:
        js = jnp.arange(value.shape[0])[:, None]
        zs = jnp.arange(4)[None, :]
        sx = (x ^ dx ^ js) if axis == 0 else x ^ dx
        sy = (y ^ dy ^ js) if axis == 1 else y ^ dy
        device = ((zs * 2 + sx) * 2 + sy) * 2 + (c ^ dc)
        tables.append((device * rows + part * (rows // 2)).reshape(-1))
    return jnp.concatenate(tables).astype(jnp.int32)


def pick(value, index, axis):
    return lax.dynamic_index_in_dim(value, index, axis, keepdims=False)


def fold_cores(kept, came, after):
    z, x, y, c = coordinates()
    shape = (4, 2, 2) + kept.shape[1:]
    return fold(jnp.stack([x, y]), kept.reshape(shape), came.reshape(shape), after)


def natural(kept, sent):
    return jnp.stack([kept, sent], axis=1).reshape(-1, kept.shape[2])


def joined_shards(up_weight, out_weight, norm_params):
    norm_wide = jnp.pad(norm_params, ((0, 0), (0, 128 - norm_params.shape[1])))
    return jnp.concatenate([up_weight, out_weight, norm_wide], axis=1)


def split_up(grad, width):
    inner = grad.shape[1] - width - 128
    last = inner + width
    return tuple(
        part.astype(jnp.float32)
        for part in (grad[:, :inner], grad[:, inner:last], grad[:, last : last + 4])
    )


def buffers_of(a2, ay, b2, bx):
    return [(a2, 0, 0, 0, 0), (ay, 0, 0, 0, 1), (b2, 1, 1, 0, 0), (bx, 1, 1, 1, 0)]


def with_partner(shard, own, partner):
    buffers = [b + (0,) for b in own]
    buffers += [(v,) + b[1:] + (1,) for v, b in zip(partner, own)]
    return slot_rows(buffers, shard.shape[0]), [b[0] for b in buffers]


def body_lines(
    tokens, doc_lengths, qkv_weight, out_weight, up_weight, down_weight, norm_params, out_cotangent
):
    seqs_here, local_len, width = tokens.shape
    full_len = local_len * 4
    z, x, y, c = coordinates()
    place = y * 2 + c
    core = c.reshape(1)
    slab, ff_slab = up_weight.shape[0], down_weight.shape[0]
    exchange = lambda v: lax.all_to_all(v, GROUP, split_axis=0, concat_axis=0, tiled=True)
    to_sequence = lambda v: exchange(v).reshape(full_len, width)
    to_positions = lambda v: exchange(v.reshape(seqs_here, local_len, width))
    own_lengths = lax.dynamic_slice_in_dim(doc_lengths, place, 1, 0)
    seg_row = segments_of(own_lengths, full_len)
    seg_col = seg_row.reshape(full_len, 1)
    first_own, up_own = qkv_weight, joined_shards(up_weight, out_weight, norm_params)
    half, ff_half = slab // 2, ff_slab // 2
    line = lambda v: lax.all_gather(v, "dp", axis_index_groups=LINES)

    first_line = line(first_own)
    down_a, down_b = down_weight[:ff_half], down_weight[ff_half:]
    down_ax, down_by = send(down_a, ROUTE_X), send(down_b, ROUTE_Y)
    both = exchange(side_by_side(tokens, out_cotangent, ()))
    rows, upstream = (
        v.reshape(full_len, width) for v in (both[:, :local_len], both[:, local_len:])
    )
    down_own = jnp.stack([down_a, down_ax, down_b, down_by])

    a, b = gate(
        (first_line[:, :half], first_line[:, half:]),
        (rows, upstream, down_own, seg_row, seg_col),
    )
    ax, by = send(a, ROUTE_X), send(b, ROUTE_Y)
    up_line = line(up_own)

    a2, b2 = gate((jnp.stack([a, ax]), jnp.stack([b, by])))
    ay, bx = send(a2, ROUTE_Y), send(b2, ROUTE_X)

    up_a, up_b, down_own = gate((up_line[:, :half], up_line[:, half:], down_own))
    up_ax, up_by = send(up_a, ROUTE_X), send(up_b, ROUTE_Y)
    down_line = line(down_own)

    ay, bx, up_ax, up_by, a2, b2 = gate((ay, bx, up_ax, up_by, a2, b2))
    a2c, b2c = send(a2, ROUTE_C), send(b2, ROUTE_C)
    ayc, bxc = send(ay, ROUTE_C), send(bx, ROUTE_C)
    up_a2, up_b2 = jnp.stack([up_a, up_ax]), jnp.stack([up_b, up_by])
    up_ay, up_bx = send(up_a2, ROUTE_Y), send(up_b2, ROUTE_X)
    up_a2c, up_b2c = send(up_a2, ROUTE_C), send(up_b2, ROUTE_C)
    table, buffers = with_partner(
        first_own, buffers_of(a2, ay, b2, bx), (a2c, ayc, b2c, bxc)
    )
    projected, w_first = project(rows, table, buffers, 3 * width)
    context, log_sums = attention(projected, seg_col, seg_row)

    up_ay, up_bx, up_a2c, up_b2c, down_line, context = gate(
        (up_ay, up_bx, up_a2c, up_b2c, down_line, context)
    )
    down_a2, down_b2 = jnp.swapaxes(down_line[:, :2], 0, 1), jnp.swapaxes(down_line[:, 2:], 0, 1)
    down_ay, down_bx = send(down_a2, ROUTE_Y), send(down_b2, ROUTE_X)
    down_a2c, down_b2c = send(down_a2, ROUTE_C), send(down_b2, ROUTE_C)
    up_ayc, up_bxc = send(up_ay, ROUTE_C), send(up_bx, ROUTE_C)
    table, buffers = with_partner(
        up_own, buffers_of(up_a2, up_ay, up_b2, up_bx), (up_a2c, up_ayc, up_b2c, up_bxc)
    )
    xhat, scale, first_low, norm_rows, act, slope, w_up = middle(context, rows, table, buffers)

    down_ay, down_bx, down_a2c, down_b2c, act = gate((down_ay, down_bx, down_a2c, down_b2c, act))
    down_ayc, down_bxc = send(down_ay, ROUTE_C), send(down_bx, ROUTE_C)
    table, buffers = with_partner(
        down_weight,
        buffers_of(down_a2, down_ay, down_b2, down_bx),
        (down_a2c, down_ayc, down_b2c, down_bxc),
    )
    result, grad_second, grad_ff, norms_two, w_down = down_norm(
        act, table, buffers, xhat, norm_rows, upstream
    )

    low = lambda *v: sum_of(v).astype(jnp.bfloat16)
    place_xy = jnp.stack([x, y])
    layer_out = to_positions(result)
    down_kept, down_sent, up_kept, up_sent, grad_first_in, grad_branch, norms_one = ffn_back(
        core,
        act,
        slope,
        w_down,
        w_up,
        grad_ff,
        first_low,
        grad_second,
        xhat,
        scale,
        norm_rows,
        slab,
        ff_slab,
    )

    down_sent, grad_branch = gate((down_sent, grad_branch), (layer_out,))
    down_came = send(down_sent, ROUTE_C)
    grad_context, up_kept, up_sent = out_grad(
        core, context, grad_branch, w_up, norms_one, norms_two, up_kept, up_sent
    )

    da_own, da_out, db_own, db_out = fold_cores(down_kept, down_came, (grad_context,))
    da_out, db_out, up_sent, grad_context = gate((da_out, db_out, up_sent, grad_context), (), 1)
    da_in, db_in = send(da_out, ROUTE_Y), send(db_out, ROUTE_X)
    up_came = send(up_sent, ROUTE_C)
    grad_mixed = attention_back(projected, grad_context, seg_col, seg_row, log_sums)

    ua_own, ua_out, ub_own, ub_out = fold_cores(up_kept, up_came, (grad_mixed, da_in, db_in))
    down_blocks = jnp.concatenate([low(da_own, da_in), low(db_own, db_in)], axis=1)
    ua_out, ub_out, down_blocks, grad_mixed = gate((ua_out, ub_out, down_blocks, grad_mixed), (), 1)
    ua_in, ub_in = send(ua_out, ROUTE_Y), send(ub_out, ROUTE_X)
    down_sum = lax.psum_scatter(
        down_blocks, "dp", scatter_dimension=0, axis_index_groups=LINES, tiled=False
    )
    last_kept, last_sent = rows_grad(core, rows, grad_mixed, slab)
    grad_tokens = tokens_grad(grad_mixed, w_first, grad_first_in, (last_sent,))

    ua_own, ua_out, ub_own, ub_out = fold_plane(
        place_xy, ua_own, ua_in, ub_own, ub_in, (grad_tokens,)
    )
    ua_out, ub_out, last_sent = gate((ua_out, ub_out, last_sent), (), 1)
    ua_in2, ub_in2 = send(ua_out, ROUTE_X), send(ub_out, ROUTE_Y)
    last_came = send(last_sent, ROUTE_C)

    la_own, la_out, lb_own, lb_out = fold_cores(last_kept, last_came, (ua_in2, ub_in2))
    up_blocks = jnp.concatenate([low(ua_own, ua_in2), low(ub_own, ub_in2)], axis=1)
    up_blocks, la_out, lb_out, down_sum = gate((up_blocks, la_out, lb_out, down_sum), (), 1)
    up_sum = lax.psum_scatter(
        up_blocks, "dp", scatter_dimension=0, axis_index_groups=LINES, tiled=False
    )
    la_in, lb_in = send(la_out, ROUTE_Y), send(lb_out, ROUTE_X)
    da_in = send(pick(down_sum[:2], 1 - x, 0), ROUTE_X)
    db_in = send(pick(down_sum[2:], 1 - y, 0), ROUTE_Y)

    la_own, la_out, lb_own, lb_out = fold_plane(
        place_xy, la_own, la_in, lb_own, lb_in, (da_in, db_in)
    )
    la_out, lb_out, grad_tokens = gate((la_out, lb_out, grad_tokens), (), 1)
    la_in2, lb_in2 = send(la_out, ROUTE_X), send(lb_out, ROUTE_Y)
    grad_down = jnp.concatenate(
        [sum_of([pick(down_sum[:2], x, 0), da_in]), sum_of([pick(down_sum[2:], y, 0), db_in])],
        axis=0,
    )

    last_blocks = jnp.concatenate([low(la_own, la_in2), low(lb_own, lb_in2)], axis=1)
    last_blocks, grad_tokens, up_sum = gate((last_blocks, grad_tokens, up_sum), (), 1)
    input_grad = to_positions(grad_tokens)
    last_sum = lax.psum_scatter(
        last_blocks, "dp", scatter_dimension=0, axis_index_groups=LINES, tiled=False
    )
    grad_qkv = last_sum.astype(jnp.float32)
    grad_up, grad_out, grad_norm = split_up(up_sum, width)
    return (
        layer_out,
        input_grad.astype(jnp.float32),
        grad_qkv,
        grad_out,
        grad_up,
        grad_down,
        grad_norm,
    )


def body_any(
    tokens, doc_lengths, qkv_weight, out_weight, up_weight, down_weight, norm_params, out_cotangent
):
    seqs_here, local_len, width = tokens.shape
    ff = up_weight.shape[1]
    full_len = local_len * lax.axis_size("blk") * lax.axis_size("head")
    place = lax.axis_index("blk") * lax.axis_size("head") + lax.axis_index("head")
    core = jnp.zeros((1,), jnp.int32)
    slab, ff_slab = width // 32, ff // 32
    exchange = lambda v: lax.all_to_all(v, GROUP, split_axis=0, concat_axis=0, tiled=True)
    to_sequence = lambda v: exchange(v).reshape(full_len, width)
    to_positions = lambda v: exchange(v.reshape(seqs_here, local_len, width))

    def gather(shard):
        return core, [lax.all_gather(shard, ALL, axis=0, tiled=True)[None, None]]

    def scatter(kept, sent):
        total = lax.psum_scatter(natural(kept, sent), ALL, scatter_dimension=0, tiled=True)
        return total.astype(jnp.float32)

    rows = to_sequence(tokens)
    upstream = to_sequence(out_cotangent)
    own_lengths = lax.dynamic_slice_in_dim(doc_lengths, place, 1, 0)
    seg_row = segments_of(own_lengths, full_len)
    seg_col = seg_row.reshape(full_len, 1)
    first_slots = gather(qkv_weight)
    up_slots = gather(joined_shards(up_weight, out_weight, norm_params))
    projected, w_first = project(rows, *first_slots, 3 * width)
    context, log_sums = attention(projected, seg_col, seg_row)
    xhat, scale, first_low, norm_rows, act, slope, w_up = middle(context, rows, *up_slots)
    result, grad_second, grad_ff, norms_two, w_down = down_norm(
        act, *gather(down_weight), xhat, norm_rows, upstream
    )
    down_kept, down_sent, up_kept, up_sent, grad_first_in, grad_branch, norms_one = ffn_back(
        core,
        act,
        slope,
        w_down,
        w_up,
        grad_ff,
        first_low,
        grad_second,
        xhat,
        scale,
        norm_rows,
        slab,
        ff_slab,
    )
    grad_down = scatter(down_kept, down_sent)
    grad_context, up_kept, up_sent = out_grad(
        core, context, grad_branch, w_up, norms_one, norms_two, up_kept, up_sent
    )
    grad_up, grad_out, grad_norm = split_up(scatter(up_kept, up_sent), width)
    grad_mixed = attention_back(projected, grad_context, seg_col, seg_row, log_sums)
    grad_qkv = scatter(*rows_grad(core, rows, grad_mixed, slab))
    grad_tokens = tokens_grad(grad_mixed, w_first, grad_first_in)
    return (
        to_positions(result),
        to_positions(grad_tokens).astype(jnp.float32),
        grad_qkv,
        grad_out,
        grad_up,
        grad_down,
        grad_norm,
    )


def solution(mesh):
    sizes = tuple(mesh.shape[name] for name in ALL)
    body = body_lines if sizes == (8, 2, 2) else body_any
    placed = (
        P("dp", ("blk", "head"), None),
        P("dp", None),
        P(("dp", "blk", "head"), None),
        P(("dp", "blk", "head"), None),
        P(("dp", "blk", "head"), None),
        P(("dp", "blk", "head"), None),
        P(("dp", "blk", "head"), None),
        P("dp", ("blk", "head"), None),
    )
    return jax.shard_map(
        body,
        mesh=mesh,
        in_specs=placed,
        out_specs=(
            P("dp", ("blk", "head"), None),
            P("dp", ("blk", "head"), None),
            P(("dp", "blk", "head"), None),
            P(("dp", "blk", "head"), None),
            P(("dp", "blk", "head"), None),
            P(("dp", "blk", "head"), None),
            P(("dp", "blk", "head"), None),
        ),
        check_vma=False,
    )
```

```python
import functools

import jax
import jax.numpy as jnp
from jax import lax
from jax.experimental import pallas as pl
from jax.experimental.pallas import tpu as pltpu
from jax.sharding import PartitionSpec as P

HEAD_DIM = 64
ALL = ("dp", "blk", "head")
GROUP = ("blk", "head")
LINES = [[0, 2, 4, 6], [1, 3, 5, 7]]
epsilon = 1e-12


def segments_of(doc_lengths, length):
    doc_ends = jnp.cumsum(doc_lengths, axis=-1, dtype=jnp.int32)
    places = jnp.arange(length, dtype=jnp.int32)
    passed = jnp.sum(
        (doc_ends[..., None, :] <= places[:, None]).astype(jnp.int32), axis=-1, dtype=jnp.int32
    )
    return jnp.where(places < doc_ends[..., -1:], passed + 1, 0)


def run(kernel, operands, after=(), in_specs=(), scalars=0, grid=(1,), out_specs=None, scratch_shapes=(), **rest):
    count = len(operands)

    def body(*refs):
        kernel(*refs[:count], *refs[count + len(after) :])

    specs = list(in_specs) + [pl.BlockSpec(memory_space=pl.ANY)] * len(after)
    spec = pltpu.PrefetchScalarGridSpec(
        num_scalar_prefetch=scalars,
        grid=grid,
        in_specs=specs,
        out_specs=out_specs,
        scratch_shapes=scratch_shapes,
    )
    return pl.pallas_call(body, grid_spec=spec, **rest)(*operands, *after)


MIB = 2**20
NO_COST = pl.CostEstimate(flops=1, bytes_accessed=1, transcendentals=0)
LAST = (((1,), (1,)), ((), ()))
FIRST = (((0,), (0,)), ((), ()))


def grant(mib):
    return pltpu.CompilerParams(vmem_limit_bytes=mib * MIB)


def dot(left, right, form=(((1,), (0,)), ((), ()))):
    return lax.dot_general(left, right, form, preferred_element_type=jnp.float32)


def whole(shape):
    return pl.BlockSpec(shape, lambda *_: (0,) * len(shape))


HBM = pl.BlockSpec(memory_space=pltpu.HBM)
SCALARS = pl.BlockSpec(memory_space=pltpu.SMEM)


def attn_fwd_kernel(q_ref, k_ref, v_ref, segc_ref, segr_ref, out_ref, lse_ref):
    length = q_ref.shape[0]
    scaled = q_ref[...] * jnp.bfloat16(HEAD_DIM ** (-0.5))
    key_pair = k_ref[...]
    value_t = v_ref[...].T
    lanes = lax.broadcasted_iota(jnp.int32, key_pair.shape, 1)
    allowed = segc_ref[...] == segr_ref[...]
    parts = []
    for h in range(2):
        own = (lanes >= h * HEAD_DIM) & (lanes < (h + 1) * HEAD_DIM)
        keys = jnp.where(own, key_pair, jnp.zeros_like(key_pair))
        scores = lax.dot_general(
            keys, scaled, (((1,), (1,)), ((), ())), preferred_element_type=jnp.float32
        )
        scores = jnp.where(allowed, scores, -1e30)
        largest = jnp.max(scores, axis=0, keepdims=True)
        powers = jnp.exp(scores - largest)
        totals = jnp.sum(powers, axis=0, keepdims=True)
        probs = (powers * (1.0 / totals)).astype(jnp.bfloat16)
        parts.append(
            jnp.dot(
                value_t[h * HEAD_DIM : (h + 1) * HEAD_DIM], probs, preferred_element_type=jnp.float32
            )
        )
        lse_ref[0, h : h + 1, :] = largest + jnp.log(totals)
    live = (segc_ref[...] != 0).astype(jnp.float32)
    context = jnp.concatenate(parts, axis=0).T * live
    out_ref[...] = context.astype(jnp.bfloat16)


def attn_bwd_kernel(
    q_ref, k_ref, v_ref, g_ref, segc_ref, segr_ref, lse_ref, *refs
):
    out_ref = refs[-1]
    scaled = q_ref[...] * jnp.bfloat16(HEAD_DIM ** (-0.5))
    key_pair = k_ref[...]
    value_pair = v_ref[...]
    key_t = key_pair.T
    grads = jnp.where(segc_ref[...] != 0, g_ref[...], jnp.zeros_like(g_ref[...]))
    lanes = lax.broadcasted_iota(jnp.int32, key_pair.shape, 1)
    allowed = segc_ref[...] == segr_ref[...]
    contract = (((1,), (1,)), ((), ()))
    dq_parts = []
    dk = None
    dv = None
    for h in range(2):
        own = (lanes >= h * HEAD_DIM) & (lanes < (h + 1) * HEAD_DIM)
        zero = jnp.zeros_like(key_pair)
        keys = jnp.where(own, key_pair, zero)
        values = jnp.where(own, value_pair, zero)
        queries = jnp.where(own, scaled, zero)
        grad_own = jnp.where(own, grads, zero)
        scores = lax.dot_general(keys, scaled, contract, preferred_element_type=jnp.float32)
        scores = jnp.where(allowed, scores, -1e30)
        probs = jnp.exp(scores - lse_ref[0, h : h + 1, :])
        grad_probs = lax.dot_general(values, grads, contract, preferred_element_type=jnp.float32)
        inner = jnp.sum(probs * grad_probs, axis=0, keepdims=True)
        grad_scores = (probs * (grad_probs - inner)).astype(jnp.bfloat16)
        dv_h = jnp.dot(probs.astype(jnp.bfloat16), grad_own, preferred_element_type=jnp.float32)
        dk_h = jnp.dot(grad_scores, queries, preferred_element_type=jnp.float32)
        dv = dv_h if dv is None else dv + dv_h
        dk = dk_h if dk is None else dk + dk_h
        dq_parts.append(
            jnp.dot(
                key_t[h * HEAD_DIM : (h + 1) * HEAD_DIM],
                grad_scores,
                preferred_element_type=jnp.float32,
            )
        )
    dq = jnp.concatenate(dq_parts, axis=0).T * (HEAD_DIM ** (-0.5))
    out_ref[0] = dq.astype(jnp.bfloat16)
    out_ref[1] = dk.astype(jnp.bfloat16)
    out_ref[2] = dv.astype(jnp.bfloat16)


def attention(projected, seg_col, seg_row, after=()):
    length, width3 = projected.shape
    width = width3 // 3
    pairs = width // (2 * HEAD_DIM)
    lane = 2 * HEAD_DIM
    col = lambda base: pl.BlockSpec((length, lane), lambda i: (0, base * pairs + i))
    return run(
        attn_fwd_kernel,
        (projected, projected, projected, seg_col, seg_row,),
        after,
        grid=(pairs,),
        in_specs=[
            col(0),
            col(1),
            col(2),
            pl.BlockSpec((length, 1), lambda i: (0, 0)),
            pl.BlockSpec((1, length), lambda i: (0, 0)),
        ],
        out_specs=[
            pl.BlockSpec((length, lane), lambda i: (0, i)),
            pl.BlockSpec((1, 2, length), lambda i: (i, 0, 0)),
        ],
        out_shape=[
            jax.ShapeDtypeStruct((length, width3 // 3), jnp.bfloat16),
            jax.ShapeDtypeStruct((pairs, 2, length), jnp.float32),
        ],
        compiler_params=grant(56),
        cost_estimate=NO_COST,
    )


def attention_back(projected, grad_context, seg_col, seg_row, lse, first=0, count=None, into=None, after=()):
    length, width3 = projected.shape
    width = width3 // 3
    pairs = width // (2 * HEAD_DIM)
    count = count or pairs
    lane = 2 * HEAD_DIM
    col = lambda base: pl.BlockSpec((length, lane), lambda i: (0, base * pairs + first + i))
    into = () if into is None else (into,)
    return run(
        attn_bwd_kernel,
        (projected, projected, projected, grad_context, seg_col, seg_row, lse, *into,),
        after,
        grid=(count,),
        in_specs=[
            col(0),
            col(1),
            col(2),
            col(0),
            pl.BlockSpec((length, 1), lambda i: (0, 0)),
            pl.BlockSpec((1, length), lambda i: (0, 0)),
            pl.BlockSpec((1, 2, length), lambda i: (first + i, 0, 0)),
        ]
        + [HBM] * len(into),
        out_specs=pl.BlockSpec((3, length, lane), lambda i: (0, 0, first + i)),
        out_shape=jax.ShapeDtypeStruct((3, length, width), jnp.bfloat16),
        input_output_aliases={7: 0} if into else {},
        compiler_params=grant(20),
        cost_estimate=NO_COST,
    )


def start_slabs(table_ref, sources, full_ref, sem):
    copies = []
    for source in sources:
        outer, inner, rows, _ = source.shape
        for o in range(outer):
            for i in range(inner):
                start = pl.multiple_of(table_ref[len(copies)], rows)
                copies.append(
                    pltpu.make_async_copy(source.at[o, i], full_ref.at[pl.ds(start, rows)], sem)
                )
                copies[-1].start()
    return copies


def project_kernel(count, table_ref, x_ref, *refs):
    sources, (out_ref, kept_ref, full_ref, sem, back_sem) = refs[:count], refs[count:]
    for copy in start_slabs(table_ref, sources, full_ref, sem):
        copy.wait()
    back = pltpu.make_async_copy(full_ref, kept_ref, back_sem)
    back.start()
    x = x_ref[...]
    step = 512
    for j in range(out_ref.shape[1] // step):
        here = slice(j * step, (j + 1) * step)
        out_ref[:, here] = dot(x, full_ref[:, here]).astype(jnp.bfloat16)
    back.wait()


def project(x, table, buffers, columns, after=()):
    total, full_columns = x.shape[1], buffers[0].shape[3]
    return run(
        functools.partial(project_kernel, len(buffers)),
        (table, x, *buffers,),
        after,
        in_specs=[SCALARS, whole(x.shape)] + [HBM] * len(buffers),
        out_specs=[whole((x.shape[0], columns)), HBM],
        out_shape=[
            jax.ShapeDtypeStruct((x.shape[0], columns), jnp.bfloat16),
            jax.ShapeDtypeStruct((total, full_columns), jnp.bfloat16),
        ],
        grid=(1,),
        scratch_shapes=[
            pltpu.VMEM((total, full_columns), jnp.bfloat16),
            pltpu.SemaphoreType.DMA,
            pltpu.SemaphoreType.DMA,
        ],
        compiler_params=grant(56),
        cost_estimate=NO_COST,
    )


def normalise(hidden):
    average = jnp.mean(hidden, axis=-1, keepdims=True)
    centred = hidden - average
    spread = jnp.mean(centred * centred, axis=-1, keepdims=True)
    scale = lax.rsqrt(spread + epsilon)
    return centred * scale, scale


def norm_back(grad, xhat, scale, gain):
    inner = grad * gain
    return scale * (
        inner
        - jnp.mean(inner, axis=-1, keepdims=True)
        - xhat * jnp.mean(inner * xhat, axis=-1, keepdims=True)
    )


def middle_kernel(count, table_ref, context_ref, tokens_ref, *refs):
    sources = refs[:count]
    (xhat_ref, scale_ref, low_ref, norms_ref, act_ref, slope_ref, kept_ref) = refs[count : count + 7]
    full_ref, sem, back_sem = refs[count + 7 :]
    for copy in start_slabs(table_ref, sources, full_ref, sem):
        copy.wait()
    back = pltpu.make_async_copy(full_ref, kept_ref, back_sem)
    back.start()
    inner, width = act_ref.shape[1], context_ref.shape[1]
    norms = full_ref[:, -128:].astype(jnp.float32).T[:8]
    norms_ref[...] = norms
    step = 128
    for j in range(context_ref.shape[0] // step):
        here = slice(j * step, (j + 1) * step)
        first_in = tokens_ref[here].astype(jnp.float32) + dot(
            context_ref[here], full_ref[:, inner : inner + width]
        )
        xhat, scale = normalise(first_in)
        xhat_ref[here] = xhat
        scale_ref[here] = scale
        low_ref[here] = (xhat * norms[0:1] + norms[1:2]).astype(jnp.bfloat16)
    x = low_ref[...]
    step = 256
    for j in range(inner // step):
        here = slice(j * step, (j + 1) * step)
        pre = dot(x, full_ref[:, here])
        below = 0.5 + 0.5 * lax.erf(pre * 0.7071067811865476)
        bell = jnp.exp(pre * pre * -0.5) * 0.3989422804014327
        act_ref[:, here] = (pre * below).astype(jnp.bfloat16)
        slope_ref[:, here] = (below + pre * bell).astype(jnp.bfloat16)
    back.wait()


def middle(context, tokens, table, buffers, after=()):
    rows, width = context.shape
    columns = buffers[0].shape[3]
    inner = columns - width - 128
    return run(
        functools.partial(middle_kernel, len(buffers)),
        (table, context, tokens, *buffers),
        after,
        in_specs=[SCALARS, whole((rows, width)), whole((rows, width))] + [HBM] * len(buffers),
        out_specs=[
            whole((rows, width)),
            whole((rows, 1)),
            whole((rows, width)),
            whole((8, width)),
            whole((rows, inner)),
            whole((rows, inner)),
            HBM,
        ],
        out_shape=[
            jax.ShapeDtypeStruct((rows, width), jnp.float32),
            jax.ShapeDtypeStruct((rows, 1), jnp.float32),
            jax.ShapeDtypeStruct((rows, width), jnp.bfloat16),
            jax.ShapeDtypeStruct((8, width), jnp.float32),
            jax.ShapeDtypeStruct((rows, inner), jnp.bfloat16),
            jax.ShapeDtypeStruct((rows, inner), jnp.bfloat16),
            jax.ShapeDtypeStruct((width, columns), jnp.bfloat16),
        ],
        scratch_shapes=[
            pltpu.VMEM((width, columns), jnp.bfloat16),
            pltpu.SemaphoreType.DMA,
            pltpu.SemaphoreType.DMA,
        ],
        compiler_params=grant(56),
        cost_estimate=NO_COST,
    )


def down_kernel(count, table_ref, act_ref, xhat_ref, norm_ref, up_ref, *refs):
    sources = refs[:count]
    out_ref, second_ref, ff_ref, norms_ref, kept_ref, full_ref, sem, back_sem = refs[count:]
    step = pl.program_id(0)
    back = pltpu.make_async_copy(full_ref, kept_ref, back_sem)

    @pl.when(step == 0)
    def _():
        for copy in start_slabs(table_ref, sources, full_ref, sem):
            copy.wait()
        back.start()
        norms_ref[...] = jnp.zeros_like(norms_ref)

    first_out = xhat_ref[...] * norm_ref[0:1] + norm_ref[1:2]
    xhat, scale = normalise(first_out + dot(act_ref[...], full_ref[...]))
    out_ref[...] = (xhat * norm_ref[2:3] + norm_ref[3:4]).astype(jnp.bfloat16)
    upstream = up_ref[...].astype(jnp.float32)
    grad = norm_back(upstream, xhat, scale, norm_ref[2:3])
    second_ref[...] = grad
    ff_ref[...] = grad.astype(jnp.bfloat16)
    norms_ref[0:1] += jnp.sum(upstream * xhat, axis=0, keepdims=True)
    norms_ref[1:2] += jnp.sum(upstream, axis=0, keepdims=True)

    @pl.when(step == pl.num_programs(0) - 1)
    def _():
        back.wait()


def down_norm(act, table, buffers, xhat, norm_rows, upstream, after=()):
    rows, inner = act.shape
    width = xhat.shape[1]
    step = 128
    block = pl.BlockSpec((step, width), lambda i: (i, 0))
    return run(
        functools.partial(down_kernel, len(buffers)),
        (table, act, xhat, norm_rows, upstream, *buffers),
        after,
        grid=(rows // step,),
        in_specs=[
            SCALARS,
            pl.BlockSpec((step, inner), lambda i: (i, 0)),
            block,
            whole(norm_rows.shape),
            block,
        ]
        + [HBM] * len(buffers),
        out_specs=[block] * 3 + [whole((2, width)), HBM],
        out_shape=[
            jax.ShapeDtypeStruct((rows, width), jnp.bfloat16),
            jax.ShapeDtypeStruct((rows, width), jnp.float32),
            jax.ShapeDtypeStruct((rows, width), jnp.bfloat16),
            jax.ShapeDtypeStruct((2, width), jnp.float32),
            jax.ShapeDtypeStruct((inner, width), jnp.bfloat16),
        ],
        scratch_shapes=[
            pltpu.VMEM((inner, width), jnp.bfloat16),
            pltpu.SemaphoreType.DMA,
            pltpu.SemaphoreType.DMA,
        ],
        compiler_params=grant(56),
        cost_estimate=NO_COST,
    )


def share(core, value, kept_ref, sent_ref, columns):
    places, rows, _ = kept_ref.shape
    value = value.astype(jnp.bfloat16).reshape(places, 2, rows, value.shape[1])
    low, high = value[:, 0], value[:, 1]
    kept_ref[:, :, columns] = jnp.where(core == 0, low, high)
    sent_ref[:, :, columns] = jnp.where(core == 0, high, low)


def rows_grad_kernel(core_ref, left_ref, right_ref, *refs):
    kept_ref, sent_ref, turned_ref = refs[-3:]

    @pl.when(pl.program_id(0) == 0)
    def _():
        turned_ref[...] = left_ref[...].T

    right = right_ref[...].reshape(right_ref.shape[-2:])
    share(core_ref[0], dot(turned_ref[...], right), kept_ref, sent_ref, slice(None))


def rows_grad(core, left, right, rows, into=None, after=()):
    tokens, width = left.shape
    places = width // rows // 2
    step = 512
    each = right.shape[-1] // step
    steps = right.size // tokens // step
    if right.ndim == 3:
        block = pl.BlockSpec((1, tokens, step), lambda i: (i // each, 0, i % each))
    else:
        block = pl.BlockSpec((tokens, step), lambda i: (0, i))
    out = pl.BlockSpec((places, rows, step), lambda i: (0, 0, i))
    into = tuple(into) if into else ()
    columns = into[0].shape[2] if into else steps * step
    return run(
        rows_grad_kernel,
        (core, left, right, *into,),
        after,
        grid=(steps,),
        in_specs=[SCALARS, whole((tokens, width)), block] + [HBM] * len(into),
        out_specs=[out, out],
        out_shape=[jax.ShapeDtypeStruct((places, rows, columns), jnp.bfloat16)] * 2,
        input_output_aliases={3: 0, 4: 1} if into else {},
        scratch_shapes=[pltpu.VMEM((width, tokens), jnp.bfloat16)],
        compiler_params=grant(56),
        cost_estimate=NO_COST,
    )


def ffn_back_kernel(
    core_ref,
    act_ref,
    slope_ref,
    w_down_ref,
    w_up_ref,
    grad_ref,
    low_ref,
    second_ref,
    xhat_ref,
    scale_ref,
    norm_ref,
    down_kept_ref,
    down_sent_ref,
    up_kept_ref,
    up_sent_ref,
    in_ref,
    branch_ref,
    norms_ref,
    turned_ref,
    sum_ref,
):
    step = pl.program_id(0)
    core = core_ref[0]

    @pl.when(step == 0)
    def _():
        turned_ref[...] = low_ref[...].T
        sum_ref[...] = second_ref[...]

    grad = grad_ref[...]
    back = dot(grad, w_down_ref[...], LAST) * slope_ref[...].astype(jnp.float32)
    back = back.astype(jnp.bfloat16)
    share(core, dot(act_ref[...].T, grad), down_kept_ref, down_sent_ref, slice(None))
    share(core, dot(turned_ref[...], back), up_kept_ref, up_sent_ref, slice(None))
    sum_ref[...] += dot(back, w_up_ref[...], LAST)

    @pl.when(step == pl.num_programs(0) - 1)
    def _():
        gain_sum = shift_sum = 0.0
        chunk = 128
        for j in range(sum_ref.shape[0] // chunk):
            here = slice(j * chunk, (j + 1) * chunk)
            first, xhat = sum_ref[here], xhat_ref[here]
            back = norm_back(first, xhat, scale_ref[here], norm_ref[0:1])
            in_ref[here] = back
            branch_ref[here] = back.astype(jnp.bfloat16)
            gain_sum = gain_sum + jnp.sum(first * xhat, axis=0, keepdims=True)
            shift_sum = shift_sum + jnp.sum(first, axis=0, keepdims=True)
        norms_ref[0:1] = gain_sum
        norms_ref[1:2] = shift_sum


def ffn_back(core, act, slope, w_down, w_up, grad, low, second, xhat, scale, norm_rows, rows, ff_rows):
    tokens, inner = act.shape
    width = grad.shape[1]
    step = 512
    places = width // rows // 2
    ff_places = inner // ff_rows // 2
    here = step // ff_rows // 2
    columns = pl.BlockSpec((tokens, step), lambda i: (0, i))
    down_out = pl.BlockSpec((here, ff_rows, width), lambda i: (i, 0, 0))
    up_out = pl.BlockSpec((places, rows, step), lambda i: (0, 0, i))
    down_shape = jax.ShapeDtypeStruct((ff_places, ff_rows, width), jnp.bfloat16)
    up_shape = jax.ShapeDtypeStruct((places, rows, inner + width + 128), jnp.bfloat16)
    return run(
        ffn_back_kernel,
        (core, act, slope, w_down, w_up, grad, low, second, xhat, scale, norm_rows),
        grid=(inner // step,),
        in_specs=[
            SCALARS,
            columns,
            columns,
            pl.BlockSpec((step, width), lambda i: (i, 0)),
            pl.BlockSpec((width, step), lambda i: (0, i)),
            whole((tokens, width)),
            whole((tokens, width)),
            whole((tokens, width)),
            whole((tokens, width)),
            whole((tokens, 1)),
            whole(norm_rows.shape),
        ],
        out_specs=[down_out, down_out, up_out, up_out]
        + [whole((tokens, width))] * 2
        + [whole((2, width))],
        out_shape=[
            down_shape,
            down_shape,
            up_shape,
            up_shape,
            jax.ShapeDtypeStruct((tokens, width), jnp.float32),
            jax.ShapeDtypeStruct((tokens, width), jnp.bfloat16),
            jax.ShapeDtypeStruct((2, width), jnp.float32),
        ],
        scratch_shapes=[
            pltpu.VMEM((width, tokens), jnp.bfloat16),
            pltpu.VMEM((tokens, width), jnp.float32),
        ],
        compiler_params=grant(56),
        cost_estimate=NO_COST,
    )


def out_grad_kernel(
    core_ref,
    context_ref,
    grad_ref,
    w_ref,
    one_ref,
    two_ref,
    kept_in,
    sent_in,
    back_ref,
    kept_hbm,
    sent_hbm,
    kept_ref,
    sent_ref,
    sems,
):
    core = core_ref[0]
    width = w_ref.shape[0]
    grad = grad_ref[...]
    turned = context_ref[...].T
    step = 256
    for j in range(width // step):
        here = slice(j * step, (j + 1) * step)
        share(core, dot(turned, grad[:, here]), kept_ref, sent_ref, here)
    norms = jnp.concatenate([one_ref[...], two_ref[...], jnp.zeros((124, width), jnp.float32)], 0)
    share(core, norms.T, kept_ref, sent_ref, slice(width, width + 128))
    last = pl.ds(kept_hbm.shape[2] - width - 128, width + 128)
    copies = [
        pltpu.make_async_copy(kept_ref, kept_hbm.at[:, :, last], sems.at[0]),
        pltpu.make_async_copy(sent_ref, sent_hbm.at[:, :, last], sems.at[1]),
    ]
    for copy in copies:
        copy.start()
    for j in range(width // step):
        here = slice(j * step, (j + 1) * step)
        back_ref[:, here] = dot(grad, w_ref[here], LAST).astype(jnp.bfloat16)
    for copy in copies:
        copy.wait()


def out_grad(core, context, grad, w_up, norms_one, norms_two, kept, sent, after=()):
    tokens, width = context.shape
    part = pltpu.VMEM(kept.shape[:2] + (width + 128,), jnp.bfloat16)
    out = kept.shape
    return run(
        out_grad_kernel,
        (core, context, grad, w_up, norms_one, norms_two, kept, sent),
        after,
        grid=(1,),
        in_specs=[
            SCALARS,
            whole((tokens, width)),
            whole((tokens, width)),
            pl.BlockSpec((width, width), lambda i: (0, w_up.shape[1] // width - 1)),
            whole((2, width)),
            whole((2, width)),
            HBM,
            HBM,
        ],
        out_specs=[whole((tokens, width)), HBM, HBM],
        out_shape=[
            jax.ShapeDtypeStruct((tokens, width), jnp.bfloat16),
            jax.ShapeDtypeStruct(out, jnp.bfloat16),
            jax.ShapeDtypeStruct(out, jnp.bfloat16),
        ],
        input_output_aliases={6: 1, 7: 2},
        scratch_shapes=[part, part, pltpu.SemaphoreType.DMA((2,))],
        compiler_params=grant(56),
        cost_estimate=NO_COST,
    )


def tokens_grad_kernel(grad_ref, w_ref, first_ref, out_ref, sum_ref):
    step = pl.program_id(0)

    @pl.when(step == 0)
    def _():
        sum_ref[...] = first_ref[...]

    sum_ref[...] += dot(grad_ref[0], w_ref[...], LAST)

    @pl.when(step == pl.num_programs(0) - 1)
    def _():
        out_ref[...] = sum_ref[...].astype(jnp.bfloat16)


def tokens_grad(grad_mixed, w_first, first, after=()):
    count, tokens, width = grad_mixed.shape
    return run(
        tokens_grad_kernel,
        (grad_mixed, w_first, first,),
        after,
        grid=(count,),
        in_specs=[
            pl.BlockSpec((1, tokens, width), lambda i: (i, 0, 0)),
            pl.BlockSpec((width, width), lambda i: (0, i)),
            whole((tokens, width)),
        ],
        out_specs=whole((tokens, width)),
        out_shape=jax.ShapeDtypeStruct((tokens, width), jnp.bfloat16),
        scratch_shapes=[pltpu.VMEM((tokens, width), jnp.float32)],
        compiler_params=grant(56),
        cost_estimate=NO_COST,
    )


def fold_kernel(place_ref, kept_ref, came_ref, a_own_ref, a_out_ref, b_own_ref, b_out_ref):
    x, y = place_ref[0], place_ref[1]
    half = a_own_ref.shape[2]
    part = lambda ref, i, j, rows: ref[0, i, j, rows].astype(jnp.float32)
    low, high = pl.ds(0, half), pl.ds(half, half)
    for i in range(2):
        both = lambda a, b, rows: (part(kept_ref, a, b, rows) + part(came_ref, a, b, rows)).astype(
            jnp.bfloat16
        )
        a_own_ref[0, i] = both(i, y, low)
        a_out_ref[0, i] = both(i, 1 - y, low)
        b_own_ref[0, i] = both(x, i, high)
        b_out_ref[0, i] = both(1 - x, i, high)


def fold_plane_kernel(place_ref, *refs):
    for i in range(2):
        own_ref, came_ref = refs[2 * i], refs[2 * i + 1]
        keep_ref, out_ref = refs[4 + 2 * i], refs[5 + 2 * i]
        place = place_ref[i]
        for ref, index in ((keep_ref, place), (out_ref, 1 - place)):
            total = own_ref[0, index].astype(jnp.float32) + came_ref[0, index].astype(jnp.float32)
            ref[0] = total.astype(jnp.bfloat16)


def fold_plane(place, a_own, a_came, b_own, b_came, after=()):
    zs, both, rows, columns = a_own.shape
    block = pl.BlockSpec((1, both, rows, columns), lambda i: (i, 0, 0, 0))
    out = pl.BlockSpec((1, rows, columns), lambda i: (i, 0, 0))
    return run(
        fold_plane_kernel,
        (place, a_own, a_came, b_own, b_came),
        after,
        grid=(zs,),
        in_specs=[SCALARS] + [block] * 4,
        out_specs=[out] * 4,
        out_shape=[jax.ShapeDtypeStruct((zs, rows, columns), jnp.bfloat16)] * 4,
        compiler_params=grant(20),
        cost_estimate=NO_COST,
    )


def fold(place, kept, came, after=()):
    zs, xs, ys, rows, columns = kept.shape
    out = pl.BlockSpec((1, 2, rows // 2, columns), lambda i: (i, 0, 0, 0))
    block = pl.BlockSpec((1, xs, ys, rows, columns), lambda i: (i, 0, 0, 0, 0))
    return run(
        fold_kernel,
        (place, kept, came,),
        after,
        grid=(zs,),
        in_specs=[SCALARS, block, block],
        out_specs=[out] * 4,
        out_shape=[jax.ShapeDtypeStruct((zs, 2, rows // 2, columns), jnp.bfloat16)] * 4,
        compiler_params=grant(20),
        cost_estimate=NO_COST,
    )


def gate(values, after=(), room=None):
    return run(
        lambda *refs: None,
        values,
        after,
        in_specs=[pl.BlockSpec(memory_space=pl.ANY)] * len(values),
        out_specs=[pl.BlockSpec(memory_space=pl.ANY)] * len(values),
        out_shape=[jax.ShapeDtypeStruct(v.shape, v.dtype) for v in values],
        input_output_aliases={i: i for i in range(len(values))},
        compiler_params=grant(room) if room else None,
    )


def routes(move):
    pairs = []
    for place in range(32):
        z, x, y, c = place // 8, place // 4 % 2, place // 2 % 2, place % 2
        target = move(z, x, y, c)
        if target is not None:
            tz, tx, ty, tc = target
            pairs.append((place, tz * 8 + tx * 4 + ty * 2 + tc))
    return pairs


ROUTE_X = routes(lambda z, x, y, c: (z, 1 - x, y, c))
ROUTE_Y = routes(lambda z, x, y, c: (z, x, 1 - y, c))
ROUTE_C = routes(lambda z, x, y, c: (z, x, y, 1 - c))


def send(value, route):
    return lax.ppermute(value, ALL, route)


def coordinates():
    dp = lax.axis_index("dp")
    return dp // 2, dp % 2, lax.axis_index("blk"), lax.axis_index("head")


def side_kernel(left_ref, right_ref, out_ref):
    middle = left_ref.shape[1]
    out_ref[:, :middle] = left_ref[...]
    out_ref[:, middle:] = right_ref[...]


def side_by_side(left, right, after):
    blocks, first, columns = left.shape
    both = first + right.shape[1]
    return run(
        side_kernel,
        (left, right),
        after,
        grid=(blocks,),
        in_specs=[
            pl.BlockSpec((1,) + left.shape[1:], lambda i: (i, 0, 0)),
            pl.BlockSpec((1,) + right.shape[1:], lambda i: (i, 0, 0)),
        ],
        out_specs=pl.BlockSpec((1, both, columns), lambda i: (i, 0, 0)),
        out_shape=jax.ShapeDtypeStruct((blocks, both, columns), left.dtype),
        cost_estimate=NO_COST,
    )


def sum_of(values):
    total = None
    for value in values:
        value = value.astype(jnp.float32)
        total = value if total is None else total + value
    return total


def slot_rows(buffers, rows):
    z, x, y, c = coordinates()
    tables = []
    for value, part, axis, dx, dy, dc in buffers:
        js = jnp.arange(value.shape[0])[:, None]
        zs = jnp.arange(4)[None, :]
        sx = (x ^ dx ^ js) if axis == 0 else x ^ dx
        sy = (y ^ dy ^ js) if axis == 1 else y ^ dy
        device = ((zs * 2 + sx) * 2 + sy) * 2 + (c ^ dc)
        tables.append((device * rows + part * (rows // 2)).reshape(-1))
    return jnp.concatenate(tables).astype(jnp.int32)


def pick(value, index, axis):
    return lax.dynamic_index_in_dim(value, index, axis, keepdims=False)


def fold_cores(kept, came, after):
    z, x, y, c = coordinates()
    shape = (4, 2, 2) + kept.shape[1:]
    return fold(jnp.stack([x, y]), kept.reshape(shape), came.reshape(shape), after)


def natural(kept, sent):
    return jnp.stack([kept, sent], axis=1).reshape(-1, kept.shape[2])


def joined_shards(up_weight, out_weight, norm_params):
    norm_wide = jnp.pad(norm_params, ((0, 0), (0, 128 - norm_params.shape[1])))
    return jnp.concatenate([up_weight, out_weight, norm_wide], axis=1)


def split_up(grad, width):
    inner = grad.shape[1] - width - 128
    last = inner + width
    return tuple(
        part.astype(jnp.float32)
        for part in (grad[:, :inner], grad[:, inner:last], grad[:, last : last + 4])
    )


def buffers_of(a2, ay, b2, bx):
    return [(a2, 0, 0, 0, 0), (ay, 0, 0, 0, 1), (b2, 1, 1, 0, 0), (bx, 1, 1, 1, 0)]


def with_partner(shard, own, partner):
    buffers = [b + (0,) for b in own]
    buffers += [(v,) + b[1:] + (1,) for v, b in zip(partner, own)]
    return slot_rows(buffers, shard.shape[0]), [b[0] for b in buffers]


def body_lines(
    tokens, doc_lengths, qkv_weight, out_weight, up_weight, down_weight, norm_params, out_cotangent
):
    seqs_here, local_len, width = tokens.shape
    full_len = local_len * 4
    z, x, y, c = coordinates()
    place = y * 2 + c
    core = c.reshape(1)
    slab, ff_slab = up_weight.shape[0], down_weight.shape[0]
    exchange = lambda v: lax.all_to_all(v, GROUP, split_axis=0, concat_axis=0, tiled=True)
    to_sequence = lambda v: exchange(v).reshape(full_len, width)
    own_lengths = lax.dynamic_slice_in_dim(doc_lengths, place, 1, 0)
    seg_row = segments_of(own_lengths, full_len)
    seg_col = seg_row.reshape(full_len, 1)
    first_own, up_own = qkv_weight, joined_shards(up_weight, out_weight, norm_params)
    half, ff_half = slab // 2, ff_slab // 2
    line = lambda v: lax.all_gather(v, "dp", axis_index_groups=LINES)

    first_line = line(first_own)
    down_a, down_b = down_weight[:ff_half], down_weight[ff_half:]
    down_ax, down_by = send(down_a, ROUTE_X), send(down_b, ROUTE_Y)
    both = exchange(side_by_side(tokens, out_cotangent, ()))
    rows, upstream = (
        v.reshape(full_len, width) for v in (both[:, :local_len], both[:, local_len:])
    )
    down_own = jnp.stack([down_a, down_ax, down_b, down_by])

    a, b = gate(
        (first_line[:, :half], first_line[:, half:]),
        (rows, upstream, down_own, seg_row, seg_col),
    )
    ax, by = send(a, ROUTE_X), send(b, ROUTE_Y)
    up_line = line(up_own)

    a2, b2 = gate((jnp.stack([a, ax]), jnp.stack([b, by])))
    ay, bx = send(a2, ROUTE_Y), send(b2, ROUTE_X)

    up_a, up_b, down_own = gate((up_line[:, :half], up_line[:, half:], down_own))
    up_ax, up_by = send(up_a, ROUTE_X), send(up_b, ROUTE_Y)
    down_line = line(down_own)

    ay, bx, up_ax, up_by, a2, b2 = gate((ay, bx, up_ax, up_by, a2, b2))
    a2c, b2c = send(a2, ROUTE_C), send(b2, ROUTE_C)
    ayc, bxc = send(ay, ROUTE_C), send(bx, ROUTE_C)
    up_a2, up_b2 = jnp.stack([up_a, up_ax]), jnp.stack([up_b, up_by])
    up_ay, up_bx = send(up_a2, ROUTE_Y), send(up_b2, ROUTE_X)
    up_a2c, up_b2c = send(up_a2, ROUTE_C), send(up_b2, ROUTE_C)
    table, buffers = with_partner(
        first_own, buffers_of(a2, ay, b2, bx), (a2c, ayc, b2c, bxc)
    )
    projected, w_first = project(rows, table, buffers, 3 * width)
    context, log_sums = attention(projected, seg_col, seg_row)

    up_ay, up_bx, up_a2c, up_b2c, down_line, context = gate(
        (up_ay, up_bx, up_a2c, up_b2c, down_line, context)
    )
    down_a2, down_b2 = jnp.swapaxes(down_line[:, :2], 0, 1), jnp.swapaxes(down_line[:, 2:], 0, 1)
    down_ay, down_bx = send(down_a2, ROUTE_Y), send(down_b2, ROUTE_X)
    down_a2c, down_b2c = send(down_a2, ROUTE_C), send(down_b2, ROUTE_C)
    up_ayc, up_bxc = send(up_ay, ROUTE_C), send(up_bx, ROUTE_C)
    table, buffers = with_partner(
        up_own, buffers_of(up_a2, up_ay, up_b2, up_bx), (up_a2c, up_ayc, up_b2c, up_bxc)
    )
    xhat, scale, first_low, norm_rows, act, slope, w_up = middle(context, rows, table, buffers)

    down_ay, down_bx, down_a2c, down_b2c, act = gate((down_ay, down_bx, down_a2c, down_b2c, act))
    down_ayc, down_bxc = send(down_ay, ROUTE_C), send(down_bx, ROUTE_C)
    table, buffers = with_partner(
        down_weight,
        buffers_of(down_a2, down_ay, down_b2, down_bx),
        (down_a2c, down_ayc, down_b2c, down_bxc),
    )
    result, grad_second, grad_ff, norms_two, w_down = down_norm(
        act, table, buffers, xhat, norm_rows, upstream
    )

    low = lambda *v: sum_of(v).astype(jnp.bfloat16)
    place_xy = jnp.stack([x, y])
    down_kept, down_sent, up_kept, up_sent, grad_first_in, grad_branch, norms_one = ffn_back(
        core,
        act,
        slope,
        w_down,
        w_up,
        grad_ff,
        first_low,
        grad_second,
        xhat,
        scale,
        norm_rows,
        slab,
        ff_slab,
    )

    down_sent, grad_branch = gate((down_sent, grad_branch))
    down_came = send(down_sent, ROUTE_C)
    grad_context, up_kept, up_sent = out_grad(
        core, context, grad_branch, w_up, norms_one, norms_two, up_kept, up_sent
    )

    da_own, da_out, db_own, db_out = fold_cores(down_kept, down_came, (grad_context,))
    da_out, db_out, up_sent, grad_context = gate((da_out, db_out, up_sent, grad_context), (), 1)
    da_in, db_in = send(da_out, ROUTE_Y), send(db_out, ROUTE_X)
    up_came = send(up_sent, ROUTE_C)
    grad_mixed = attention_back(projected, grad_context, seg_col, seg_row, log_sums)

    ua_own, ua_out, ub_own, ub_out = fold_cores(up_kept, up_came, (grad_mixed, da_in, db_in))
    down_blocks = jnp.concatenate([low(da_own, da_in), low(db_own, db_in)], axis=1)
    ua_out, ub_out, down_blocks, grad_mixed = gate((ua_out, ub_out, down_blocks, grad_mixed), (), 1)
    ua_in, ub_in = send(ua_out, ROUTE_Y), send(ub_out, ROUTE_X)
    down_sum = lax.psum_scatter(
        down_blocks, "dp", scatter_dimension=0, axis_index_groups=LINES, tiled=False
    )
    last_kept, last_sent = rows_grad(core, rows, grad_mixed, slab)
    grad_tokens = tokens_grad(grad_mixed, w_first, grad_first_in, (last_sent,))

    ua_own, ua_out, ub_own, ub_out = fold_plane(
        place_xy, ua_own, ua_in, ub_own, ub_in, (grad_tokens,)
    )
    ua_out, ub_out, last_sent = gate((ua_out, ub_out, last_sent), (), 1)
    ua_in2, ub_in2 = send(ua_out, ROUTE_X), send(ub_out, ROUTE_Y)
    last_came = send(last_sent, ROUTE_C)

    la_own, la_out, lb_own, lb_out = fold_cores(last_kept, last_came, (ua_in2, ub_in2))
    up_blocks = jnp.concatenate([low(ua_own, ua_in2), low(ub_own, ub_in2)], axis=1)
    up_blocks, la_out, lb_out, down_sum = gate((up_blocks, la_out, lb_out, down_sum), (), 1)
    up_sum = lax.psum_scatter(
        up_blocks, "dp", scatter_dimension=0, axis_index_groups=LINES, tiled=False
    )
    la_in, lb_in = send(la_out, ROUTE_Y), send(lb_out, ROUTE_X)
    da_in = send(pick(down_sum[:2], 1 - x, 0), ROUTE_X)
    db_in = send(pick(down_sum[2:], 1 - y, 0), ROUTE_Y)

    la_own, la_out, lb_own, lb_out = fold_plane(
        place_xy, la_own, la_in, lb_own, lb_in, (da_in, db_in)
    )
    la_out, lb_out, grad_tokens = gate((la_out, lb_out, grad_tokens), (), 1)
    la_in2, lb_in2 = send(la_out, ROUTE_X), send(lb_out, ROUTE_Y)
    grad_down = jnp.concatenate(
        [sum_of([pick(down_sum[:2], x, 0), da_in]), sum_of([pick(down_sum[2:], y, 0), db_in])],
        axis=0,
    )

    last_blocks = jnp.concatenate([low(la_own, la_in2), low(lb_own, lb_in2)], axis=1)
    as_blocks = lambda v: v.reshape(seqs_here, local_len, width)
    packed = side_by_side(as_blocks(result), as_blocks(grad_tokens), ())
    last_blocks, packed, up_sum = gate((last_blocks, packed, up_sum), (), 1)
    returned = exchange(packed)
    layer_out, input_grad = returned[:, :local_len], returned[:, local_len:]
    last_sum = lax.psum_scatter(
        last_blocks, "dp", scatter_dimension=0, axis_index_groups=LINES, tiled=False
    )
    grad_qkv = last_sum.astype(jnp.float32)
    grad_up, grad_out, grad_norm = split_up(up_sum, width)
    return (
        layer_out,
        input_grad.astype(jnp.float32),
        grad_qkv,
        grad_out,
        grad_up,
        grad_down,
        grad_norm,
    )


def body_any(
    tokens, doc_lengths, qkv_weight, out_weight, up_weight, down_weight, norm_params, out_cotangent
):
    seqs_here, local_len, width = tokens.shape
    ff = up_weight.shape[1]
    full_len = local_len * lax.axis_size("blk") * lax.axis_size("head")
    place = lax.axis_index("blk") * lax.axis_size("head") + lax.axis_index("head")
    core = jnp.zeros((1,), jnp.int32)
    slab, ff_slab = width // 32, ff // 32
    exchange = lambda v: lax.all_to_all(v, GROUP, split_axis=0, concat_axis=0, tiled=True)
    to_sequence = lambda v: exchange(v).reshape(full_len, width)
    to_positions = lambda v: exchange(v.reshape(seqs_here, local_len, width))

    def gather(shard):
        return core, [lax.all_gather(shard, ALL, axis=0, tiled=True)[None, None]]

    def scatter(kept, sent):
        total = lax.psum_scatter(natural(kept, sent), ALL, scatter_dimension=0, tiled=True)
        return total.astype(jnp.float32)

    rows = to_sequence(tokens)
    upstream = to_sequence(out_cotangent)
    own_lengths = lax.dynamic_slice_in_dim(doc_lengths, place, 1, 0)
    seg_row = segments_of(own_lengths, full_len)
    seg_col = seg_row.reshape(full_len, 1)
    first_slots = gather(qkv_weight)
    up_slots = gather(joined_shards(up_weight, out_weight, norm_params))
    projected, w_first = project(rows, *first_slots, 3 * width)
    context, log_sums = attention(projected, seg_col, seg_row)
    xhat, scale, first_low, norm_rows, act, slope, w_up = middle(context, rows, *up_slots)
    result, grad_second, grad_ff, norms_two, w_down = down_norm(
        act, *gather(down_weight), xhat, norm_rows, upstream
    )
    down_kept, down_sent, up_kept, up_sent, grad_first_in, grad_branch, norms_one = ffn_back(
        core,
        act,
        slope,
        w_down,
        w_up,
        grad_ff,
        first_low,
        grad_second,
        xhat,
        scale,
        norm_rows,
        slab,
        ff_slab,
    )
    grad_down = scatter(down_kept, down_sent)
    grad_context, up_kept, up_sent = out_grad(
        core, context, grad_branch, w_up, norms_one, norms_two, up_kept, up_sent
    )
    grad_up, grad_out, grad_norm = split_up(scatter(up_kept, up_sent), width)
    grad_mixed = attention_back(projected, grad_context, seg_col, seg_row, log_sums)
    grad_qkv = scatter(*rows_grad(core, rows, grad_mixed, slab))
    grad_tokens = tokens_grad(grad_mixed, w_first, grad_first_in)
    return (
        to_positions(result),
        to_positions(grad_tokens).astype(jnp.float32),
        grad_qkv,
        grad_out,
        grad_up,
        grad_down,
        grad_norm,
    )


def solution(mesh):
    sizes = tuple(mesh.shape[name] for name in ALL)
    body = body_lines if sizes == (8, 2, 2) else body_any
    placed = (
        P("dp", ("blk", "head"), None),
        P("dp", None),
        P(("dp", "blk", "head"), None),
        P(("dp", "blk", "head"), None),
        P(("dp", "blk", "head"), None),
        P(("dp", "blk", "head"), None),
        P(("dp", "blk", "head"), None),
        P("dp", ("blk", "head"), None),
    )
    return jax.shard_map(
        body,
        mesh=mesh,
        in_specs=placed,
        out_specs=(
            P("dp", ("blk", "head"), None),
            P("dp", ("blk", "head"), None),
            P(("dp", "blk", "head"), None),
            P(("dp", "blk", "head"), None),
            P(("dp", "blk", "head"), None),
            P(("dp", "blk", "head"), None),
            P(("dp", "blk", "head"), None),
        ),
        check_vma=False,
    )
```
